32 devices in a mesh: leaf: 4 (over x, core), row: 2 (over y), col: 4 (over z).
Axes of the slice: x: 2, y: 2, z: 4, core: 2. Of those that a mesh axis runs over, the one named last changes fastest.
Arguments:
- top_inverse: float32 [4096, 4096], P('row', ('leaf', 'col')), as said below
- pattern: int32 [4, 16], P('leaf'), may hold values from 0 to 31, as said below
- panel: float32 [4, 2048, 2048], P('leaf', None, 'col'), may hold values from -1.6 to 1.6
- diag_inverse: float32 [4, 2048, 2048], P('leaf', 'row', 'col'), as said below
Outputs:
- sigma_top: float32 [4096, 4096], P('row', ('leaf', 'col'))
- sigma_panel: float32 [4, 2048, 2048], P('leaf', 'row', 'col')
- sigma_diag: float32 [4, 2048, 2048], P('leaf', 'row', 'col')
The draws below stay inside these ranges and needn't reach their ends.
Inputs may be any that keep to these rules, and one draw needn't show every extreme that they name: `pattern`: each row holds 16 distinct block indices in rising order, among them 0 and 31. `top_inverse`: lower triangular with a positive diagonal. `diag_inverse`: each group's block is symmetric.
All inputs are finite; a program needn't handle non-finite values.
Results may differ from the reference program's by a relative error of at most 0.00016.
Values sent between devices are 32-bit elements; how exact they have to be, the bound alone decides.
No kernel may reach another device: no remote copies, remote signals or barrier semaphores. Data moves between devices by JAX's collectives and lax.ppermute only.
A program may use at most 128 MiB of HBM per device.

```python
import math
import jax
import jax.numpy as jnp
from jax import lax

BLK = 128
NBA = 32
NS = 16
W = 2048
WA = 4096
SROWS = 2048
GROUPS = 4


def draw_pattern(key, part):

    def single(one_key):
        inner = jax.random.permutation(one_key, NBA - 2)[:NS - 2].astype(jnp.int32) + 1
        ends = jnp.array([0, NBA - 1], dtype=jnp.int32)
        return jnp.sort(jnp.concatenate([ends, inner]))
    keys = jax.random.split(jax.random.fold_in(key, 11), GROUPS)
    return jax.vmap(single)(keys).astype(jnp.int32)


def draw_top_inverse(key, part):
    first, second = jax.random.split(jax.random.fold_in(key, 23), 2)
    rows_idx = lax.broadcasted_iota(jnp.int32, (WA, WA), 0)
    cols_idx = lax.broadcasted_iota(jnp.int32, (WA, WA), 1)
    rough = jax.random.normal(first, (WA, WA), jnp.float32)
    diagonal = jnp.exp(jax.random.uniform(second, (WA, WA), jnp.float32, math.log(0.3), math.log(3.0)))
    lower = rough / math.sqrt(WA)
    result = jnp.where(rows_idx > cols_idx, lower, jnp.where(rows_idx == cols_idx, diagonal, 0.0))
    return result.astype(jnp.float32)


def draw_diag_inverse(key, part):
    first, second = jax.random.split(jax.random.fold_in(key, 37), 2)
    rough = jax.random.normal(first, (GROUPS, W, W), jnp.float32)
    symmetric = (rough + jnp.swapaxes(rough, 1, 2)) * (0.5 / math.sqrt(W)) * 3.0
    rows_idx = lax.broadcasted_iota(jnp.int32, (GROUPS, W, W), 1)
    cols_idx = lax.broadcasted_iota(jnp.int32, (GROUPS, W, W), 2)
    levels = jnp.exp(jax.random.uniform(second, (GROUPS, W, 1), jnp.float32, 0.0, math.log(3.0)))
    result = symmetric + jnp.where(rows_idx == cols_idx, levels, 0.0)
    return result.astype(jnp.float32)


def block_levels(key, shape, cuts, least, largest):
    loudness, own = 1.0, jax.random.fold_in(key, 6)
    for position, shards_of in cuts:
        steps = jnp.exp(jax.random.uniform(jax.random.fold_in(own, position), (shards_of,), jnp.float32, least / len(cuts), largest / len(cuts)))
        loudness = loudness * jnp.repeat(steps, shape[position] // shards_of).reshape([-1 if axis == position else 1 for axis in range(len(shape))])
    return loudness


def scatter_about(own_key, shape, width, limit, pieces=(), kind=jnp.bfloat16):
    level = block_levels(own_key, shape, pieces, -0.22, 0.18) if pieces else 1.0
    values = jax.random.normal(own_key, shape, jnp.float32) * width * level
    return jnp.minimum(jnp.maximum(values, -limit), limit).astype(kind)


def setup_inputs(seed: int = 0) -> dict:
    seeds = jax.random.split(jax.random.key(seed), 5)
    top_inverse = draw_top_inverse(jax.random.fold_in(seeds[4], 71), 0)
    pattern = draw_pattern(jax.random.fold_in(seeds[4], 71), 0)
    panel = scatter_about(seeds[2], (GROUPS, SROWS, W), 0.2, 1.6, ((0, 4), (2, 4)), jnp.float32)
    diag_inverse = draw_diag_inverse(jax.random.fold_in(seeds[4], 71), 0)
    return {"top_inverse": top_inverse, "pattern": pattern, "panel": panel, "diag_inverse": diag_inverse}


def reference(top_inverse, pattern, panel, diag_inverse):
    exact = lax.Precision.HIGHEST
    sigma_top = jnp.dot(top_inverse.T, top_inverse, precision=exact, preferred_element_type=jnp.float32)
    offsets = jnp.arange(BLK, dtype=jnp.int32)
    panels = []
    diagonals = []
    for group_id in range(GROUPS):
        rows_sel = (pattern[group_id][:, None].astype(jnp.int32) * BLK + offsets[None, :]).reshape(-1).astype(jnp.int32)
        sub_block = jnp.take(jnp.take(sigma_top, rows_sel, axis=0), rows_sel, axis=1)
        sig_panel = -jnp.dot(sub_block, panel[group_id], precision=exact, preferred_element_type=jnp.float32)
        sig_diag = diag_inverse[group_id] - jnp.dot(panel[group_id].T, sig_panel, precision=exact, preferred_element_type=jnp.float32)
        panels.append(sig_panel)
        diagonals.append(sig_diag)
    return sigma_top, jnp.stack(panels), jnp.stack(diagonals)
```

```python
import jax
import jax.numpy as jnp
from jax import lax
from jax.sharding import PartitionSpec as P

BLK = 128


def contract_rows(left, right):
    return lax.dot_general(
        left,
        right,
        (((0,), (0,)), ((), ())),
        precision=lax.Precision.HIGH,
        preferred_element_type=jnp.float32,
    )


def shift(value, axis, pairs):
    return lax.ppermute(value, axis, pairs)


def line_gather(own, axis):
    count = lax.axis_size(axis)
    right, left = [own], [own]
    for step in range(count - 1):
        right.append(shift(right[-1], axis, [(i, i + 1) for i in range(step, count - 1)]))
        left.append(shift(left[-1], axis, [(i, i - 1) for i in range(1, count - step)]))
    me = lax.axis_index(axis)
    return [own] + [jnp.where(me >= t, right[t], left[count - t]) for t in range(1, count)]


def sum_scatter(part, axis):
    count = lax.axis_size(axis)
    me = lax.axis_index(axis)
    sent = []
    for away in range(1, count):
        pairs = [(i, (i + away) % count) for i in range(count)]
        sent.append(shift(part((me + away) % count), axis, pairs))
    total = part(me)
    for term in sent:
        total = total + term
    return total


def rows_of(array, index, count):
    return lax.dynamic_slice_in_dim(array, index * count, count, 0)


def per_device(top_inverse, pattern, panel, diag_inverse):
    rows = lax.axis_size("row")
    normed = panel[0]
    panel_count = normed.shape[0] // rows
    own_rows = rows_of(normed, lax.axis_index("row"), panel_count)
    pieces = line_gather(own_rows, "col")

    rows_here = lax.all_gather(top_inverse, ("leaf", "col"), axis=1, tiled=True)
    offsets = jnp.arange(BLK, dtype=jnp.int32)
    wanted = (pattern[0][:, None] * BLK + offsets[None, :]).reshape(-1)
    selected = jnp.take(rows_here, wanted, axis=1, mode="clip")
    image = jnp.dot(
        selected, normed, precision=lax.Precision.HIGH, preferred_element_type=jnp.float32
    )
    width = selected.shape[1] // rows
    sigma_panel = -sum_scatter(
        lambda i: contract_rows(lax.dynamic_slice_in_dim(selected, i * width, width, 1), image), "row"
    )
    top_width = rows_here.shape[1] // rows
    sigma_top = sum_scatter(
        lambda i: contract_rows(lax.dynamic_slice_in_dim(rows_here, i * top_width, top_width, 1), top_inverse),
        "row",
    )
    cols = lax.axis_size("col")
    me = lax.axis_index("col")
    wide = own_rows.shape[1]
    whole = jnp.concatenate(pieces[::-1] + pieces[::-1], axis=1)
    whole_rows = lax.dynamic_slice_in_dim(whole, (cols - 1 - me) * wide, cols * wide, 1)
    diag_width = whole_rows.shape[1] // rows
    update = sum_scatter(
        lambda i: contract_rows(
            lax.dynamic_slice_in_dim(whole_rows, i * diag_width, diag_width, 1), sigma_panel
        ),
        "row",
    )
    sigma_diag = diag_inverse[0] - update
    return (sigma_top, sigma_panel[None], sigma_diag[None])


def solution(mesh):
    placed = (
        P("row", ("leaf", "col")),
        P("leaf", None),
        P("leaf", None, "col"),
        P("leaf", "row", "col"),
    )
    return jax.shard_map(
        per_device,
        mesh=mesh,
        in_specs=placed,
        out_specs=(P("row", ("leaf", "col")), P("leaf", "row", "col"), P("leaf", "row", "col")),
        check_vma=False,
    )
```

```python
import functools

import jax
import jax.numpy as jnp
import numpy as np
from jax import lax
from jax.experimental import pallas as pl
from jax.experimental.pallas import tpu as pltpu
from jax.sharding import PartitionSpec as P

BLK = 128
VMEM_BYTES = 58 * 1024 * 1024


def halves(value):
    high = value.astype(jnp.bfloat16)
    low = (value - high.astype(jnp.float32)).astype(jnp.bfloat16)
    return high, low


def dot(left, right):
    return jnp.dot(left, right, preferred_element_type=jnp.float32)


def contract_rows(left, right):
    return lax.dot_general(
        left,
        right,
        (((0,), (0,)), ((), ())),
        precision=lax.Precision.HIGH,
        preferred_element_type=jnp.float32,
    )


class Layout:
    def __init__(self, rows, leaves, cols, half, width):
        self.leaves, self.cols, self.half, self.width = leaves, cols, half, width
        self.part = half // leaves
        self.span = width * cols
        self.counts, self.holder, self.source = [], [], []
        for r in range(rows):
            count = [min(leaves, (q * half + half - 1) // self.span + 1) for q in (2 * r + 1, 2 * (rows - 1 - r))]
            assert count[0] + count[1] <= leaves + 1
            free = list(range(count[1], leaves))
            moved = [leaf for leaf in range(1, count[0]) if leaf not in free]
            slot = {leaf: leaf for leaf in range(1, count[0]) if leaf in free}
            left = [s for s in free if s not in slot]
            slot.update(zip(moved, left))
            self.counts.append(count)
            self.holder.append(slot)
        table = np.full((rows, 2, leaves, leaves), -1, np.int32)
        for r in range(rows):
            for j in range(leaves):
                table[r, 0, 0, j] = j * (leaves + 1) + leaves
                for leaf, slot in self.holder[r].items():
                    table[r, 0, leaf, j] = slot * (leaves + 1) + j
                for leaf in range(self.counts[r][1]):
                    table[r, 1, leaf, j] = leaf * (leaves + 1) + j
        self.table = table


def panel_kernel(lay, pat, tab, shift, *refs):
    count = len(refs) - 9
    gathered = refs[:count]
    p_ref, y_ref, t, th, tl, image, turned_high, turned_low, sems = refs[count:]
    number, parts, part = t.shape[0], t.shape[2], t.shape[3]
    half = parts * part

    def place(k):
        first = pat[k] * BLK
        leaf = first // lay.span
        rest = first - leaf * lay.span
        col = rest // lay.width
        return leaf, col, (rest - col * lay.width) // BLK

    def valid(k, s):
        return tab[s, place(k)[0], 0] >= 0

    @pl.loop(0, number)
    def _(k):
        leaf, col, sub = place(k)
        for s in range(2):
            here = tab[s, leaf, 0] >= 0

            @pl.when(here)
            def _():
                for j in range(parts):
                    entry = tab[s, leaf, j]
                    slot = entry // (parts + 1)
                    position = entry - slot * (parts + 1)
                    for which in range(count):

                        @pl.when(sub == which)
                        def _():
                            pltpu.make_async_copy(
                                gathered[which].at[slot * lay.cols + col, position],
                                t.at[k, s, j],
                                sems.at[k, s],
                            ).start()

            @pl.when(jnp.logical_not(here))
            def _():
                t[k, s] = jnp.zeros(t.shape[2:], t.dtype)

    image[...] = jnp.zeros_like(image)

    @pl.loop(0, number // 2)
    def _(kp):
        rows = pl.ds(pl.multiple_of(kp * 2 * BLK, 2 * BLK), 2 * BLK)
        p_high, p_low = halves(p_ref[rows, :])
        stacked = jnp.concatenate([p_high, p_low, p_high], axis=0)
        for s in range(2):
            for m in range(2):

                @pl.when(valid(2 * kp + m, s))
                def _():
                    pltpu.make_async_copy(t.at[2 * kp + m, s], t.at[2 * kp + m, s], sems.at[2 * kp + m, s]).wait()

            @pl.when(jnp.logical_or(valid(2 * kp, s), valid(2 * kp + 1, s)))
            def _():
                @pl.loop(0, parts)
                def _(j):
                    both = jnp.concatenate([t[2 * kp, s, j], t[2 * kp + 1, s, j]], axis=1)
                    high, low = halves(both)
                    th[kp, s, j] = high
                    tl[kp, s, j] = low
                    image[s, j] += dot(jnp.concatenate([high, high, low], axis=1), stacked)

    for s in range(2):

        @pl.loop(0, parts)
        def _(j):
            high, low = halves(image[s, j].T)
            turned_high[s, j] = high
            turned_low[s, j] = low

    @pl.loop(0, number // 2)
    def _(kp):
        def term(s, j):
            high, low = th[kp, s, j], tl[kp, s, j]
            left = jnp.concatenate([turned_high[s, j], turned_low[s, j], turned_high[s, j]], axis=1)
            return dot(left, jnp.concatenate([high, high, low], axis=0))

        out = y_ref.at[lax.rem(kp + shift[0], number // 2)]
        out[...] = jnp.zeros(out.shape, out.dtype)
        for s in range(2):

            @pl.when(jnp.logical_or(valid(2 * kp, s), valid(2 * kp + 1, s)))
            def _():
                total = term(s, 0)
                for j in range(1, parts):
                    total = total + term(s, j)
                out[...] += total.T


def panel_product(lay, pattern, table, shift, gathered, normed):
    number, wide = pattern.shape[0], normed.shape[1]
    half, part, parts = lay.half, lay.part, lay.leaves
    any_space = pl.BlockSpec(memory_space=pl.ANY)
    vmem = pl.BlockSpec(memory_space=pltpu.VMEM)
    smem = pl.BlockSpec(memory_space=pltpu.SMEM)
    return pl.pallas_call(
        functools.partial(panel_kernel, lay),
        out_shape=jax.ShapeDtypeStruct((number // 2, 2 * BLK, wide), jnp.float32),
        in_specs=[smem] * 3 + [any_space] * len(gathered) + [vmem],
        out_specs=vmem,
        scratch_shapes=[
            pltpu.VMEM((number, 2, parts, part, BLK), jnp.float32),
            pltpu.VMEM((number // 2, 2, parts, part, 2 * BLK), jnp.bfloat16),
            pltpu.VMEM((number // 2, 2, parts, part, 2 * BLK), jnp.bfloat16),
            pltpu.VMEM((2, parts, part, wide), jnp.float32),
            pltpu.VMEM((2, parts, wide, part), jnp.bfloat16),
            pltpu.VMEM((2, parts, wide, part), jnp.bfloat16),
            pltpu.SemaphoreType.DMA((number, 2)),
        ],
        compiler_params=pltpu.CompilerParams(vmem_limit_bytes=VMEM_BYTES),
        cost_estimate=pl.CostEstimate(
            flops=12 * 2 * half * number * BLK * wide,
            bytes_accessed=4 * (2 * half * number * BLK + 2 * number * BLK * wide),
            transcendentals=0,
        ),
    )(pattern, table, shift, *gathered, normed)


def top_kernel(lay, tab, info, g_ref, own_ref, out_ref, own_turned):
    blocks, _, part, _ = g_ref.shape
    parts = lay.leaves
    for s in range(2):

        @pl.loop(0, parts)
        def _(j):
            high, low = halves(own_ref[s, j].T)
            own_turned[s, j] = jnp.concatenate([high, low, high], axis=1)

    @pl.loop(0, blocks // 2)
    def _(pair):
        block = 2 * pair
        leaf = block // lay.cols
        col = block - leaf * lay.cols
        out = out_ref.at[lax.rem(pair + info[0], blocks // 2)]
        out[...] = jnp.zeros(out.shape, out.dtype)
        for s in range(2):

            @pl.when(jnp.logical_and(tab[s, leaf, 0] >= 0, tab[s, info[1], 0] >= 0))
            def _():
                total = None
                for j in range(parts):
                    entry = tab[s, leaf, j]
                    slot = entry // (parts + 1)
                    position = entry - slot * (parts + 1)
                    at = slot * lay.cols + col
                    both = jnp.concatenate([g_ref[at, position], g_ref[at + 1, position]], axis=1)
                    high, low = halves(both)
                    term = dot(own_turned[s, j], jnp.concatenate([high, high, low], axis=0))
                    total = term if total is None else total + term
                out[...] += total.T


def top_product(lay, table, info, gathered, own):
    blocks = gathered.shape[0]
    parts, part, width = lay.leaves, lay.part, lay.width
    vmem = pl.BlockSpec(memory_space=pltpu.VMEM)
    smem = pl.BlockSpec(memory_space=pltpu.SMEM)
    return pl.pallas_call(
        functools.partial(top_kernel, lay),
        out_shape=jax.ShapeDtypeStruct((blocks // 2, 2 * BLK, width), jnp.float32),
        in_specs=[smem, smem, vmem, vmem],
        out_specs=vmem,
        scratch_shapes=[pltpu.VMEM((2, parts, width, 3 * part), jnp.bfloat16)],
        compiler_params=pltpu.CompilerParams(vmem_limit_bytes=VMEM_BYTES),
        cost_estimate=pl.CostEstimate(
            flops=6 * 2 * lay.half * blocks * BLK * width,
            bytes_accessed=4 * gathered.size,
            transcendentals=0,
        ),
    )(table, info, gathered, own)


def exchange(value, axis, away):
    count = lax.axis_size(axis)
    return lax.ppermute(value, axis, [(i, (i + away) % count) for i in range(count)])


def sum_rotated(value):
    rows = lax.axis_size("row")
    each = value.shape[0] // rows
    received = [exchange(value[(away - 1) * each : away * each], "row", away) for away in range(1, rows)]
    total = value[(rows - 1) * each :]
    for term in received:
        total = total + term
    return total


def per_device(lay, top_inverse, pattern, panel, diag_inverse):
    rows, cols, leaves = (lax.axis_size(axis) for axis in ("row", "col", "leaf"))
    me_row, me_col, me_leaf = (lax.axis_index(axis) for axis in ("row", "col", "leaf"))
    half, width, parts, part = lay.half, lay.width, lay.leaves, lay.part
    normed = panel[0]

    table = jnp.asarray(lay.table)[me_row]
    second = jnp.asarray([count[1] for count in lay.counts], jnp.int32)[me_row]
    is_moved = np.zeros((rows, leaves), bool)
    pairs = []
    for r in range(rows):
        for leaf, slot in lay.holder[r].items():
            if leaf != slot:
                is_moved[r, slot] = True
                pairs.append((leaf * rows + r, slot * rows + r))
    moved_here = jnp.asarray(is_moved)[me_row, me_leaf]
    gathered, own = [], []
    for sub in range(width // BLK):
        lanes = slice(sub * BLK, (sub + 1) * BLK)
        lower, upper = top_inverse[half:, lanes], top_inverse[:half, lanes]
        swapped = lax.ppermute(upper, "row", [(r, rows - 1 - r) for r in range(rows)])
        moved = lax.ppermute(lower, ("leaf", "row"), pairs) if pairs else lower
        whole = jnp.where(me_leaf < second, swapped, jnp.where(moved_here, moved, lower))
        extra = lower[:part]
        for j in range(1, parts):
            sent = lax.ppermute(lower[j * part : (j + 1) * part], "leaf", [(0, j)])
            extra = jnp.where(me_leaf == j, sent, extra)
        held = jnp.concatenate([whole.reshape(parts, part, BLK), extra[None]], axis=0)
        gathered.append(lax.all_gather(held, ("leaf", "col"), axis=0, tiled=False))
        own.append(jnp.stack([lower, swapped]))
    own = jnp.concatenate(own, axis=2).reshape(2, parts, part, width)

    own_rows = lax.dynamic_slice_in_dim(normed, me_row * (normed.shape[0] // rows), normed.shape[0] // rows, 0)
    right, left = [own_rows], [own_rows]
    for step in range(cols - 1):
        if step == 1:
            right[-1], left[-1], gathered[-1] = lax.optimization_barrier((right[-1], left[-1], gathered[-1]))
        right.append(lax.ppermute(right[-1], "col", [(i, i + 1) for i in range(step, cols - 1)]))
        left.append(lax.ppermute(left[-1], "col", [(i, i - 1) for i in range(1, cols - step)]))

    blocks = gathered[0].shape[0] // 2
    info = jnp.stack([(rows - 1 - me_row) * (blocks // rows), me_leaf]).astype(jnp.int32)
    tops = [sum_rotated(top_product(lay, table, info, part_of, own)) for part_of in gathered]
    tops = [top.reshape(-1, 1, BLK, width) for top in tops]
    sigma_top = jnp.concatenate(tops, axis=1).reshape(-1, width)

    pairs_of = pattern.shape[1] // 2
    shift = ((rows - 1 - me_row) * (pairs_of // rows)).astype(jnp.int32)[None]
    product = panel_product(lay, pattern[0], table, shift, gathered, normed)
    sigma_panel = -sum_rotated(product).reshape(-1, normed.shape[1])

    updates = [contract_rows(own_rows, sigma_panel)]
    for t in range(1, cols):
        piece = jnp.where(me_col >= t, right[t], left[cols - t])
        updates.append(contract_rows(piece, sigma_panel))
    ordered = jnp.stack(updates[::-1] + updates[::-1])
    first = (cols - 1 - me_col + (me_row + 1) * (cols // rows)) % cols
    update = sum_rotated(lax.dynamic_slice_in_dim(ordered, first, cols, 0))
    sigma_diag = diag_inverse[0] - update.reshape(diag_inverse.shape[1:])
    return (sigma_top, sigma_panel[None], sigma_diag[None])


def solution(mesh):
    placed = (
        P("row", ("leaf", "col")),
        P("leaf", None),
        P("leaf", None, "col"),
        P("leaf", "row", "col"),
    )

    def whole(top_inverse, pattern, panel, diag_inverse):
        rows, leaves, cols = (mesh.shape[axis] for axis in ("row", "leaf", "col"))
        size = top_inverse.shape[0]
        lay = Layout(rows, leaves, cols, size // rows // 2, size // leaves // cols)
        return jax.shard_map(
            functools.partial(per_device, lay),
            mesh=mesh,
            in_specs=placed,
            out_specs=(P("row", ("leaf", "col")), P("leaf", "row", "col"), P("leaf", "row", "col")),
            check_vma=False,
        )(top_inverse, pattern, panel, diag_inverse)

    return whole
```

```python
import functools

import jax
import jax.numpy as jnp
import numpy as np
from jax import lax
from jax.experimental import pallas as pl
from jax.experimental.pallas import tpu as pltpu
from jax.sharding import PartitionSpec as P

BLK = 128
VMEM_BYTES = 58 * 1024 * 1024


def halves(value):
    high = value.astype(jnp.bfloat16)
    low = (value - high.astype(jnp.float32)).astype(jnp.bfloat16)
    return high, low


def dot(left, right):
    return jnp.dot(left, right, preferred_element_type=jnp.float32)


class Layout:
    def __init__(self, rows, leaves, cols, half, width):
        self.leaves, self.cols, self.half, self.width = leaves, cols, half, width
        self.part = half // leaves
        self.span = width * cols
        self.counts, self.holder, self.source = [], [], []
        for r in range(rows):
            count = [min(leaves, (q * half + half - 1) // self.span + 1) for q in (2 * r + 1, 2 * (rows - 1 - r))]
            assert count[0] + count[1] <= leaves + 1
            free = list(range(count[1], leaves))
            moved = [leaf for leaf in range(1, count[0]) if leaf not in free]
            slot = {leaf: leaf for leaf in range(1, count[0]) if leaf in free}
            left = [s for s in free if s not in slot]
            slot.update(zip(moved, left))
            self.counts.append(count)
            self.holder.append(slot)
        table = np.full((rows, 2, leaves, leaves), -1, np.int32)
        for r in range(rows):
            for j in range(leaves):
                table[r, 0, 0, j] = j * (leaves + 1) + leaves
                for leaf, slot in self.holder[r].items():
                    table[r, 0, leaf, j] = slot * (leaves + 1) + j
                for leaf in range(self.counts[r][1]):
                    table[r, 1, leaf, j] = leaf * (leaves + 1) + j
        self.table = table


def place_of(lay, pat, k):
    first = pat[k] * BLK
    leaf = first // lay.span
    rest = first - leaf * lay.span
    col = rest // lay.width
    return leaf, col, (rest - col * lay.width) // BLK


def fetch_entry(lay, pat, tab, gathered, t, sems, k):
    leaf, col, sub = place_of(lay, pat, k)
    for s in range(2):
        here = tab[s, leaf, 0] >= 0

        @pl.when(here)
        def _():
            for j in range(lay.leaves):
                entry = tab[s, leaf, j]
                slot = entry // (lay.leaves + 1)
                position = entry - slot * (lay.leaves + 1)
                for which in range(len(gathered)):

                    @pl.when(sub == which)
                    def _():
                        pltpu.make_async_copy(
                            gathered[which].at[slot * lay.cols + col, position],
                            t.at[k, s, pl.ds(j * lay.part, lay.part)],
                            sems.at[k, s],
                        ).start()

        @pl.when(jnp.logical_not(here))
        def _():
            t[k, s] = jnp.zeros(t.shape[2:], t.dtype)


def any_valid(lay, pat, tab, kp, s):
    first = tab[s, place_of(lay, pat, 2 * kp)[0], 0] >= 0
    second = tab[s, place_of(lay, pat, 2 * kp + 1)[0], 0] >= 0
    return jnp.logical_or(first, second)


def wait_pair(lay, pat, tab, t, sems, kp, s):
    for m in range(2):
        k = 2 * kp + m

        @pl.when(tab[s, place_of(lay, pat, k)[0], 0] >= 0)
        def _():
            pltpu.make_async_copy(t.at[k, s], t.at[k, s], sems.at[k, s]).wait()


def back_product(turned_high, turned_low, high, low, s):
    return dot(turned_high[s], high) + dot(turned_low[s], high) + dot(turned_high[s], low)


def panel_kernel(lay, rows, pat, tab, order, *refs):
    count = lay.width // BLK
    gathered, p_ref = refs[:count], refs[count]
    outs = refs[count + 1 : count + rows]
    turned_high, turned_low, t, th, tl, image, sems = refs[count + rows :]
    number = t.shape[0]
    each = number // 2 // rows

    @pl.loop(0, number)
    def _(k):
        fetch_entry(lay, pat, tab, gathered, t, sems, k)

    image[...] = jnp.zeros_like(image)

    @pl.loop(0, number // 2)
    def _(kp):
        span = pl.ds(pl.multiple_of(kp * 2 * BLK, 2 * BLK), 2 * BLK)
        p_high, p_low = halves(p_ref[span, :])
        stacked = jnp.concatenate([p_high, p_low, p_high], axis=0)
        for s in range(2):
            wait_pair(lay, pat, tab, t, sems, kp, s)

            @pl.when(any_valid(lay, pat, tab, kp, s))
            def _():
                high, low = halves(jnp.concatenate([t[2 * kp, s], t[2 * kp + 1, s]], axis=1))
                th[kp, s] = high
                tl[kp, s] = low
                image[s] += dot(jnp.concatenate([high, high, low], axis=1), stacked)

    for s in range(2):
        high, low = halves(image[s].T)
        turned_high[s] = high
        turned_low[s] = low

    for a in range(rows - 1):

        @pl.loop(0, each)
        def _(i):
            kp = order[a] * each + i
            out = outs[a].at[i]
            out[...] = jnp.zeros(out.shape, out.dtype)
            for s in range(2):

                @pl.when(any_valid(lay, pat, tab, kp, s))
                def _():
                    out[...] += back_product(turned_high, turned_low, th[kp, s], tl[kp, s], s).T


def own_panel_kernel(lay, rows, pat, tab, order, *refs):
    count = lay.width // BLK
    gathered, (turned_high, turned_low, out_ref, t, sems) = refs[:count], refs[count:]
    each = t.shape[0] // 2 // rows
    first = order[rows - 1] * each

    @pl.loop(0, 2 * each)
    def _(i):
        fetch_entry(lay, pat, tab, gathered, t, sems, 2 * first + i)

    @pl.loop(0, each)
    def _(i):
        kp = first + i
        out = out_ref.at[i]
        out[...] = jnp.zeros(out.shape, out.dtype)
        for s in range(2):
            wait_pair(lay, pat, tab, t, sems, kp, s)

            @pl.when(any_valid(lay, pat, tab, kp, s))
            def _():
                high, low = halves(jnp.concatenate([t[2 * kp, s], t[2 * kp + 1, s]], axis=1))
                out[...] += back_product(turned_high, turned_low, high, low, s).T


ANY = pl.BlockSpec(memory_space=pl.ANY)
VMEM = pl.BlockSpec(memory_space=pltpu.VMEM)
SMEM = pl.BlockSpec(memory_space=pltpu.SMEM)


def estimate(flops, values):
    return pl.CostEstimate(flops=flops, bytes_accessed=4 * values, transcendentals=0)


def panel_product(lay, pattern, table, order, gathered, normed):
    number, wide, rows = pattern.shape[0], normed.shape[1], order.shape[0]
    half = lay.half
    pairs = number // 2
    block = jax.ShapeDtypeStruct((pairs // rows, 2 * BLK, wide), jnp.float32)
    turned = jax.ShapeDtypeStruct((2, wide, half), jnp.bfloat16)
    result = pl.pallas_call(
        functools.partial(panel_kernel, lay, rows),
        out_shape=[block] * (rows - 1) + [turned] * 2,
        in_specs=[SMEM] * 3 + [ANY] * len(gathered) + [VMEM],
        out_specs=[VMEM] * (rows + 1),
        scratch_shapes=[
            pltpu.VMEM((number, 2, half, BLK), jnp.float32),
            pltpu.VMEM((pairs, 2, half, 2 * BLK), jnp.bfloat16),
            pltpu.VMEM((pairs, 2, half, 2 * BLK), jnp.bfloat16),
            pltpu.VMEM((2, half, wide), jnp.float32),
            pltpu.SemaphoreType.DMA((number, 2)),
        ],
        compiler_params=pltpu.CompilerParams(vmem_limit_bytes=VMEM_BYTES),
        cost_estimate=estimate(18 * half * number * BLK * wide, 2 * half * number * BLK),
    )(pattern, table, order, *gathered, normed)
    return result[: rows - 1], result[rows - 1 :]


def own_panel_product(lay, pattern, table, order, gathered, turned):
    number, wide, rows = pattern.shape[0], turned[0].shape[1], order.shape[0]
    half = lay.half
    return pl.pallas_call(
        functools.partial(own_panel_kernel, lay, rows),
        out_shape=jax.ShapeDtypeStruct((number // 2 // rows, 2 * BLK, wide), jnp.float32),
        in_specs=[SMEM] * 3 + [ANY] * len(gathered) + [VMEM] * 2,
        out_specs=VMEM,
        scratch_shapes=[
            pltpu.VMEM((number, 2, half, BLK), jnp.float32),
            pltpu.SemaphoreType.DMA((number, 2)),
        ],
        compiler_params=pltpu.CompilerParams(vmem_limit_bytes=VMEM_BYTES),
        cost_estimate=estimate(6 * half * number * BLK * wide, half * number * BLK),
    )(pattern, table, order, *gathered, *turned)


def top_kernel(lay, rows, tab, info, g_ref, own_ref, *refs):
    outs, own_turned = refs[:rows], refs[rows]
    blocks = g_ref.shape[0]
    parts = lay.leaves
    each = blocks // 2 // rows
    for s in range(2):

        @pl.loop(0, parts)
        def _(j):
            high, low = halves(own_ref[s, j].T)
            own_turned[s, j] = jnp.concatenate([high, low, high], axis=1)

    for a in range(rows):

        @pl.loop(0, each)
        def _(i):
            block = 2 * (info[a] * each + i)
            leaf = block // lay.cols
            col = block - leaf * lay.cols
            out = outs[a].at[i]
            out[...] = jnp.zeros(out.shape, out.dtype)
            for s in range(2):

                @pl.when(jnp.logical_and(tab[s, leaf, 0] >= 0, tab[s, info[rows], 0] >= 0))
                def _():
                    total = None
                    for j in range(parts):
                        entry = tab[s, leaf, j]
                        slot = entry // (parts + 1)
                        position = entry - slot * (parts + 1)
                        at = slot * lay.cols + col
                        both = jnp.concatenate([g_ref[at, position], g_ref[at + 1, position]], axis=1)
                        high, low = halves(both)
                        term = dot(own_turned[s, j], jnp.concatenate([high, high, low], axis=0))
                        total = term if total is None else total + term
                    out[...] += total.T


def top_product(lay, table, info, gathered, own):
    blocks, rows = gathered.shape[0], info.shape[0] - 1
    parts, part, width = lay.leaves, lay.part, lay.width
    block = jax.ShapeDtypeStruct((blocks // 2 // rows, 2 * BLK, width), jnp.float32)
    return pl.pallas_call(
        functools.partial(top_kernel, lay, rows),
        out_shape=[block] * rows,
        in_specs=[SMEM, SMEM, VMEM, VMEM],
        out_specs=[VMEM] * rows,
        scratch_shapes=[pltpu.VMEM((2, parts, width, 3 * part), jnp.bfloat16)],
        compiler_params=pltpu.CompilerParams(vmem_limit_bytes=VMEM_BYTES),
        cost_estimate=estimate(12 * lay.half * blocks * BLK * width, gathered.size),
    )(table, info, gathered, own)


def diagonal_kernel(cols, info, *refs):
    lefts, own, rights = refs[: cols - 1], refs[cols - 1], refs[cols : 2 * cols - 1]
    sigma, out_ref, held, sems = refs[2 * cols - 1 :]
    each = out_ref.shape[0]
    sources = {0: own}
    for t in range(1, cols):
        sources[t], sources[-t] = lefts[t - 1], rights[t - 1]
    for i in range(each):
        away = info[0] * each + i - info[1]
        for step, source in sources.items():

            @pl.when(away == step)
            def _():
                pltpu.make_async_copy(source, held.at[i], sems.at[i]).start()

    turned_high, turned_low = halves(sigma[...].T)
    for i in range(each):
        pltpu.make_async_copy(held.at[i], held.at[i], sems.at[i]).wait()
        high, low = halves(held[i])
        total = dot(turned_high, high) + dot(turned_low, high) + dot(turned_high, low)
        out_ref[i] = total.T


def diagonal_product(info, rows, lefts, own, rights, sigma):
    cols = len(lefts) + 1
    each = cols // rows
    depth, wide = sigma.shape
    return pl.pallas_call(
        functools.partial(diagonal_kernel, cols),
        out_shape=jax.ShapeDtypeStruct((each, wide, wide), jnp.float32),
        in_specs=[SMEM] + [ANY] * (2 * cols - 1) + [VMEM],
        out_specs=VMEM,
        scratch_shapes=[pltpu.VMEM((each, depth, wide), jnp.float32), pltpu.SemaphoreType.DMA((each,))],
        compiler_params=pltpu.CompilerParams(vmem_limit_bytes=VMEM_BYTES),
        cost_estimate=estimate(6 * each * depth * wide * wide, (each + 1) * depth * wide),
    )(info, *lefts, own, *rights, sigma)


def after(value, *earlier):
    return pl.pallas_call(
        lambda *refs: None,
        out_shape=jax.ShapeDtypeStruct(value.shape, value.dtype),
        in_specs=[ANY] * (1 + len(earlier)),
        out_specs=ANY,
        input_output_aliases={0: 0},
        cost_estimate=estimate(0, 0),
    )(value, *earlier)


def sum_over_rows(sent, own):
    rows = lax.axis_size("row")
    for a, value in enumerate(sent):
        own = own + lax.ppermute(value, "row", [(i, (i + a + 1) % rows) for i in range(rows)])
    return own


def per_device(lay, top_inverse, pattern, panel, diag_inverse):
    rows, cols, leaves = (lax.axis_size(axis) for axis in ("row", "col", "leaf"))
    me_row, me_col, me_leaf = (lax.axis_index(axis) for axis in ("row", "col", "leaf"))
    half, width, parts, part = lay.half, lay.width, lay.leaves, lay.part
    normed = panel[0]

    own_rows = lax.dynamic_slice_in_dim(normed, me_row * (normed.shape[0] // rows), normed.shape[0] // rows, 0)

    def hop(value, step, way):
        if way > 0:
            return lax.ppermute(value, "col", [(i, i + 1) for i in range(step, cols - 1)])
        return lax.ppermute(value, "col", [(i, i - 1) for i in range(1, cols - step)])

    right, left = [hop(own_rows, 0, 1)], [hop(own_rows, 0, -1)]

    table = jnp.asarray(lay.table)[me_row]
    second = jnp.asarray([count[1] for count in lay.counts], jnp.int32)[me_row]
    is_moved = np.zeros((rows, leaves), bool)
    pairs = []
    for r in range(rows):
        for leaf, slot in lay.holder[r].items():
            if leaf != slot:
                is_moved[r, slot] = True
                pairs.append((leaf * rows + r, slot * rows + r))
    moved_here = jnp.asarray(is_moved)[me_row, me_leaf]
    gathered, own, held = [], [], None
    for sub in range(width // BLK):
        lanes = slice(sub * BLK, (sub + 1) * BLK)
        lower, upper = top_inverse[half:, lanes], top_inverse[:half, lanes]
        if held is not None:
            lower, upper = after(lower, held), after(upper, held)
        swapped = lax.ppermute(upper, "row", [(r, rows - 1 - r) for r in range(rows)])
        moved = lax.ppermute(lower, ("leaf", "row"), pairs) if pairs else lower
        whole = jnp.where(me_leaf < second, swapped, jnp.where(moved_here, moved, lower))
        extra = lower[:part]
        for j in range(1, parts):
            sent = lax.ppermute(lower[j * part : (j + 1) * part], "leaf", [(0, j)])
            extra = jnp.where(me_leaf == j, sent, extra)
        earlier = held
        held = jnp.concatenate([whole.reshape(parts, part, BLK), extra[None]], axis=0)
        if earlier is not None:
            held = after(held, right[0], left[0])
        gathered.append(lax.all_gather(held, ("leaf", "col"), axis=0, tiled=False))
        own.append(jnp.stack([lower, swapped]))
    own = jnp.concatenate(own, axis=2).reshape(2, parts, part, width)

    right[0], left[0] = after(right[0], gathered[-1]), after(left[0], gathered[-1])
    for step in range(1, cols - 1):
        right.append(hop(right[-1], step, 1))
        left.append(hop(left[-1], step, -1))

    order = ((me_row + 1 + jnp.arange(rows)) % rows).astype(jnp.int32)
    info = jnp.append(order, me_leaf.astype(jnp.int32))
    tops = [top_product(lay, table, info, part_of, own) for part_of in gathered[:-1]]
    tops = [sum_over_rows(top[:-1], top[-1]) for top in tops]
    if tops:
        order = after(order, tops[-1])

    sent, turned = panel_product(lay, pattern[0], table, order, gathered, normed)
    kept = own_panel_product(lay, pattern[0], table, order, gathered, turned)
    sigma_panel = -sum_over_rows(sent, kept).reshape(-1, normed.shape[1])

    *away, here = top_product(lay, table, after(info, kept), gathered[-1], own)
    tops.append(sum_over_rows([after(value, sigma_panel) for value in away], here))
    sigma_top = jnp.concatenate([top.reshape(-1, 1, BLK, width) for top in tops], axis=1).reshape(-1, width)

    terms = [
        diagonal_product(jnp.stack([order[a], me_col.astype(jnp.int32)]), rows, left, own_rows, right, sigma_panel)
        for a in range(rows)
    ]
    update = sum_over_rows(terms[:-1], terms[-1])
    sigma_diag = diag_inverse[0] - update.reshape(diag_inverse.shape[1:])
    return (sigma_top, sigma_panel[None], sigma_diag[None])


def solution(mesh):
    placed = (
        P("row", ("leaf", "col")),
        P("leaf", None),
        P("leaf", None, "col"),
        P("leaf", "row", "col"),
    )

    def whole(top_inverse, pattern, panel, diag_inverse):
        rows, leaves, cols = (mesh.shape[axis] for axis in ("row", "leaf", "col"))
        size = top_inverse.shape[0]
        lay = Layout(rows, leaves, cols, size // rows // 2, size // leaves // cols)
        return jax.shard_map(
            functools.partial(per_device, lay),
            mesh=mesh,
            in_specs=placed,
            out_specs=(P("row", ("leaf", "col")), P("leaf", "row", "col"), P("leaf", "row", "col")),
            check_vma=False,
        )(top_inverse, pattern, panel, diag_inverse)

    return whole
```

```python
import functools

import jax
import jax.numpy as jnp
import numpy as np
from jax import lax
from jax.experimental import pallas as pl
from jax.experimental.pallas import tpu as pltpu
from jax.sharding import PartitionSpec as P

BLK = 128
VMEM_BYTES = 58 * 1024 * 1024


def halves(value):
    high = value.astype(jnp.bfloat16)
    low = (value - high.astype(jnp.float32)).astype(jnp.bfloat16)
    return high, low


def dot(left, right):
    return jnp.dot(left, right, preferred_element_type=jnp.float32)


class Layout:
    def __init__(self, rows, leaves, cols, half, width):
        self.rows, self.leaves, self.cols, self.half, self.width = rows, leaves, cols, half, width
        self.part = half // leaves
        self.span = width * cols
        self.counts, self.holder, self.source = [], [], []
        for r in range(rows):
            count = [min(leaves, (q * half + half - 1) // self.span + 1) for q in (2 * r + 1, 2 * (rows - 1 - r))]
            assert count[0] + count[1] <= leaves + 1
            free = list(range(count[1], leaves))
            moved = [leaf for leaf in range(1, count[0]) if leaf not in free]
            slot = {leaf: leaf for leaf in range(1, count[0]) if leaf in free}
            left = [s for s in free if s not in slot]
            slot.update(zip(moved, left))
            self.counts.append(count)
            self.holder.append(slot)
        table = np.full((rows, 2, leaves, leaves), -1, np.int32)
        for r in range(rows):
            for j in range(leaves):
                table[r, 0, 0, j] = j * (leaves + 1) + leaves
                for leaf, slot in self.holder[r].items():
                    table[r, 0, leaf, j] = slot * (leaves + 1) + j
                for leaf in range(self.counts[r][1]):
                    table[r, 1, leaf, j] = leaf * (leaves + 1) + j
        self.table = table


def place_of(lay, pat, k):
    first = pat[k] * BLK
    leaf = first // lay.span
    rest = first - leaf * lay.span
    col = rest // lay.width
    return leaf, col, (rest - col * lay.width) // BLK


def fetch_entry(lay, pat, tab, gathered, t, sems, k):
    leaf, col, sub = place_of(lay, pat, k)
    lanes = pl.ds(pl.multiple_of(sub * BLK, BLK), BLK)
    for s in range(2):
        here = tab[s, leaf, 0] >= 0

        @pl.when(here)
        def _():
            for j in range(lay.leaves):
                entry = tab[s, leaf, j]
                slot = entry // (lay.leaves + 1)
                position = entry - slot * (lay.leaves + 1)
                pltpu.make_async_copy(
                    gathered.at[slot * lay.cols + col, position, :, lanes],
                    t.at[k, s, pl.ds(j * lay.part, lay.part)],
                    sems.at[k, s],
                ).start()

        @pl.when(jnp.logical_not(here))
        def _():
            t[k, s] = jnp.zeros(t.shape[2:], t.dtype)


def any_valid(lay, pat, tab, kp, s):
    first = tab[s, place_of(lay, pat, 2 * kp)[0], 0] >= 0
    second = tab[s, place_of(lay, pat, 2 * kp + 1)[0], 0] >= 0
    return jnp.logical_or(first, second)


def wait_pair(lay, pat, tab, t, sems, kp, s):
    for m in range(2):
        k = 2 * kp + m

        @pl.when(tab[s, place_of(lay, pat, k)[0], 0] >= 0)
        def _():
            pltpu.make_async_copy(t.at[k, s], t.at[k, s], sems.at[k, s]).wait()


def back_product(turned_high, turned_low, high, low, s):
    return dot(turned_high[s], high) + dot(turned_low[s], high) + dot(turned_high[s], low)


def panel_kernel(lay, rows, pat, tab, order, gathered, p_ref, *refs):
    outs = refs[: rows - 1]
    turned_high, turned_low, t, th, tl, image, sems = refs[rows - 1 :]
    number = t.shape[0]
    each = number // 2 // rows

    @pl.loop(0, number)
    def _(k):
        fetch_entry(lay, pat, tab, gathered, t, sems, k)

    image[...] = jnp.zeros_like(image)

    @pl.loop(0, number // 2)
    def _(kp):
        span = pl.ds(pl.multiple_of(kp * 2 * BLK, 2 * BLK), 2 * BLK)
        p_high, p_low = halves(p_ref[span, :])
        stacked = jnp.concatenate([p_high, p_low, p_high], axis=0)
        for s in range(2):
            wait_pair(lay, pat, tab, t, sems, kp, s)

            @pl.when(any_valid(lay, pat, tab, kp, s))
            def _():
                high, low = halves(jnp.concatenate([t[2 * kp, s], t[2 * kp + 1, s]], axis=1))
                th[kp, s] = high
                tl[kp, s] = low
                image[s] += dot(jnp.concatenate([high, high, low], axis=1), stacked)

    for s in range(2):
        high, low = halves(image[s].T)
        turned_high[s] = high
        turned_low[s] = low

    for a in range(rows - 1):

        @pl.loop(0, each)
        def _(i):
            kp = order[a] * each + i
            out = outs[a].at[i]
            out[...] = jnp.zeros(out.shape, out.dtype)
            for s in range(2):

                @pl.when(any_valid(lay, pat, tab, kp, s))
                def _():
                    out[...] += back_product(turned_high, turned_low, th[kp, s], tl[kp, s], s).T


def own_panel_kernel(lay, rows, pat, tab, order, gathered, turned_high, turned_low, out_ref, t, sems):
    each = t.shape[0] // 2 // rows
    first = order[rows - 1] * each

    @pl.loop(0, 2 * each)
    def _(i):
        fetch_entry(lay, pat, tab, gathered, t, sems, 2 * first + i)

    @pl.loop(0, each)
    def _(i):
        kp = first + i
        out = out_ref.at[i]
        out[...] = jnp.zeros(out.shape, out.dtype)
        for s in range(2):
            wait_pair(lay, pat, tab, t, sems, kp, s)

            @pl.when(any_valid(lay, pat, tab, kp, s))
            def _():
                high, low = halves(jnp.concatenate([t[2 * kp, s], t[2 * kp + 1, s]], axis=1))
                out[...] += back_product(turned_high, turned_low, high, low, s).T


ANY = pl.BlockSpec(memory_space=pl.ANY)
VMEM = pl.BlockSpec(memory_space=pltpu.VMEM)
SMEM = pl.BlockSpec(memory_space=pltpu.SMEM)


def estimate(flops, values):
    return pl.CostEstimate(flops=flops, bytes_accessed=4 * values, transcendentals=0)


def panel_product(lay, pattern, table, order, gathered, normed):
    number, wide, rows = pattern.shape[0], normed.shape[1], order.shape[0]
    half = lay.half
    pairs = number // 2
    block = jax.ShapeDtypeStruct((pairs // rows, 2 * BLK, wide), jnp.float32)
    turned = jax.ShapeDtypeStruct((2, wide, half), jnp.bfloat16)
    result = pl.pallas_call(
        functools.partial(panel_kernel, lay, rows),
        out_shape=[block] * (rows - 1) + [turned] * 2,
        in_specs=[SMEM] * 3 + [ANY, VMEM],
        out_specs=[VMEM] * (rows + 1),
        scratch_shapes=[
            pltpu.VMEM((number, 2, half, BLK), jnp.float32),
            pltpu.VMEM((pairs, 2, half, 2 * BLK), jnp.bfloat16),
            pltpu.VMEM((pairs, 2, half, 2 * BLK), jnp.bfloat16),
            pltpu.VMEM((2, half, wide), jnp.float32),
            pltpu.SemaphoreType.DMA((number, 2)),
        ],
        compiler_params=pltpu.CompilerParams(vmem_limit_bytes=VMEM_BYTES),
        cost_estimate=estimate(18 * half * number * BLK * wide, 2 * half * number * BLK),
    )(pattern, table, order, gathered, normed)
    return result[: rows - 1], result[rows - 1 :]


def own_panel_product(lay, pattern, table, order, gathered, turned):
    number, wide, rows = pattern.shape[0], turned[0].shape[1], order.shape[0]
    half = lay.half
    return pl.pallas_call(
        functools.partial(own_panel_kernel, lay, rows),
        out_shape=jax.ShapeDtypeStruct((number // 2 // rows, 2 * BLK, wide), jnp.float32),
        in_specs=[SMEM] * 3 + [ANY, VMEM, VMEM],
        out_specs=VMEM,
        scratch_shapes=[
            pltpu.VMEM((number, 2, half, BLK), jnp.float32),
            pltpu.SemaphoreType.DMA((number, 2)),
        ],
        compiler_params=pltpu.CompilerParams(vmem_limit_bytes=VMEM_BYTES),
        cost_estimate=estimate(6 * half * number * BLK * wide, half * number * BLK),
    )(pattern, table, order, gathered, *turned)


def top_kernel(lay, chunks, chunk, tab, dests, leaf_ref, g_ref, own_ref, *refs):
    count = dests.shape[0]
    outs, (own_turned, held, sems) = refs[:count], refs[count:]
    parts, part = lay.leaves, lay.part
    each = outs[0].shape[0]

    def place(a, i):
        block = (dests[a] * chunks + chunk) * each + i
        leaf = block // lay.cols
        return leaf, block - leaf * lay.cols

    def wanted(leaf, s):
        return jnp.logical_and(tab[s, leaf, 0] >= 0, tab[s, leaf_ref[0], 0] >= 0)

    for a in range(count):

        @pl.loop(0, each)
        def _(i):
            leaf, col = place(a, i)
            for s in range(2):

                @pl.when(wanted(leaf, s))
                def _():
                    for j in range(parts):
                        entry = tab[s, leaf, j]
                        slot = entry // (parts + 1)
                        position = entry - slot * (parts + 1)
                        pltpu.make_async_copy(
                            g_ref.at[slot * lay.cols + col, position],
                            held.at[a, i, s, pl.ds(j * part, part)],
                            sems.at[a, i, s],
                        ).start()

    for s in range(2):
        high, low = halves(own_ref[s].T)
        own_turned[s, 0] = high
        own_turned[s, 1] = low

    for a in range(count):

        @pl.loop(0, each)
        def _(i):
            leaf, col = place(a, i)
            out = outs[a].at[i]
            out[...] = jnp.zeros(out.shape, out.dtype)
            for s in range(2):

                @pl.when(wanted(leaf, s))
                def _():
                    pltpu.make_async_copy(held.at[a, i, s], held.at[a, i, s], sems.at[a, i, s]).wait()
                    high, low = halves(held[a, i, s])
                    total = dot(own_turned[s, 0], high) + dot(own_turned[s, 1], high) + dot(own_turned[s, 0], low)
                    out[...] += total.T


def top_product(lay, table, dests, me_leaf, gathered, own, chunks, chunk):
    count, width, half = dests.shape[0], lay.width, lay.half
    each = gathered.shape[0] // lay.rows // chunks
    block = jax.ShapeDtypeStruct((each, width, width), jnp.float32)
    return pl.pallas_call(
        functools.partial(top_kernel, lay, chunks, chunk),
        out_shape=[block] * count,
        in_specs=[SMEM] * 3 + [ANY, VMEM],
        out_specs=[VMEM] * count,
        scratch_shapes=[
            pltpu.VMEM((2, 2, width, half), jnp.bfloat16),
            pltpu.VMEM((count, each, 2, half, width), jnp.float32),
            pltpu.SemaphoreType.DMA((count, each, 2)),
        ],
        compiler_params=pltpu.CompilerParams(vmem_limit_bytes=VMEM_BYTES),
        cost_estimate=estimate(12 * half * count * each * width * width, 2 * half * count * each * width),
    )(table, dests, me_leaf, gathered, own)


def diagonal_kernel(cols, info, *refs):
    lefts, own, rights = refs[: cols - 1], refs[cols - 1], refs[cols : 2 * cols - 1]
    sigma, out_ref, held, sems = refs[2 * cols - 1 :]
    each = out_ref.shape[0]
    sources = {0: own}
    for t in range(1, cols):
        sources[t], sources[-t] = lefts[t - 1], rights[t - 1]
    for i in range(each):
        away = info[0] * each + i - info[1]
        for step, source in sources.items():

            @pl.when(away == step)
            def _():
                pltpu.make_async_copy(source, held.at[i], sems.at[i]).start()

    turned_high, turned_low = halves(sigma[...].T)
    for i in range(each):
        pltpu.make_async_copy(held.at[i], held.at[i], sems.at[i]).wait()
        high, low = halves(held[i])
        total = dot(turned_high, high) + dot(turned_low, high) + dot(turned_high, low)
        out_ref[i] = total.T


def diagonal_product(info, rows, lefts, own, rights, sigma):
    cols = len(lefts) + 1
    each = cols // rows
    depth, wide = sigma.shape
    return pl.pallas_call(
        functools.partial(diagonal_kernel, cols),
        out_shape=jax.ShapeDtypeStruct((each, wide, wide), jnp.float32),
        in_specs=[SMEM] + [ANY] * (2 * cols - 1) + [VMEM],
        out_specs=VMEM,
        scratch_shapes=[pltpu.VMEM((each, depth, wide), jnp.float32), pltpu.SemaphoreType.DMA((each,))],
        compiler_params=pltpu.CompilerParams(vmem_limit_bytes=VMEM_BYTES),
        cost_estimate=estimate(6 * each * depth * wide * wide, (each + 1) * depth * wide),
    )(info, *lefts, own, *rights, sigma)


def after(value, *earlier):
    return pl.pallas_call(
        lambda *refs: None,
        out_shape=jax.ShapeDtypeStruct(value.shape, value.dtype),
        in_specs=[ANY] * (1 + len(earlier)),
        out_specs=ANY,
        input_output_aliases={0: 0},
        cost_estimate=estimate(0, 0),
    )(value, *earlier)


def send_over_rows(sent):
    rows = lax.axis_size("row")
    return [lax.ppermute(value, "row", [(i, (i + a + 1) % rows) for i in range(rows)]) for a, value in enumerate(sent)]


def per_device(lay, top_inverse, pattern, panel, diag_inverse):
    rows, cols, leaves = (lax.axis_size(axis) for axis in ("row", "col", "leaf"))
    me_row, me_col, me_leaf = (lax.axis_index(axis) for axis in ("row", "col", "leaf"))
    half, width, parts, part = lay.half, lay.width, lay.leaves, lay.part
    normed = panel[0]

    own_rows = lax.dynamic_slice_in_dim(normed, me_row * (normed.shape[0] // rows), normed.shape[0] // rows, 0)

    def hop(value, step, way):
        if way > 0:
            return lax.ppermute(value, "col", [(i, i + 1) for i in range(step, cols - 1)])
        return lax.ppermute(value, "col", [(i, i - 1) for i in range(1, cols - step)])

    right, left = [hop(own_rows, 0, 1)], [hop(own_rows, 0, -1)]

    table = jnp.asarray(lay.table)[me_row]
    second = jnp.asarray([count[1] for count in lay.counts], jnp.int32)[me_row]
    is_moved = np.zeros((rows, leaves), bool)
    pairs = []
    for r in range(rows):
        for leaf, slot in lay.holder[r].items():
            if leaf != slot:
                is_moved[r, slot] = True
                pairs.append((leaf * rows + r, slot * rows + r))
    moved_here = jnp.asarray(is_moved)[me_row, me_leaf]
    lower, upper = top_inverse[half:], top_inverse[:half]
    swapped = lax.ppermute(upper, "row", [(r, rows - 1 - r) for r in range(rows)])
    moved = lax.ppermute(lower, ("leaf", "row"), pairs) if pairs else lower
    whole = jnp.where(me_leaf < second, swapped, jnp.where(moved_here, moved, lower))
    extra = lower[:part]
    for j in range(1, parts):
        extra = jnp.where(me_leaf == j, lax.ppermute(lower[j * part : (j + 1) * part], "leaf", [(0, j)]), extra)
    held = jnp.concatenate([whole.reshape(parts, part, width), extra[None]], axis=0)
    gathered = lax.all_gather(after(held, right[0], left[0]), ("leaf", "col"), axis=0, tiled=False)
    own = jnp.stack([lower, swapped])

    right[0], left[0] = after(right[0], gathered), after(left[0], gathered)
    for step in range(1, cols - 1):
        right.append(hop(right[-1], step, 1))
        left.append(hop(left[-1], step, -1))

    chunks = 2
    order = ((me_row + 1 + jnp.arange(rows)) % rows).astype(jnp.int32)
    leaf_here = me_leaf.astype(jnp.int32)[None]
    top_args = (leaf_here, gathered, own, chunks)
    early = top_product(lay, table, order[: rows - 1], *top_args, 0)
    early_in = send_over_rows(early)
    sent, turned = panel_product(lay, pattern[0], table, after(order, *early), gathered, normed)
    sent_in = send_over_rows(sent)
    kept = own_panel_product(lay, pattern[0], table, after(order, *early_in), gathered, turned)
    sigma_panel = -sum(sent_in, kept).reshape(-1, normed.shape[1])
    late = top_product(lay, table, after(order[: rows - 1], kept), *top_args, 1)
    late_in = send_over_rows([after(value, sigma_panel) for value in late])

    def diagonal(a, sigma):
        return diagonal_product(jnp.stack([order[a], me_col.astype(jnp.int32)]), rows, left, own_rows, right, sigma)

    terms = [diagonal(a, after(sigma_panel, *late)) for a in range(rows - 1)]
    terms_in = send_over_rows([after(term, *late_in) for term in terms])
    update = sum(terms_in, diagonal(rows - 1, after(sigma_panel, *terms)))
    sigma_diag = diag_inverse[0] - update.reshape(diag_inverse.shape[1:])

    last = after(order[rows - 1 :], *terms)
    tops = [top_product(lay, table, last, *top_args, chunk)[0] for chunk in range(chunks)]
    tops = [sum(early_in, tops[0]), sum(late_in, tops[1])]
    sigma_top = jnp.concatenate(tops, axis=0).reshape(-1, width)
    return (sigma_top, sigma_panel[None], sigma_diag[None])


def solution(mesh):
    placed = (
        P("row", ("leaf", "col")),
        P("leaf", None),
        P("leaf", None, "col"),
        P("leaf", "row", "col"),
    )

    def whole(top_inverse, pattern, panel, diag_inverse):
        rows, leaves, cols = (mesh.shape[axis] for axis in ("row", "leaf", "col"))
        size = top_inverse.shape[0]
        lay = Layout(rows, leaves, cols, size // rows // 2, size // leaves // cols)
        return jax.shard_map(
            functools.partial(per_device, lay),
            mesh=mesh,
            in_specs=placed,
            out_specs=(P("row", ("leaf", "col")), P("leaf", "row", "col"), P("leaf", "row", "col")),
            check_vma=False,
        )(top_inverse, pattern, panel, diag_inverse)

    return whole
```

```python
import functools

import jax
import jax.numpy as jnp
import numpy as np
from jax import lax
from jax.experimental import pallas as pl
from jax.experimental.pallas import tpu as pltpu
from jax.sharding import PartitionSpec as P

BLK = 128
VMEM_BYTES = 58 * 1024 * 1024


def halves(value):
    high = value.astype(jnp.bfloat16)
    low = (value - high.astype(jnp.float32)).astype(jnp.bfloat16)
    return high, low


def dot(left, right):
    return jnp.dot(left, right, preferred_element_type=jnp.float32)


class Layout:
    def __init__(self, rows, leaves, cols, half, width):
        self.rows, self.leaves, self.cols, self.half, self.width = rows, leaves, cols, half, width
        self.part = half // leaves
        self.span = width * cols
        self.counts, self.holder, self.source = [], [], []
        for r in range(rows):
            count = [min(leaves, (q * half + half - 1) // self.span + 1) for q in (2 * r + 1, 2 * (rows - 1 - r))]
            assert count[0] + count[1] <= leaves + 1
            free = list(range(count[1], leaves))
            moved = [leaf for leaf in range(1, count[0]) if leaf not in free]
            slot = {leaf: leaf for leaf in range(1, count[0]) if leaf in free}
            left = [s for s in free if s not in slot]
            slot.update(zip(moved, left))
            self.counts.append(count)
            self.holder.append(slot)
        table = np.full((rows, 2, leaves, leaves), -1, np.int32)
        for r in range(rows):
            for j in range(leaves):
                table[r, 0, 0, j] = j * (leaves + 1) + leaves
                for leaf, slot in self.holder[r].items():
                    table[r, 0, leaf, j] = slot * (leaves + 1) + j
                for leaf in range(self.counts[r][1]):
                    table[r, 1, leaf, j] = leaf * (leaves + 1) + j
        self.table = table


def place_of(lay, pat, k):
    first = pat[k] * BLK
    leaf = first // lay.span
    rest = first - leaf * lay.span
    col = rest // lay.width
    return leaf, col, (rest - col * lay.width) // BLK


def fetch_entry(lay, pat, tab, gathered, t, sems, k):
    leaf, col, sub = place_of(lay, pat, k)
    lanes = pl.ds(pl.multiple_of(sub * BLK, BLK), BLK)
    for s in range(2):
        here = tab[s, leaf, 0] >= 0

        @pl.when(here)
        def _():
            for j in range(lay.leaves):
                entry = tab[s, leaf, j]
                slot = entry // (lay.leaves + 1)
                position = entry - slot * (lay.leaves + 1)
                pltpu.make_async_copy(
                    gathered.at[slot * lay.cols + col, position, :, lanes],
                    t.at[k, s, pl.ds(j * lay.part, lay.part)],
                    sems.at[k, s],
                ).start()

        @pl.when(jnp.logical_not(here))
        def _():
            t[k, s] = jnp.zeros(t.shape[2:], t.dtype)


def any_valid(lay, pat, tab, kp, s):
    first = tab[s, place_of(lay, pat, 2 * kp)[0], 0] >= 0
    second = tab[s, place_of(lay, pat, 2 * kp + 1)[0], 0] >= 0
    return jnp.logical_or(first, second)


def wait_pair(lay, pat, tab, t, sems, kp, s):
    for m in range(2):
        k = 2 * kp + m

        @pl.when(tab[s, place_of(lay, pat, k)[0], 0] >= 0)
        def _():
            pltpu.make_async_copy(t.at[k, s], t.at[k, s], sems.at[k, s]).wait()


def back_product(turned_high, turned_low, high, low, s):
    return dot(turned_high[s], high) + dot(turned_low[s], high) + dot(turned_high[s], low)


def panel_kernel(lay, rows, pat, tab, order, gathered, p_ref, *refs):
    outs = refs[: rows - 1]
    turned_high, turned_low, t, th, tl, image, sems = refs[rows - 1 :]
    number = t.shape[0]
    each = number // 2 // rows

    @pl.loop(0, number)
    def _(k):
        fetch_entry(lay, pat, tab, gathered, t, sems, k)

    image[...] = jnp.zeros_like(image)

    @pl.loop(0, number // 2)
    def _(kp):
        span = pl.ds(pl.multiple_of(kp * 2 * BLK, 2 * BLK), 2 * BLK)
        p_high, p_low = halves(p_ref[span, :])
        stacked = jnp.concatenate([p_high, p_low, p_high], axis=0)
        for s in range(2):
            wait_pair(lay, pat, tab, t, sems, kp, s)

            @pl.when(any_valid(lay, pat, tab, kp, s))
            def _():
                high, low = halves(jnp.concatenate([t[2 * kp, s], t[2 * kp + 1, s]], axis=1))
                th[kp, s] = high
                tl[kp, s] = low
                image[s] += dot(jnp.concatenate([high, high, low], axis=1), stacked)

    for s in range(2):
        high, low = halves(image[s].T)
        turned_high[s] = high
        turned_low[s] = low

    for a in range(rows - 1):

        @pl.loop(0, each)
        def _(i):
            kp = order[a] * each + i
            out = outs[a].at[i]
            out[...] = jnp.zeros(out.shape, out.dtype)
            for s in range(2):

                @pl.when(any_valid(lay, pat, tab, kp, s))
                def _():
                    out[...] += back_product(turned_high, turned_low, th[kp, s], tl[kp, s], s).T


def own_panel_kernel(lay, rows, pat, tab, order, gathered, turned_high, turned_low, out_ref, t, sems):
    each = t.shape[0] // 2 // rows
    first = order[rows - 1] * each

    @pl.loop(0, 2 * each)
    def _(i):
        fetch_entry(lay, pat, tab, gathered, t, sems, 2 * first + i)

    @pl.loop(0, each)
    def _(i):
        kp = first + i
        out = out_ref.at[i]
        out[...] = jnp.zeros(out.shape, out.dtype)
        for s in range(2):
            wait_pair(lay, pat, tab, t, sems, kp, s)

            @pl.when(any_valid(lay, pat, tab, kp, s))
            def _():
                high, low = halves(jnp.concatenate([t[2 * kp, s], t[2 * kp + 1, s]], axis=1))
                out[...] += back_product(turned_high, turned_low, high, low, s).T


ANY = pl.BlockSpec(memory_space=pl.ANY)
VMEM = pl.BlockSpec(memory_space=pltpu.VMEM)
SMEM = pl.BlockSpec(memory_space=pltpu.SMEM)


def estimate(flops, values):
    return pl.CostEstimate(flops=flops, bytes_accessed=4 * values, transcendentals=0)


def panel_product(lay, pattern, table, order, gathered, normed):
    number, wide, rows = pattern.shape[0], normed.shape[1], order.shape[0]
    half = lay.half
    pairs = number // 2
    block = jax.ShapeDtypeStruct((pairs // rows, 2 * BLK, wide), jnp.float32)
    turned = jax.ShapeDtypeStruct((2, wide, half), jnp.bfloat16)
    result = pl.pallas_call(
        functools.partial(panel_kernel, lay, rows),
        out_shape=[block] * (rows - 1) + [turned] * 2,
        in_specs=[SMEM] * 3 + [ANY, VMEM],
        out_specs=[VMEM] * (rows + 1),
        scratch_shapes=[
            pltpu.VMEM((number, 2, half, BLK), jnp.float32),
            pltpu.VMEM((pairs, 2, half, 2 * BLK), jnp.bfloat16),
            pltpu.VMEM((pairs, 2, half, 2 * BLK), jnp.bfloat16),
            pltpu.VMEM((2, half, wide), jnp.float32),
            pltpu.SemaphoreType.DMA((number, 2)),
        ],
        compiler_params=pltpu.CompilerParams(vmem_limit_bytes=VMEM_BYTES),
        cost_estimate=estimate(18 * half * number * BLK * wide, 2 * half * number * BLK),
    )(pattern, table, order, gathered, normed)
    return result[: rows - 1], result[rows - 1 :]


def own_panel_product(lay, pattern, table, order, gathered, turned):
    number, wide, rows = pattern.shape[0], turned[0].shape[1], order.shape[0]
    half = lay.half
    return pl.pallas_call(
        functools.partial(own_panel_kernel, lay, rows),
        out_shape=jax.ShapeDtypeStruct((number // 2 // rows, 2 * BLK, wide), jnp.float32),
        in_specs=[SMEM] * 3 + [ANY, VMEM, VMEM],
        out_specs=VMEM,
        scratch_shapes=[
            pltpu.VMEM((number, 2, half, BLK), jnp.float32),
            pltpu.SemaphoreType.DMA((number, 2)),
        ],
        compiler_params=pltpu.CompilerParams(vmem_limit_bytes=VMEM_BYTES),
        cost_estimate=estimate(24 * half * number * BLK * wide, half * number * BLK),
    )(pattern, table, order, gathered, *turned)


def top_kernel(lay, chunks, chunk, tab, dests, leaf_ref, g_ref, own_ref, *refs):
    count = dests.shape[0]
    outs, (own_turned, held, sems) = refs[:count], refs[count:]
    parts, part = lay.leaves, lay.part
    each = outs[0].shape[0]

    def place(a, i):
        block = (dests[a] * chunks + chunk) * each + i
        leaf = block // lay.cols
        return leaf, block - leaf * lay.cols

    def wanted(leaf, s):
        return jnp.logical_and(tab[s, leaf, 0] >= 0, tab[s, leaf_ref[0], 0] >= 0)

    for a in range(count):

        @pl.loop(0, each)
        def _(i):
            leaf, col = place(a, i)
            for s in range(2):

                @pl.when(wanted(leaf, s))
                def _():
                    for j in range(parts):
                        entry = tab[s, leaf, j]
                        slot = entry // (parts + 1)
                        position = entry - slot * (parts + 1)
                        pltpu.make_async_copy(
                            g_ref.at[slot * lay.cols + col, position],
                            held.at[a, i, s, pl.ds(j * part, part)],
                            sems.at[a, i, s],
                        ).start()

    for s in range(2):
        high, low = halves(own_ref[s].T)
        own_turned[s, 0] = high
        own_turned[s, 1] = low

    for a in range(count):

        @pl.loop(0, each)
        def _(i):
            leaf, col = place(a, i)
            out = outs[a].at[i]
            out[...] = jnp.zeros(out.shape, out.dtype)
            for s in range(2):

                @pl.when(wanted(leaf, s))
                def _():
                    pltpu.make_async_copy(held.at[a, i, s], held.at[a, i, s], sems.at[a, i, s]).wait()
                    high, low = halves(held[a, i, s])
                    total = dot(own_turned[s, 0], high) + dot(own_turned[s, 1], high) + dot(own_turned[s, 0], low)
                    out[...] += total.T


def top_product(lay, table, dests, me_leaf, gathered, own, chunks, chunk):
    count, width, half = dests.shape[0], lay.width, lay.half
    each = gathered.shape[0] // lay.rows // chunks
    block = jax.ShapeDtypeStruct((each, width, width), jnp.float32)
    return pl.pallas_call(
        functools.partial(top_kernel, lay, chunks, chunk),
        out_shape=[block] * count,
        in_specs=[SMEM] * 3 + [ANY, VMEM],
        out_specs=[VMEM] * count,
        scratch_shapes=[
            pltpu.VMEM((2, 2, width, half), jnp.bfloat16),
            pltpu.VMEM((count, each, 2, half, width), jnp.float32),
            pltpu.SemaphoreType.DMA((count, each, 2)),
        ],
        compiler_params=pltpu.CompilerParams(vmem_limit_bytes=VMEM_BYTES),
        cost_estimate=estimate(12 * half * count * each * width * width, 2 * half * count * each * width),
    )(table, dests, me_leaf, gathered, own)


def diagonal_kernel(reach, info, *refs):
    lefts, own, rights = refs[:reach], refs[reach], refs[reach + 1 : 2 * reach + 1]
    sigma, out_ref, held, sems = refs[2 * reach + 1 :]
    each = out_ref.shape[0]
    sources = {0: own}
    for t in range(1, reach + 1):
        sources[t], sources[-t] = lefts[t - 1], rights[t - 1]
    for i in range(each):
        away = info[i] - info[each]
        for step, source in sources.items():

            @pl.when(away == step)
            def _():
                pltpu.make_async_copy(source, held.at[i], sems.at[i]).start()

    turned_high, turned_low = halves(sigma[...].T)
    for i in range(each):
        pltpu.make_async_copy(held.at[i], held.at[i], sems.at[i]).wait()
        high, low = halves(held[i])
        total = dot(turned_high, high) + dot(turned_low, high) + dot(turned_high, low)
        out_ref[i] = total.T


def diagonal_product(blocks, me_col, lefts, own, rights, sigma):
    each, reach = blocks.shape[0], len(lefts)
    depth, wide = sigma.shape
    return pl.pallas_call(
        functools.partial(diagonal_kernel, reach),
        out_shape=jax.ShapeDtypeStruct((each, wide, wide), jnp.float32),
        in_specs=[SMEM] + [ANY] * (2 * reach + 1) + [VMEM],
        out_specs=VMEM,
        scratch_shapes=[pltpu.VMEM((each, depth, wide), jnp.float32), pltpu.SemaphoreType.DMA((each,))],
        compiler_params=pltpu.CompilerParams(vmem_limit_bytes=VMEM_BYTES),
        cost_estimate=estimate(6 * each * depth * wide * wide, (each + 1) * depth * wide),
    )(jnp.append(blocks, me_col).astype(jnp.int32), *lefts, own, *rights, sigma)


def after(value, *earlier):
    return pl.pallas_call(
        lambda *refs: None,
        out_shape=jax.ShapeDtypeStruct(value.shape, value.dtype),
        in_specs=[ANY] * (1 + len(earlier)),
        out_specs=ANY,
        input_output_aliases={0: 0},
        cost_estimate=estimate(0, 0),
    )(value, *earlier)


def send_over_rows(sent):
    rows = lax.axis_size("row")
    return [lax.ppermute(value, "row", [(i, (i + a + 1) % rows) for i in range(rows)]) for a, value in enumerate(sent)]


def per_device(lay, top_inverse, pattern, panel, diag_inverse):
    rows, cols, leaves = (lax.axis_size(axis) for axis in ("row", "col", "leaf"))
    me_row, me_col, me_leaf = (lax.axis_index(axis) for axis in ("row", "col", "leaf"))
    half, width, parts, part = lay.half, lay.width, lay.leaves, lay.part
    normed = panel[0]

    own_rows = lax.dynamic_slice_in_dim(normed, me_row * (normed.shape[0] // rows), normed.shape[0] // rows, 0)

    def hop(value, step, way):
        if way > 0:
            return lax.ppermute(value, "col", [(i, i + 1) for i in range(step, cols - 1)])
        return lax.ppermute(value, "col", [(i, i - 1) for i in range(1, cols - step)])

    table = jnp.asarray(lay.table)[me_row]
    second = jnp.asarray([count[1] for count in lay.counts], jnp.int32)[me_row]
    is_moved = np.zeros((rows, leaves), bool)
    pairs = []
    for r in range(rows):
        for leaf, slot in lay.holder[r].items():
            if leaf != slot:
                is_moved[r, slot] = True
                pairs.append((leaf * rows + r, slot * rows + r))
    moved_here = jnp.asarray(is_moved)[me_row, me_leaf]
    lower, upper = top_inverse[half:], top_inverse[:half]
    swapped = lax.ppermute(upper, "row", [(r, rows - 1 - r) for r in range(rows)])
    moved = lax.ppermute(lower, ("leaf", "row"), pairs) if pairs else lower
    whole = jnp.where(me_leaf < second, swapped, jnp.where(moved_here, moved, lower))
    both = lower[: 2 * part]
    for chip in range(2, leaves, 2):
        both = jnp.where(me_leaf == chip, lax.ppermute(lower[chip * part : (chip + 2) * part], "leaf", [(0, chip)]), both)
    other = lax.ppermute(both[part:], "leaf", [(chip, chip + 1) for chip in range(0, leaves, 2)])
    extra = jnp.where(me_leaf % 2 == 0, both[:part], other)
    held = jnp.concatenate([whole.reshape(parts, part, width), extra[None]], axis=0)
    gathered = lax.all_gather(held, ("leaf", "col"), axis=0, tiled=False)
    own = jnp.stack([lower, swapped])

    start = after(own_rows, gathered)
    right, left = [hop(start, 0, 1)], [hop(start, 0, -1)]

    def hop_on(step, *earlier):
        right.append(hop(after(right[-1], *earlier), step, 1))
        left.append(hop(after(left[-1], *earlier), step, -1))

    chunks, each = 2, cols // rows
    order = ((me_row + 1 + jnp.arange(rows)) % rows).astype(jnp.int32)
    leaf_here = me_leaf.astype(jnp.int32)[None]
    top_args = (leaf_here, gathered, own, chunks)
    early = top_product(lay, table, order[: rows - 1], *top_args, 0)
    early_in = send_over_rows(early)
    sent, turned = panel_product(lay, pattern[0], table, after(order, *early), gathered, normed)
    sent_in = send_over_rows(sent)
    for step in range(1, cols // 2):
        hop_on(step, *sent)
    kept = own_panel_product(lay, pattern[0], table, after(order, *early_in), gathered, turned)
    sigma_panel = -sum(sent_in, kept).reshape(-1, normed.shape[1])
    late = top_product(lay, table, after(order[: rows - 1], kept), *top_args, 1)
    for step in range(cols // 2, cols - 1):
        hop_on(step, sigma_panel, *late)
    late_in = send_over_rows([after(value, sigma_panel) for value in late])

    near = [[sorted(range(d * each, d * each + each), key=lambda block: abs(block - c)) for c in range(cols)] for d in range(rows)]
    near = np.asarray(near, np.int32)
    reach = np.abs(near - np.arange(cols)[None, :, None]).max(axis=(0, 1))
    near_here = jnp.asarray(near)[:, me_col]
    ready, terms_in, terms = after(sigma_panel, *late), [], []
    for i in range(each):
        pieces = (left[: reach[i]], own_rows, right[: reach[i]])
        term = [diagonal_product(near_here[order[a]][i : i + 1], me_col, *pieces, ready) for a in range(rows - 1)]
        terms_in.append(send_over_rows(term))
        terms += term
        ready = after(sigma_panel, *terms)
    mine = me_row * each + jnp.arange(each)
    update = list(diagonal_product(mine, me_col, left, own_rows, right, ready))
    for block in range(each):
        for i in range(each):
            for value in terms_in[i]:
                update[block] += jnp.where(near_here[me_row, i] == mine[block], value[0], 0.0)
    sigma_diag = diag_inverse[0] - jnp.concatenate(update, axis=0)

    last = after(order[rows - 1 :], *terms)
    tops = [top_product(lay, table, last, *top_args, chunk)[0] for chunk in range(chunks)]
    tops = [sum(early_in, tops[0]), sum(late_in, tops[1])]
    sigma_top = jnp.concatenate(tops, axis=0).reshape(-1, width)
    return (sigma_top, sigma_panel[None], sigma_diag[None])


def solution(mesh):
    placed = (
        P("row", ("leaf", "col")),
        P("leaf", None),
        P("leaf", None, "col"),
        P("leaf", "row", "col"),
    )

    def whole(top_inverse, pattern, panel, diag_inverse):
        rows, leaves, cols = (mesh.shape[axis] for axis in ("row", "leaf", "col"))
        size = top_inverse.shape[0]
        lay = Layout(rows, leaves, cols, size // rows // 2, size // leaves // cols)
        return jax.shard_map(
            functools.partial(per_device, lay),
            mesh=mesh,
            in_specs=placed,
            out_specs=(P("row", ("leaf", "col")), P("leaf", "row", "col"), P("leaf", "row", "col")),
            check_vma=False,
        )(top_inverse, pattern, panel, diag_inverse)

    return whole
```

```python
import functools

import jax
import jax.numpy as jnp
import numpy as np
from jax import lax
from jax.experimental import pallas as pl
from jax.experimental.pallas import tpu as pltpu
from jax.sharding import PartitionSpec as P

BLK = 128
VMEM_BYTES = 58 * 1024 * 1024


def halves(value):
    high = value.astype(jnp.bfloat16)
    low = (value - high.astype(jnp.float32)).astype(jnp.bfloat16)
    return high, low


def dot(left, right):
    return jnp.dot(left, right, preferred_element_type=jnp.float32)


class Layout:
    def __init__(self, rows, leaves, cols, half, width):
        self.rows, self.leaves, self.cols, self.half, self.width = rows, leaves, cols, half, width
        self.part = half // leaves
        self.span = width * cols
        self.counts, self.holder, self.source = [], [], []
        for r in range(rows):
            count = [min(leaves, (q * half + half - 1) // self.span + 1) for q in (2 * r + 1, 2 * (rows - 1 - r))]
            assert count[0] + count[1] <= leaves + 1
            free = list(range(count[1], leaves))
            moved = [leaf for leaf in range(1, count[0]) if leaf not in free]
            slot = {leaf: leaf for leaf in range(1, count[0]) if leaf in free}
            left = [s for s in free if s not in slot]
            slot.update(zip(moved, left))
            self.counts.append(count)
            self.holder.append(slot)
        table = np.full((rows, 2, leaves, leaves), -1, np.int32)
        for r in range(rows):
            for j in range(leaves):
                table[r, 0, 0, j] = j * (leaves + 1) + leaves
                for leaf, slot in self.holder[r].items():
                    table[r, 0, leaf, j] = slot * (leaves + 1) + j
                for leaf in range(self.counts[r][1]):
                    table[r, 1, leaf, j] = leaf * (leaves + 1) + j
        self.table = table


def place_of(lay, pat, k):
    first = pat[k] * BLK
    leaf = first // lay.span
    rest = first - leaf * lay.span
    col = rest // lay.width
    return leaf, col, (rest - col * lay.width) // BLK


def fetch_entry(lay, pat, tab, gathered, t, sems, k):
    leaf, col, sub = place_of(lay, pat, k)
    lanes = pl.ds(pl.multiple_of(sub * BLK, BLK), BLK)
    for s in range(2):
        here = tab[s, leaf, 0] >= 0

        @pl.when(here)
        def _():
            for j in range(lay.leaves):
                entry = tab[s, leaf, j]
                slot = entry // (lay.leaves + 1)
                position = entry - slot * (lay.leaves + 1)
                pltpu.make_async_copy(
                    gathered.at[slot * lay.cols + col, position, :, lanes],
                    t.at[k, s, pl.ds(j * lay.part, lay.part)],
                    sems.at[k, s],
                ).start()

        @pl.when(jnp.logical_not(here))
        def _():
            t[k, s] = jnp.zeros(t.shape[2:], t.dtype)


def any_valid(lay, pat, tab, kp, s):
    first = tab[s, place_of(lay, pat, 2 * kp)[0], 0] >= 0
    second = tab[s, place_of(lay, pat, 2 * kp + 1)[0], 0] >= 0
    return jnp.logical_or(first, second)


def wait_pair(lay, pat, tab, t, sems, kp, s):
    for m in range(2):
        k = 2 * kp + m

        @pl.when(tab[s, place_of(lay, pat, k)[0], 0] >= 0)
        def _():
            pltpu.make_async_copy(t.at[k, s], t.at[k, s], sems.at[k, s]).wait()


def back_product(turned_high, turned_low, high, low, s):
    return dot(turned_high[s], high) + dot(turned_low[s], high) + dot(turned_high[s], low)


def panel_kernel(lay, rows, tokens, pat, tab, order, gathered, p_ref, *refs):
    outs = refs[tokens : tokens + rows - 1]
    turned_high, turned_low, t, th, tl, image, sems = refs[tokens + rows - 1 :]
    number = t.shape[0]
    each = number // 2 // rows

    @pl.loop(0, number)
    def _(k):
        fetch_entry(lay, pat, tab, gathered, t, sems, k)

    image[...] = jnp.zeros_like(image)

    @pl.loop(0, number // 2)
    def _(kp):
        span = pl.ds(pl.multiple_of(kp * 2 * BLK, 2 * BLK), 2 * BLK)
        p_high, p_low = halves(p_ref[span, :])
        stacked = jnp.concatenate([p_high, p_low, p_high], axis=0)
        for s in range(2):
            wait_pair(lay, pat, tab, t, sems, kp, s)

            @pl.when(any_valid(lay, pat, tab, kp, s))
            def _():
                high, low = halves(jnp.concatenate([t[2 * kp, s], t[2 * kp + 1, s]], axis=1))
                th[kp, s] = high
                tl[kp, s] = low
                image[s] += dot(jnp.concatenate([high, high, low], axis=1), stacked)

    for s in range(2):
        high, low = halves(image[s].T)
        turned_high[s] = high
        turned_low[s] = low

    for a in range(rows - 1):

        @pl.loop(0, each)
        def _(i):
            kp = order[a] * each + i
            out = outs[a].at[i]
            out[...] = jnp.zeros(out.shape, out.dtype)
            for s in range(2):

                @pl.when(any_valid(lay, pat, tab, kp, s))
                def _():
                    out[...] += back_product(turned_high, turned_low, th[kp, s], tl[kp, s], s).T


def own_panel_kernel(lay, rows, tokens, pat, tab, order, gathered, turned_high, turned_low, *refs):
    out_ref, t, sems = refs[tokens:]
    each = t.shape[0] // 2 // rows
    first = order[rows - 1] * each

    @pl.loop(0, 2 * each)
    def _(i):
        fetch_entry(lay, pat, tab, gathered, t, sems, 2 * first + i)

    @pl.loop(0, each)
    def _(i):
        kp = first + i
        out = out_ref.at[i]
        out[...] = jnp.zeros(out.shape, out.dtype)
        for s in range(2):
            wait_pair(lay, pat, tab, t, sems, kp, s)

            @pl.when(any_valid(lay, pat, tab, kp, s))
            def _():
                high, low = halves(jnp.concatenate([t[2 * kp, s], t[2 * kp + 1, s]], axis=1))
                out[...] += back_product(turned_high, turned_low, high, low, s).T


ANY = pl.BlockSpec(memory_space=pl.ANY)
VMEM = pl.BlockSpec(memory_space=pltpu.VMEM)
SMEM = pl.BlockSpec(memory_space=pltpu.SMEM)


def estimate(flops, values):
    return pl.CostEstimate(flops=flops, bytes_accessed=4 * values, transcendentals=0)


def panel_product(lay, pattern, table, order, gathered, normed, tokens):
    number, wide, rows = pattern.shape[0], normed.shape[1], order.shape[0]
    half = lay.half
    pairs = number // 2
    block = jax.ShapeDtypeStruct((pairs // rows, 2 * BLK, wide), jnp.float32)
    turned = jax.ShapeDtypeStruct((2, wide, half), jnp.bfloat16)
    result = pl.pallas_call(
        functools.partial(panel_kernel, lay, rows, len(tokens)),
        out_shape=[block] * (rows - 1) + [turned] * 2,
        in_specs=[SMEM] * 3 + [ANY, VMEM] + [ANY] * len(tokens),
        out_specs=[VMEM] * (rows + 1),
        scratch_shapes=[
            pltpu.VMEM((number, 2, half, BLK), jnp.float32),
            pltpu.VMEM((pairs, 2, half, 2 * BLK), jnp.bfloat16),
            pltpu.VMEM((pairs, 2, half, 2 * BLK), jnp.bfloat16),
            pltpu.VMEM((2, half, wide), jnp.float32),
            pltpu.SemaphoreType.DMA((number, 2)),
        ],
        compiler_params=pltpu.CompilerParams(vmem_limit_bytes=VMEM_BYTES),
        cost_estimate=estimate(18 * half * number * BLK * wide, 2 * half * number * BLK),
    )(pattern, table, order, gathered, normed, *tokens)
    return result[: rows - 1], result[rows - 1 :]


def own_panel_product(lay, pattern, table, order, gathered, turned, tokens):
    number, wide, rows = pattern.shape[0], turned[0].shape[1], order.shape[0]
    half = lay.half
    return pl.pallas_call(
        functools.partial(own_panel_kernel, lay, rows, len(tokens)),
        out_shape=jax.ShapeDtypeStruct((number // 2 // rows, 2 * BLK, wide), jnp.float32),
        in_specs=[SMEM] * 3 + [ANY, VMEM, VMEM] + [ANY] * len(tokens),
        out_specs=VMEM,
        scratch_shapes=[
            pltpu.VMEM((number, 2, half, BLK), jnp.float32),
            pltpu.SemaphoreType.DMA((number, 2)),
        ],
        compiler_params=pltpu.CompilerParams(vmem_limit_bytes=VMEM_BYTES),
        cost_estimate=estimate(24 * half * number * BLK * wide, half * number * BLK),
    )(pattern, table, order, gathered, *turned, *tokens)


def top_kernel(lay, chunks, chunk, tokens, tab, dests, leaf_ref, g_ref, own_ref, *refs):
    count = dests.shape[0]
    outs, (own_turned, held, sems) = refs[tokens : tokens + count], refs[tokens + count :]
    parts, part = lay.leaves, lay.part
    each = outs[0].shape[0]

    def place(a, i):
        block = (dests[a] * chunks + chunk) * each + i
        leaf = block // lay.cols
        return leaf, block - leaf * lay.cols

    def wanted(leaf, s):
        return jnp.logical_and(tab[s, leaf, 0] >= 0, tab[s, leaf_ref[0], 0] >= 0)

    for a in range(count):

        @pl.loop(0, each)
        def _(i):
            leaf, col = place(a, i)
            for s in range(2):

                @pl.when(wanted(leaf, s))
                def _():
                    for j in range(parts):
                        entry = tab[s, leaf, j]
                        slot = entry // (parts + 1)
                        position = entry - slot * (parts + 1)
                        pltpu.make_async_copy(
                            g_ref.at[slot * lay.cols + col, position],
                            held.at[a, i, s, pl.ds(j * part, part)],
                            sems.at[a, i, s],
                        ).start()

    for s in range(2):
        high, low = halves(own_ref[s].T)
        own_turned[s, 0] = high
        own_turned[s, 1] = low

    for a in range(count):

        @pl.loop(0, each)
        def _(i):
            leaf, col = place(a, i)
            out = outs[a].at[i]
            out[...] = jnp.zeros(out.shape, out.dtype)
            for s in range(2):

                @pl.when(wanted(leaf, s))
                def _():
                    pltpu.make_async_copy(held.at[a, i, s], held.at[a, i, s], sems.at[a, i, s]).wait()
                    high, low = halves(held[a, i, s])
                    total = dot(own_turned[s, 0], high) + dot(own_turned[s, 1], high) + dot(own_turned[s, 0], low)
                    out[...] += total.T


def top_product(lay, table, dests, me_leaf, gathered, own, chunks, chunk, tokens=()):
    count, width, half = dests.shape[0], lay.width, lay.half
    each = gathered.shape[0] // lay.rows // chunks
    block = jax.ShapeDtypeStruct((each, width, width), jnp.float32)
    return pl.pallas_call(
        functools.partial(top_kernel, lay, chunks, chunk, len(tokens)),
        out_shape=[block] * count,
        in_specs=[SMEM] * 3 + [ANY, VMEM] + [ANY] * len(tokens),
        out_specs=[VMEM] * count,
        scratch_shapes=[
            pltpu.VMEM((2, 2, width, half), jnp.bfloat16),
            pltpu.VMEM((count, each, 2, half, width), jnp.float32),
            pltpu.SemaphoreType.DMA((count, each, 2)),
        ],
        compiler_params=pltpu.CompilerParams(vmem_limit_bytes=VMEM_BYTES),
        cost_estimate=estimate(12 * half * count * each * width * width, 2 * half * count * each * width),
    )(table, dests, me_leaf, gathered, own, *tokens)


def diagonal_kernel(steps, tokens, info, *refs):
    sources, refs = list(zip(steps, refs)), refs[len(steps) :]
    sigma, (out_ref, held, sems) = refs[0], refs[1 + tokens :]
    each = out_ref.shape[0]
    for i in range(each):
        away = info[i] - info[each]
        for (step, run), source in sources:

            @pl.when(away == step)
            def _():
                rows = pl.ds(run * source.shape[0], source.shape[0])
                pltpu.make_async_copy(source, held.at[i, rows], sems.at[i]).start()

    turned_high, turned_low = halves(sigma[...].T)
    for i in range(each):
        pltpu.make_async_copy(held.at[i], held.at[i], sems.at[i]).wait()
        high, low = halves(held[i])
        total = dot(turned_high, high) + dot(turned_low, high) + dot(turned_high, low)
        out_ref[i] = total.T


def diagonal_product(blocks, me_col, pieces, sigma, tokens):
    each = blocks.shape[0]
    depth, wide = sigma.shape
    return pl.pallas_call(
        functools.partial(diagonal_kernel, tuple(pieces), len(tokens)),
        out_shape=jax.ShapeDtypeStruct((each, wide, wide), jnp.float32),
        in_specs=[SMEM] + [ANY] * len(pieces) + [VMEM] + [ANY] * len(tokens),
        out_specs=VMEM,
        scratch_shapes=[pltpu.VMEM((each, depth, wide), jnp.float32), pltpu.SemaphoreType.DMA((each,))],
        compiler_params=pltpu.CompilerParams(vmem_limit_bytes=VMEM_BYTES),
        cost_estimate=estimate(6 * each * depth * wide * wide, (each + 1) * depth * wide),
    )(jnp.append(blocks, me_col).astype(jnp.int32), *pieces.values(), sigma, *tokens)


def after(value, *earlier):
    return pl.pallas_call(
        lambda *refs: None,
        out_shape=jax.ShapeDtypeStruct(value.shape, value.dtype),
        in_specs=[ANY] * (1 + len(earlier)),
        out_specs=ANY,
        input_output_aliases={0: 0},
        cost_estimate=estimate(0, 0),
    )(value, *earlier)


def send_over_rows(sent):
    rows = lax.axis_size("row")
    return [lax.ppermute(value, "row", [(i, (i + a + 1) % rows) for i in range(rows)]) for a, value in enumerate(sent)]


def per_device(lay, top_inverse, pattern, panel, diag_inverse):
    rows, cols, leaves = (lax.axis_size(axis) for axis in ("row", "col", "leaf"))
    me_row, me_col, me_leaf = (lax.axis_index(axis) for axis in ("row", "col", "leaf"))
    half, width, parts, part = lay.half, lay.width, lay.leaves, lay.part
    normed = panel[0]

    count = normed.shape[0] // rows
    own_rows = lax.dynamic_slice_in_dim(normed, me_row * count, count, 0)
    runs = 2
    pieces = {(0, run): own_rows[run * count // runs : (run + 1) * count // runs] for run in range(runs)}

    def hop(run, step, *earlier):
        if earlier:
            for key in sorted({(step, run), (-step, run)}):
                pieces[key] = after(pieces[key], *earlier)
        for way in (1, -1):
            at = [i for i in range(cols) if 0 <= i - way * step < cols and 0 <= i + way < cols]
            moved_on = lax.ppermute(pieces[-way * step, run], "col", [(i, i + way) for i in at])
            pieces[-way * (step + 1), run] = moved_on

    hop(0, 0)

    table = jnp.asarray(lay.table)[me_row]
    second = jnp.asarray([count[1] for count in lay.counts], jnp.int32)[me_row]
    is_moved = np.zeros((rows, leaves), bool)
    pairs = []
    for r in range(rows):
        for leaf, slot in lay.holder[r].items():
            if leaf != slot:
                is_moved[r, slot] = True
                pairs.append((leaf * rows + r, slot * rows + r))
    moved_here = jnp.asarray(is_moved)[me_row, me_leaf]
    lower, upper = top_inverse[half:], top_inverse[:half]
    swapped = lax.ppermute(upper, "row", [(r, rows - 1 - r) for r in range(rows)])
    moved = lax.ppermute(lower, ("leaf", "row"), pairs) if pairs else lower
    whole = jnp.where(me_leaf < second, swapped, jnp.where(moved_here, moved, lower))
    both = lower[: 2 * part]
    for chip in range(2, leaves, 2):
        both = jnp.where(me_leaf == chip, lax.ppermute(lower[chip * part : (chip + 2) * part], "leaf", [(0, chip)]), both)
    other = lax.ppermute(both[part:], "leaf", [(chip, chip + 1) for chip in range(0, leaves, 2)])
    extra = jnp.where(me_leaf % 2 == 0, both[:part], other)
    held = jnp.concatenate([whole.reshape(parts, part, width), extra[None]], axis=0)
    gathered = lax.all_gather(after(held, pieces[1, 0], pieces[-1, 0]), ("leaf", "col"), axis=0, tiled=False)
    own = jnp.stack([lower, swapped])
    hop(1, 0, gathered)
    hop(0, 1, gathered)

    chunks, each = 2, cols // rows
    order = ((me_row + 1 + jnp.arange(rows)) % rows).astype(jnp.int32)
    leaf_here = me_leaf.astype(jnp.int32)[None]
    top_args = (leaf_here, gathered, own, chunks)
    early = top_product(lay, table, order[: rows - 1], *top_args, 0)
    early_in = send_over_rows(early)
    sent, turned = panel_product(lay, pattern[0], table, order, gathered, normed, early)
    if cols > 2:
        sent = [after(value, pieces[2, 0], pieces[-2, 0]) for value in sent]
    sent_in = send_over_rows(sent)
    middle = cols // 2
    for step in range(1, middle):
        hop(1, step, *sent)
        if step + 1 < cols - 1:
            hop(0, step + 1, *sent)
    kept = own_panel_product(lay, pattern[0], table, order, gathered, turned, early_in)
    late = top_product(lay, table, order[: rows - 1], *top_args, 1, [kept])
    sigma_panel = -sum(sent_in, kept).reshape(-1, normed.shape[1])
    late = [after(value, sigma_panel) for value in late]
    late_in = send_over_rows(late)
    for step in range(middle, cols - 1):
        hop(1, step, sigma_panel)
        if step + 1 < cols - 1:
            hop(0, step + 1, sigma_panel)

    near = [[sorted(range(d * each, d * each + each), key=lambda block: abs(block - c)) for c in range(cols)] for d in range(rows)]
    near = np.asarray(near, np.int32)
    reach = np.abs(near - np.arange(cols)[None, :, None]).max(axis=(0, 1))
    near_here = jnp.asarray(near)[:, me_col]
    terms_in, tokens = [], late
    for i in range(each):
        there = {key: piece for key, piece in pieces.items() if abs(key[0]) <= reach[i]}
        term = [
            diagonal_product(near_here[order[a]][i : i + 1], me_col, there, sigma_panel, tokens)
            for a in range(rows - 1)
        ]
        terms_in.append(send_over_rows(term))
        if i == 0:
            tops = list(top_product(lay, table, order[rows - 1 :], *top_args, 1, term))
        tokens = tops + late_in
    tops = list(top_product(lay, table, order[rows - 1 :], *top_args, 0, term)) + tops
    mine = me_row * each + jnp.arange(each)
    update = list(diagonal_product(mine, me_col, pieces, sigma_panel, term))
    for block in range(each):
        for i in range(each):
            for value in terms_in[i]:
                update[block] += jnp.where(near_here[me_row, i] == mine[block], value[0], 0.0)
    sigma_diag = diag_inverse[0] - jnp.concatenate(update, axis=0)

    sigma_top = jnp.concatenate([sum(early_in, tops[0]), sum(late_in, tops[1])], axis=0).reshape(-1, width)
    return (sigma_top, sigma_panel[None], sigma_diag[None])


def solution(mesh):
    placed = (
        P("row", ("leaf", "col")),
        P("leaf", None),
        P("leaf", None, "col"),
        P("leaf", "row", "col"),
    )

    def whole(top_inverse, pattern, panel, diag_inverse):
        rows, leaves, cols = (mesh.shape[axis] for axis in ("row", "leaf", "col"))
        size = top_inverse.shape[0]
        lay = Layout(rows, leaves, cols, size // rows // 2, size // leaves // cols)
        return jax.shard_map(
            functools.partial(per_device, lay),
            mesh=mesh,
            in_specs=placed,
            out_specs=(P("row", ("leaf", "col")), P("leaf", "row", "col"), P("leaf", "row", "col")),
            check_vma=False,
        )(top_inverse, pattern, panel, diag_inverse)

    return whole
```

```python
import functools

import jax
import jax.numpy as jnp
import numpy as np
from jax import lax
from jax.experimental import pallas as pl
from jax.experimental.pallas import tpu as pltpu
from jax.sharding import PartitionSpec as P

BLK = 128
VMEM_BYTES = 58 * 1024 * 1024


def halves(value):
    high = value.astype(jnp.bfloat16)
    low = (value - high.astype(jnp.float32)).astype(jnp.bfloat16)
    return high, low


def dot(left, right):
    return jnp.dot(left, right, preferred_element_type=jnp.float32)


class Layout:
    def __init__(self, rows, leaves, cols, half, width):
        self.rows, self.leaves, self.cols, self.half, self.width = rows, leaves, cols, half, width
        self.part = half // leaves
        self.span = width * cols
        self.counts, self.holder, self.source = [], [], []
        for r in range(rows):
            count = [min(leaves, (q * half + half - 1) // self.span + 1) for q in (2 * r + 1, 2 * (rows - 1 - r))]
            assert count[0] + count[1] <= leaves + 1
            free = list(range(count[1], leaves))
            moved = [leaf for leaf in range(1, count[0]) if leaf not in free]
            slot = {leaf: leaf for leaf in range(1, count[0]) if leaf in free}
            left = [s for s in free if s not in slot]
            slot.update(zip(moved, left))
            self.counts.append(count)
            self.holder.append(slot)
        table = np.full((rows, 2, leaves, leaves), -1, np.int32)
        for r in range(rows):
            for j in range(leaves):
                table[r, 0, 0, j] = j * (leaves + 1) + leaves
                for leaf, slot in self.holder[r].items():
                    table[r, 0, leaf, j] = slot * (leaves + 1) + j
                for leaf in range(self.counts[r][1]):
                    table[r, 1, leaf, j] = leaf * (leaves + 1) + j
        self.table = table


def place_of(lay, pat, k):
    first = pat[k] * BLK
    leaf = first // lay.span
    rest = first - leaf * lay.span
    col = rest // lay.width
    return leaf, col, (rest - col * lay.width) // BLK


def fetch_entry(lay, pat, tab, gathered, t, sems, k):
    leaf, col, sub = place_of(lay, pat, k)
    lanes = pl.ds(pl.multiple_of(sub * BLK, BLK), BLK)
    for s in range(2):
        here = tab[s, leaf, 0] >= 0

        @pl.when(here)
        def _():
            for j in range(lay.leaves):
                entry = tab[s, leaf, j]
                slot = entry // (lay.leaves + 1)
                position = entry - slot * (lay.leaves + 1)
                pltpu.make_async_copy(
                    gathered.at[slot * lay.cols + col, position, :, lanes],
                    t.at[k, s, pl.ds(j * lay.part, lay.part)],
                    sems.at[k, s],
                ).start()

        @pl.when(jnp.logical_not(here))
        def _():
            t[k, s] = jnp.zeros(t.shape[2:], t.dtype)


def any_valid(lay, pat, tab, kp, s):
    first = tab[s, place_of(lay, pat, 2 * kp)[0], 0] >= 0
    second = tab[s, place_of(lay, pat, 2 * kp + 1)[0], 0] >= 0
    return jnp.logical_or(first, second)


def wait_pair(lay, pat, tab, t, sems, kp, s):
    for m in range(2):
        k = 2 * kp + m

        @pl.when(tab[s, place_of(lay, pat, k)[0], 0] >= 0)
        def _():
            pltpu.make_async_copy(t.at[k, s], t.at[k, s], sems.at[k, s]).wait()


def back_product(turned_high, turned_low, high, low, s):
    return dot(turned_high[s], high) + dot(turned_low[s], high) + dot(turned_high[s], low)


def panel_kernel(lay, rows, tokens, pat, tab, order, gathered, p_ref, *refs):
    outs = refs[tokens : tokens + rows - 1]
    turned_high, turned_low, t, th, tl, image, sems = refs[tokens + rows - 1 :]
    number = t.shape[0]
    each = number // 2 // rows

    @pl.loop(0, number)
    def _(k):
        fetch_entry(lay, pat, tab, gathered, t, sems, k)

    image[...] = jnp.zeros_like(image)

    group = 2 if number % 4 == 0 else 1

    @pl.loop(0, number // 2 // group)
    def _(step):
        deep = 2 * group * BLK
        span = pl.ds(pl.multiple_of(step * deep, deep), deep)
        p_high, p_low = halves(p_ref[span, :])
        stacked = jnp.concatenate([p_high, p_low, p_high], axis=0)
        pairs = [step * group + m for m in range(group)]
        for s in range(2):
            found = False
            for kp in pairs:
                wait_pair(lay, pat, tab, t, sems, kp, s)
                found = jnp.logical_or(found, any_valid(lay, pat, tab, kp, s))

            @pl.when(found)
            def _():
                highs, lows = [], []
                for kp in pairs:
                    high, low = halves(jnp.concatenate([t[2 * kp, s], t[2 * kp + 1, s]], axis=1))
                    th[kp, s] = high
                    tl[kp, s] = low
                    highs.append(high)
                    lows.append(low)
                image[s] += dot(jnp.concatenate(highs + highs + lows, axis=1), stacked)

    for s in range(2):
        high, low = halves(image[s].T)
        turned_high[s] = high
        turned_low[s] = low

    for a in range(rows - 1):

        @pl.loop(0, each)
        def _(i):
            kp = order[a] * each + i
            out = outs[a].at[i]
            out[...] = jnp.zeros(out.shape, out.dtype)
            for s in range(2):

                @pl.when(any_valid(lay, pat, tab, kp, s))
                def _():
                    out[...] += back_product(turned_high, turned_low, th[kp, s], tl[kp, s], s).T


def own_panel_kernel(lay, rows, tokens, pat, tab, order, gathered, turned_high, turned_low, *refs):
    out_ref, t, sems = refs[tokens:]
    each = t.shape[0] // 2 // rows
    first = order[rows - 1] * each

    @pl.loop(0, 2 * each)
    def _(i):
        fetch_entry(lay, pat, tab, gathered, t, sems, 2 * first + i)

    @pl.loop(0, each)
    def _(i):
        kp = first + i
        out = out_ref.at[i]
        out[...] = jnp.zeros(out.shape, out.dtype)
        for s in range(2):
            wait_pair(lay, pat, tab, t, sems, kp, s)

            @pl.when(any_valid(lay, pat, tab, kp, s))
            def _():
                high, low = halves(jnp.concatenate([t[2 * kp, s], t[2 * kp + 1, s]], axis=1))
                out[...] += back_product(turned_high, turned_low, high, low, s).T


ANY = pl.BlockSpec(memory_space=pl.ANY)
VMEM = pl.BlockSpec(memory_space=pltpu.VMEM)
SMEM = pl.BlockSpec(memory_space=pltpu.SMEM)


def estimate(flops, values):
    return pl.CostEstimate(flops=flops, bytes_accessed=4 * values, transcendentals=0)


def panel_product(lay, pattern, table, order, gathered, normed, tokens):
    number, wide, rows = pattern.shape[0], normed.shape[1], order.shape[0]
    half = lay.half
    pairs = number // 2
    block = jax.ShapeDtypeStruct((pairs // rows, 2 * BLK, wide), jnp.float32)
    turned = jax.ShapeDtypeStruct((2, wide, half), jnp.bfloat16)
    result = pl.pallas_call(
        functools.partial(panel_kernel, lay, rows, len(tokens)),
        out_shape=[block] * (rows - 1) + [turned] * 2,
        in_specs=[SMEM] * 3 + [ANY, VMEM] + [ANY] * len(tokens),
        out_specs=[VMEM] * (rows + 1),
        scratch_shapes=[
            pltpu.VMEM((number, 2, half, BLK), jnp.float32),
            pltpu.VMEM((pairs, 2, half, 2 * BLK), jnp.bfloat16),
            pltpu.VMEM((pairs, 2, half, 2 * BLK), jnp.bfloat16),
            pltpu.VMEM((2, half, wide), jnp.float32),
            pltpu.SemaphoreType.DMA((number, 2)),
        ],
        compiler_params=pltpu.CompilerParams(vmem_limit_bytes=VMEM_BYTES),
        cost_estimate=estimate(18 * half * number * BLK * wide, 2 * half * number * BLK),
    )(pattern, table, order, gathered, normed, *tokens)
    return result[: rows - 1], result[rows - 1 :]


def own_panel_product(lay, pattern, table, order, gathered, turned, tokens):
    number, wide, rows = pattern.shape[0], turned[0].shape[1], order.shape[0]
    half = lay.half
    return pl.pallas_call(
        functools.partial(own_panel_kernel, lay, rows, len(tokens)),
        out_shape=jax.ShapeDtypeStruct((number // 2 // rows, 2 * BLK, wide), jnp.float32),
        in_specs=[SMEM] * 3 + [ANY, VMEM, VMEM] + [ANY] * len(tokens),
        out_specs=VMEM,
        scratch_shapes=[
            pltpu.VMEM((number, 2, half, BLK), jnp.float32),
            pltpu.SemaphoreType.DMA((number, 2)),
        ],
        compiler_params=pltpu.CompilerParams(vmem_limit_bytes=VMEM_BYTES),
        cost_estimate=estimate(24 * half * number * BLK * wide, half * number * BLK),
    )(pattern, table, order, gathered, *turned, *tokens)


def top_kernel(lay, chunks, chunk, tokens, tab, dests, leaf_ref, g_ref, own_ref, *refs):
    count = dests.shape[0]
    outs, (own_turned, held, sems) = refs[tokens : tokens + count], refs[tokens + count :]
    parts, part = lay.leaves, lay.part
    each = outs[0].shape[0]

    def place(a, i):
        block = (dests[a] * chunks + chunk) * each + i
        leaf = block // lay.cols
        return leaf, block - leaf * lay.cols

    def wanted(leaf, s):
        return jnp.logical_and(tab[s, leaf, 0] >= 0, tab[s, leaf_ref[0], 0] >= 0)

    for a in range(count):

        @pl.loop(0, each)
        def _(i):
            leaf, col = place(a, i)
            for s in range(2):

                @pl.when(wanted(leaf, s))
                def _():
                    for j in range(parts):
                        entry = tab[s, leaf, j]
                        slot = entry // (parts + 1)
                        position = entry - slot * (parts + 1)
                        pltpu.make_async_copy(
                            g_ref.at[slot * lay.cols + col, position],
                            held.at[a, i, s, pl.ds(j * part, part)],
                            sems.at[a, i, s],
                        ).start()

    for s in range(2):
        high, low = halves(own_ref[s].T)
        own_turned[s, 0] = high
        own_turned[s, 1] = low

    for a in range(count):

        @pl.loop(0, each)
        def _(i):
            leaf, col = place(a, i)
            out = outs[a].at[i]
            out[...] = jnp.zeros(out.shape, out.dtype)
            for s in range(2):

                @pl.when(wanted(leaf, s))
                def _():
                    pltpu.make_async_copy(held.at[a, i, s], held.at[a, i, s], sems.at[a, i, s]).wait()
                    high, low = halves(held[a, i, s])
                    total = dot(own_turned[s, 0], high) + dot(own_turned[s, 1], high) + dot(own_turned[s, 0], low)
                    out[...] += total.T


def top_product(lay, table, dests, me_leaf, gathered, own, chunks, chunk, tokens=()):
    count, width, half = dests.shape[0], lay.width, lay.half
    each = gathered.shape[0] // lay.rows // chunks
    block = jax.ShapeDtypeStruct((each, width, width), jnp.float32)
    return pl.pallas_call(
        functools.partial(top_kernel, lay, chunks, chunk, len(tokens)),
        out_shape=[block] * count,
        in_specs=[SMEM] * 3 + [ANY, VMEM] + [ANY] * len(tokens),
        out_specs=[VMEM] * count,
        scratch_shapes=[
            pltpu.VMEM((2, 2, width, half), jnp.bfloat16),
            pltpu.VMEM((count, each, 2, half, width), jnp.float32),
            pltpu.SemaphoreType.DMA((count, each, 2)),
        ],
        compiler_params=pltpu.CompilerParams(vmem_limit_bytes=VMEM_BYTES),
        cost_estimate=estimate(12 * half * count * each * width * width, 2 * half * count * each * width),
    )(table, dests, me_leaf, gathered, own, *tokens)


def diagonal_kernel(steps, first, tokens, info, *refs):
    sources, refs = list(zip(steps, refs)), refs[len(steps) :]
    sigma, (out_ref, held, sems) = refs[0], refs[1 + tokens :]
    each = out_ref.shape[0]
    for i in range(each):
        away = info[1 + first + i] - info[0]
        for (step, run), source in sources:

            @pl.when(away == step)
            def _():
                rows = pl.ds(run * source.shape[0], source.shape[0])
                pltpu.make_async_copy(source, held.at[i, rows], sems.at[i]).start()

    turned_high, turned_low = halves(sigma[...].T)
    for i in range(each):
        pltpu.make_async_copy(held.at[i], held.at[i], sems.at[i]).wait()
        high, low = halves(held[i])
        total = dot(turned_high, high) + dot(turned_low, high) + dot(turned_high, low)
        out_ref[i] = total.T


def diagonal_product(info, first, each, pieces, sigma, tokens):
    depth, wide = sigma.shape
    return pl.pallas_call(
        functools.partial(diagonal_kernel, tuple(pieces), first, len(tokens)),
        out_shape=jax.ShapeDtypeStruct((each, wide, wide), jnp.float32),
        in_specs=[SMEM] + [ANY] * len(pieces) + [VMEM] + [ANY] * len(tokens),
        out_specs=VMEM,
        scratch_shapes=[pltpu.VMEM((each, depth, wide), jnp.float32), pltpu.SemaphoreType.DMA((each,))],
        compiler_params=pltpu.CompilerParams(vmem_limit_bytes=VMEM_BYTES),
        cost_estimate=estimate(6 * each * depth * wide * wide, (each + 1) * depth * wide),
    )(info, *pieces.values(), sigma, *tokens)


def after(value, *earlier):
    return pl.pallas_call(
        lambda *refs: None,
        out_shape=jax.ShapeDtypeStruct(value.shape, value.dtype),
        in_specs=[ANY] * (1 + len(earlier)),
        out_specs=ANY,
        input_output_aliases={0: 0},
        cost_estimate=estimate(0, 0),
    )(value, *earlier)


def send_over_rows(sent):
    rows = lax.axis_size("row")
    return [lax.ppermute(value, "row", [(i, (i + a + 1) % rows) for i in range(rows)]) for a, value in enumerate(sent)]


def per_device(lay, top_inverse, pattern, panel, diag_inverse):
    rows, cols, leaves = (lax.axis_size(axis) for axis in ("row", "col", "leaf"))
    me_row, me_col, me_leaf = (lax.axis_index(axis) for axis in ("row", "col", "leaf"))
    half, width, parts, part = lay.half, lay.width, lay.leaves, lay.part
    normed = panel[0]

    count = normed.shape[0] // rows
    own_rows = lax.dynamic_slice_in_dim(normed, me_row * count, count, 0)
    runs = 2
    pieces = {(0, run): own_rows[run * count // runs : (run + 1) * count // runs] for run in range(runs)}

    def hop(run, step, *earlier):
        if earlier:
            for key in sorted({(step, run), (-step, run)}):
                pieces[key] = after(pieces[key], *earlier)
        for way in (1, -1):
            at = [i for i in range(cols) if 0 <= i - way * step < cols and 0 <= i + way < cols]
            moved_on = lax.ppermute(pieces[-way * step, run], "col", [(i, i + way) for i in at])
            pieces[-way * (step + 1), run] = moved_on

    hop(0, 0)

    table = jnp.asarray(lay.table)[me_row]
    second = jnp.asarray([count[1] for count in lay.counts], jnp.int32)[me_row]
    is_moved = np.zeros((rows, leaves), bool)
    pairs = []
    for r in range(rows):
        for leaf, slot in lay.holder[r].items():
            if leaf != slot:
                is_moved[r, slot] = True
                pairs.append((leaf * rows + r, slot * rows + r))
    moved_here = jnp.asarray(is_moved)[me_row, me_leaf]
    lower, upper = top_inverse[half:], top_inverse[:half]
    swapped = lax.ppermute(upper, "row", [(r, rows - 1 - r) for r in range(rows)])
    moved = lax.ppermute(lower, ("leaf", "row"), pairs) if pairs else lower
    whole = jnp.where(me_leaf < second, swapped, jnp.where(moved_here, moved, lower))
    both = lower[: 2 * part]
    for chip in range(2, leaves, 2):
        both = jnp.where(me_leaf == chip, lax.ppermute(lower[chip * part : (chip + 2) * part], "leaf", [(0, chip)]), both)
    other = lax.ppermute(both[part:], "leaf", [(chip, chip + 1) for chip in range(0, leaves, 2)])
    extra = jnp.where(me_leaf % 2 == 0, both[:part], other)
    held = jnp.concatenate([whole.reshape(parts, part, width), extra[None]], axis=0)
    gathered = lax.all_gather(after(held, pieces[1, 0], pieces[-1, 0]), ("leaf", "col"), axis=0, tiled=False)
    own = jnp.stack([lower, swapped])
    hop(1, 0, gathered)

    chunks, each = 2, cols // rows
    order = ((me_row + 1 + jnp.arange(rows)) % rows).astype(jnp.int32)
    near = [[sorted(range(d * each, d * each + each), key=lambda block: abs(block - c)) for c in range(cols)] for d in range(rows)]
    near = np.asarray(near, np.int32)
    reach = np.abs(near - np.arange(cols)[None, :, None]).max(axis=(0, 1))
    near_here = jnp.asarray(near)[:, me_col]
    wanted = near_here[order[: rows - 1]].reshape(-1)
    info = jnp.concatenate([me_col[None], wanted, me_row * each + jnp.arange(each)]).astype(jnp.int32)
    leaf_here = me_leaf.astype(jnp.int32)[None]
    top_args = (leaf_here, gathered, own, chunks)
    early = top_product(lay, table, order[: rows - 1], *top_args, 0, [info])
    early_in = send_over_rows(early)
    if cols > 2:
        hop(0, 1, *early)
    sent, turned = panel_product(lay, pattern[0], table, order, gathered, normed, early)
    sent_in = send_over_rows(sent)
    middle = cols // 2
    for step in range(1, middle):
        hop(1, step, *sent)
        if step + 1 < cols - 1:
            hop(0, step + 1, *sent)
    kept = own_panel_product(lay, pattern[0], table, order, gathered, turned, early_in)
    late = top_product(lay, table, order[: rows - 1], *top_args, 1, [kept])
    sigma_panel = -sum(sent_in, kept).reshape(-1, normed.shape[1])
    late = [after(value, sigma_panel) for value in late]
    late_in = send_over_rows(late)
    for step in range(middle, cols - 1):
        hop(1, step, sigma_panel)
        if step + 1 < cols - 1:
            hop(0, step + 1, sigma_panel)

    terms_in, tokens = [], late
    for i in range(each):
        there = {key: piece for key, piece in pieces.items() if abs(key[0]) <= reach[i]}
        term = [diagonal_product(info, a * each + i, 1, there, sigma_panel, tokens) for a in range(rows - 1)]
        terms_in.append(send_over_rows(term))
        tokens = term + late_in
    mine = diagonal_product(info, (rows - 1) * each, each, pieces, sigma_panel, term)
    rest = diag_inverse[0] - mine.reshape(diag_inverse.shape[1:])
    tops = [top_product(lay, table, order[rows - 1 :], *top_args, chunk, [mine])[0] for chunk in range(chunks)]
    update = []
    for block in range(each):
        total = 0.0
        for i in range(each):
            for value in terms_in[i]:
                total += jnp.where(near_here[me_row, i] == me_row * each + block, value[0], 0.0)
        update.append(total)
    sigma_diag = rest - jnp.concatenate(update, axis=0)

    sigma_top = jnp.concatenate([sum(early_in, tops[0]), sum(late_in, tops[1])], axis=0).reshape(-1, width)
    return (sigma_top, sigma_panel[None], sigma_diag[None])


def solution(mesh):
    placed = (
        P("row", ("leaf", "col")),
        P("leaf", None),
        P("leaf", None, "col"),
        P("leaf", "row", "col"),
    )

    def whole(top_inverse, pattern, panel, diag_inverse):
        rows, leaves, cols = (mesh.shape[axis] for axis in ("row", "leaf", "col"))
        size = top_inverse.shape[0]
        lay = Layout(rows, leaves, cols, size // rows // 2, size // leaves // cols)
        return jax.shard_map(
            functools.partial(per_device, lay),
            mesh=mesh,
            in_specs=placed,
            out_specs=(P("row", ("leaf", "col")), P("leaf", "row", "col"), P("leaf", "row", "col")),
            check_vma=False,
        )(top_inverse, pattern, panel, diag_inverse)

    return whole
```

```python
import functools

import jax
import jax.numpy as jnp
import numpy as np
from jax import lax
from jax.experimental import pallas as pl
from jax.experimental.pallas import tpu as pltpu
from jax.sharding import PartitionSpec as P

BLK = 128
VMEM_BYTES = 58 * 1024 * 1024


def halves(value):
    high = value.astype(jnp.bfloat16)
    low = (value - high.astype(jnp.float32)).astype(jnp.bfloat16)
    return high, low


def dot(left, right):
    return jnp.dot(left, right, preferred_element_type=jnp.float32)


class Layout:
    def __init__(self, rows, leaves, cols, half, width):
        self.rows, self.leaves, self.cols, self.half, self.width = rows, leaves, cols, half, width
        self.part = half // leaves
        self.span = width * cols
        self.counts, self.holder, self.source = [], [], []
        for r in range(rows):
            count = [min(leaves, (q * half + half - 1) // self.span + 1) for q in (2 * r + 1, 2 * (rows - 1 - r))]
            assert count[0] + count[1] <= leaves + 1
            free = list(range(count[1], leaves))
            moved = [leaf for leaf in range(1, count[0]) if leaf not in free]
            slot = {leaf: leaf for leaf in range(1, count[0]) if leaf in free}
            left = [s for s in free if s not in slot]
            slot.update(zip(moved, left))
            self.counts.append(count)
            self.holder.append(slot)
        table = np.full((rows, 2, leaves, leaves), -1, np.int32)
        for r in range(rows):
            for j in range(leaves):
                table[r, 0, 0, j] = j * (leaves + 1) + leaves
                for leaf, slot in self.holder[r].items():
                    table[r, 0, leaf, j] = slot * (leaves + 1) + j
                for leaf in range(self.counts[r][1]):
                    table[r, 1, leaf, j] = leaf * (leaves + 1) + j
        self.table = table


def place_of(lay, pat, k):
    first = pat[k] * BLK
    leaf = first // lay.span
    rest = first - leaf * lay.span
    col = rest // lay.width
    return leaf, col, (rest - col * lay.width) // BLK


def fetch_entry(lay, pat, tab, gathered, t, sems, k):
    leaf, col, sub = place_of(lay, pat, k)
    lanes = pl.ds(pl.multiple_of(sub * BLK, BLK), BLK)
    for s in range(2):
        here = tab[s, leaf, 0] >= 0

        @pl.when(here)
        def _():
            for j in range(lay.leaves):
                entry = tab[s, leaf, j]
                slot = entry // (lay.leaves + 1)
                position = entry - slot * (lay.leaves + 1)
                pltpu.make_async_copy(
                    gathered.at[col * lay.leaves + slot, position, :, lanes],
                    t.at[k, s, pl.ds(j * lay.part, lay.part)],
                    sems.at[k, s],
                ).start()

        @pl.when(jnp.logical_not(here))
        def _():
            t[k, s] = jnp.zeros(t.shape[2:], t.dtype)


def any_valid(lay, pat, tab, kp, s):
    first = tab[s, place_of(lay, pat, 2 * kp)[0], 0] >= 0
    second = tab[s, place_of(lay, pat, 2 * kp + 1)[0], 0] >= 0
    return jnp.logical_or(first, second)


def wait_pair(lay, pat, tab, t, sems, kp, s):
    for m in range(2):
        k = 2 * kp + m

        @pl.when(tab[s, place_of(lay, pat, k)[0], 0] >= 0)
        def _():
            pltpu.make_async_copy(t.at[k, s], t.at[k, s], sems.at[k, s]).wait()


def back_product(turned_high, turned_low, high, low, s):
    return dot(turned_high[s], high) + dot(turned_low[s], high) + dot(turned_high[s], low)


def panel_kernel(lay, rows, tokens, pat, tab, order, gathered, p_ref, *refs):
    outs = refs[tokens : tokens + rows - 1]
    turned_high, turned_low, t, th, tl, image, sems = refs[tokens + rows - 1 :]
    number = t.shape[0]
    each = number // 2 // rows

    @pl.loop(0, number)
    def _(k):
        fetch_entry(lay, pat, tab, gathered, t, sems, k)

    image[...] = jnp.zeros_like(image)

    group = 2 if number % 4 == 0 else 1

    @pl.loop(0, number // 2 // group)
    def _(step):
        deep = 2 * group * BLK
        span = pl.ds(pl.multiple_of(step * deep, deep), deep)
        p_high, p_low = halves(p_ref[span, :])
        stacked = jnp.concatenate([p_high, p_low, p_high], axis=0)
        pairs = [step * group + m for m in range(group)]
        for s in range(2):
            found = False
            for kp in pairs:
                wait_pair(lay, pat, tab, t, sems, kp, s)
                found = jnp.logical_or(found, any_valid(lay, pat, tab, kp, s))

            @pl.when(found)
            def _():
                highs, lows = [], []
                for kp in pairs:
                    high, low = halves(jnp.concatenate([t[2 * kp, s], t[2 * kp + 1, s]], axis=1))
                    th[kp, s] = high
                    tl[kp, s] = low
                    highs.append(high)
                    lows.append(low)
                image[s] += dot(jnp.concatenate(highs + highs + lows, axis=1), stacked)

    for s in range(2):
        high, low = halves(image[s].T)
        turned_high[s] = high
        turned_low[s] = low

    for a in range(rows - 1):

        @pl.loop(0, each)
        def _(i):
            kp = order[a] * each + i
            out = outs[a].at[i]
            out[...] = jnp.zeros(out.shape, out.dtype)
            for s in range(2):

                @pl.when(any_valid(lay, pat, tab, kp, s))
                def _():
                    out[...] += back_product(turned_high, turned_low, th[kp, s], tl[kp, s], s).T


def own_panel_kernel(lay, rows, tokens, pat, tab, order, gathered, turned_high, turned_low, *refs):
    out_ref, t, sems = refs[tokens:]
    each = t.shape[0] // 2 // rows
    first = order[rows - 1] * each

    @pl.loop(0, 2 * each)
    def _(i):
        fetch_entry(lay, pat, tab, gathered, t, sems, 2 * first + i)

    @pl.loop(0, each)
    def _(i):
        kp = first + i
        out = out_ref.at[i]
        out[...] = jnp.zeros(out.shape, out.dtype)
        for s in range(2):
            wait_pair(lay, pat, tab, t, sems, kp, s)

            @pl.when(any_valid(lay, pat, tab, kp, s))
            def _():
                high, low = halves(jnp.concatenate([t[2 * kp, s], t[2 * kp + 1, s]], axis=1))
                out[...] += back_product(turned_high, turned_low, high, low, s).T


ANY = pl.BlockSpec(memory_space=pl.ANY)
VMEM = pl.BlockSpec(memory_space=pltpu.VMEM)
SMEM = pl.BlockSpec(memory_space=pltpu.SMEM)


def estimate(flops, values):
    return pl.CostEstimate(flops=flops, bytes_accessed=4 * values, transcendentals=0)


def panel_product(lay, pattern, table, order, gathered, normed, tokens):
    number, wide, rows = pattern.shape[0], normed.shape[1], order.shape[0]
    half = lay.half
    pairs = number // 2
    block = jax.ShapeDtypeStruct((pairs // rows, 2 * BLK, wide), jnp.float32)
    turned = jax.ShapeDtypeStruct((2, wide, half), jnp.bfloat16)
    result = pl.pallas_call(
        functools.partial(panel_kernel, lay, rows, len(tokens)),
        out_shape=[block] * (rows - 1) + [turned] * 2,
        in_specs=[SMEM] * 3 + [ANY, VMEM] + [ANY] * len(tokens),
        out_specs=[VMEM] * (rows + 1),
        scratch_shapes=[
            pltpu.VMEM((number, 2, half, BLK), jnp.float32),
            pltpu.VMEM((pairs, 2, half, 2 * BLK), jnp.bfloat16),
            pltpu.VMEM((pairs, 2, half, 2 * BLK), jnp.bfloat16),
            pltpu.VMEM((2, half, wide), jnp.float32),
            pltpu.SemaphoreType.DMA((number, 2)),
        ],
        compiler_params=pltpu.CompilerParams(vmem_limit_bytes=VMEM_BYTES),
        cost_estimate=estimate(18 * half * number * BLK * wide, 2 * half * number * BLK),
    )(pattern, table, order, gathered, normed, *tokens)
    return result[: rows - 1], result[rows - 1 :]


def own_panel_product(lay, pattern, table, order, gathered, turned, tokens):
    number, wide, rows = pattern.shape[0], turned[0].shape[1], order.shape[0]
    half = lay.half
    return pl.pallas_call(
        functools.partial(own_panel_kernel, lay, rows, len(tokens)),
        out_shape=jax.ShapeDtypeStruct((number // 2 // rows, 2 * BLK, wide), jnp.float32),
        in_specs=[SMEM] * 3 + [ANY, VMEM, VMEM] + [ANY] * len(tokens),
        out_specs=VMEM,
        scratch_shapes=[
            pltpu.VMEM((number, 2, half, BLK), jnp.float32),
            pltpu.SemaphoreType.DMA((number, 2)),
        ],
        compiler_params=pltpu.CompilerParams(vmem_limit_bytes=VMEM_BYTES),
        cost_estimate=estimate(24 * half * number * BLK * wide, half * number * BLK),
    )(pattern, table, order, gathered, *turned, *tokens)


def top_kernel(lay, chunks, chunk, tokens, tab, dests, leaf_ref, g_ref, own_ref, *refs):
    count = dests.shape[0]
    outs, (own_turned, held, sems) = refs[tokens : tokens + count], refs[tokens + count :]
    parts, part = lay.leaves, lay.part
    each = outs[0].shape[0]

    def place(a, i):
        block = (dests[a] * chunks + chunk) * each + i
        leaf = block // lay.cols
        return leaf, block - leaf * lay.cols

    def wanted(leaf, s):
        return jnp.logical_and(tab[s, leaf, 0] >= 0, tab[s, leaf_ref[0], 0] >= 0)

    for a in range(count):

        @pl.loop(0, each)
        def _(i):
            leaf, col = place(a, i)
            for s in range(2):

                @pl.when(wanted(leaf, s))
                def _():
                    for j in range(parts):
                        entry = tab[s, leaf, j]
                        slot = entry // (parts + 1)
                        position = entry - slot * (parts + 1)
                        pltpu.make_async_copy(
                            g_ref.at[col * lay.leaves + slot, position],
                            held.at[a, i, s, pl.ds(j * part, part)],
                            sems.at[a, i, s],
                        ).start()

    for s in range(2):
        high, low = halves(own_ref[s].T)
        own_turned[s, 0] = high
        own_turned[s, 1] = low

    for a in range(count):

        @pl.loop(0, each)
        def _(i):
            leaf, col = place(a, i)
            out = outs[a].at[i]
            out[...] = jnp.zeros(out.shape, out.dtype)
            for s in range(2):

                @pl.when(wanted(leaf, s))
                def _():
                    pltpu.make_async_copy(held.at[a, i, s], held.at[a, i, s], sems.at[a, i, s]).wait()
                    high, low = halves(held[a, i, s])
                    total = dot(own_turned[s, 0], high) + dot(own_turned[s, 1], high) + dot(own_turned[s, 0], low)
                    out[...] += total.T


def top_product(lay, table, dests, me_leaf, gathered, own, chunks, chunk, tokens=()):
    count, width, half = dests.shape[0], lay.width, lay.half
    each = gathered.shape[0] // lay.rows // chunks
    block = jax.ShapeDtypeStruct((each, width, width), jnp.float32)
    return pl.pallas_call(
        functools.partial(top_kernel, lay, chunks, chunk, len(tokens)),
        out_shape=[block] * count,
        in_specs=[SMEM] * 3 + [ANY, VMEM] + [ANY] * len(tokens),
        out_specs=[VMEM] * count,
        scratch_shapes=[
            pltpu.VMEM((2, 2, width, half), jnp.bfloat16),
            pltpu.VMEM((count, each, 2, half, width), jnp.float32),
            pltpu.SemaphoreType.DMA((count, each, 2)),
        ],
        compiler_params=pltpu.CompilerParams(vmem_limit_bytes=VMEM_BYTES),
        cost_estimate=estimate(12 * half * count * each * width * width, 2 * half * count * each * width),
    )(table, dests, me_leaf, gathered, own, *tokens)


def diagonal_kernel(steps, first, tokens, info, *refs):
    sources, refs = list(zip(steps, refs)), refs[len(steps) :]
    sigma, (out_ref, held, sems) = refs[0], refs[1 + tokens :]
    each = out_ref.shape[0]
    for i in range(each):
        away = info[1 + first + i] - info[0]
        for (step, run), source in sources:

            @pl.when(away == step)
            def _():
                rows = pl.ds(run * source.shape[0], source.shape[0])
                pltpu.make_async_copy(source, held.at[i, rows], sems.at[i]).start()

    turned_high, turned_low = halves(sigma[...].T)
    for i in range(each):
        pltpu.make_async_copy(held.at[i], held.at[i], sems.at[i]).wait()
        high, low = halves(held[i])
        total = dot(turned_high, high) + dot(turned_low, high) + dot(turned_high, low)
        out_ref[i] = total.T


def diagonal_product(info, first, each, pieces, sigma, tokens):
    depth, wide = sigma.shape
    return pl.pallas_call(
        functools.partial(diagonal_kernel, tuple(pieces), first, len(tokens)),
        out_shape=jax.ShapeDtypeStruct((each, wide, wide), jnp.float32),
        in_specs=[SMEM] + [ANY] * len(pieces) + [VMEM] + [ANY] * len(tokens),
        out_specs=VMEM,
        scratch_shapes=[pltpu.VMEM((each, depth, wide), jnp.float32), pltpu.SemaphoreType.DMA((each,))],
        compiler_params=pltpu.CompilerParams(vmem_limit_bytes=VMEM_BYTES),
        cost_estimate=estimate(6 * each * depth * wide * wide, (each + 1) * depth * wide),
    )(info, *pieces.values(), sigma, *tokens)


def after(value, *earlier):
    return pl.pallas_call(
        lambda *refs: None,
        out_shape=jax.ShapeDtypeStruct(value.shape, value.dtype),
        in_specs=[ANY] * (1 + len(earlier)),
        out_specs=ANY,
        input_output_aliases={0: 0},
        cost_estimate=estimate(0, 0),
    )(value, *earlier)


def send_over_rows(sent):
    rows = lax.axis_size("row")
    return [lax.ppermute(value, "row", [(i, (i + a + 1) % rows) for i in range(rows)]) for a, value in enumerate(sent)]


def per_device(lay, top_inverse, pattern, panel, diag_inverse):
    rows, cols, leaves = (lax.axis_size(axis) for axis in ("row", "col", "leaf"))
    me_row, me_col, me_leaf = (lax.axis_index(axis) for axis in ("row", "col", "leaf"))
    half, width, parts, part = lay.half, lay.width, lay.leaves, lay.part
    normed = panel[0]

    count = normed.shape[0] // rows
    own_rows = lax.dynamic_slice_in_dim(normed, me_row * count, count, 0)
    runs = 2
    pieces = {(0, run): own_rows[run * count // runs : (run + 1) * count // runs] for run in range(runs)}

    def hop(run, step, *earlier):
        if earlier:
            for key in sorted({(step, run), (-step, run)}):
                pieces[key] = after(pieces[key], *earlier)
        for way in (1, -1):
            at = [i for i in range(cols) if 0 <= i - way * step < cols and 0 <= i + way < cols]
            moved_on = lax.ppermute(pieces[-way * step, run], "col", [(i, i + way) for i in at])
            pieces[-way * (step + 1), run] = moved_on

    hop(0, 0)

    table = jnp.asarray(lay.table)[me_row]
    second = jnp.asarray([count[1] for count in lay.counts], jnp.int32)[me_row]
    is_moved = np.zeros((rows, leaves), bool)
    pairs = []
    for r in range(rows):
        for leaf, slot in lay.holder[r].items():
            if leaf != slot:
                is_moved[r, slot] = True
                pairs.append((leaf * rows + r, slot * rows + r))
    moved_here = jnp.asarray(is_moved)[me_row, me_leaf]
    lower, upper = top_inverse[half:], top_inverse[:half]
    swapped = lax.ppermute(upper, "row", [(r, rows - 1 - r) for r in range(rows)])
    moved = lax.ppermute(lower, ("leaf", "row"), pairs) if pairs else lower
    whole = jnp.where(me_leaf < second, swapped, jnp.where(moved_here, moved, lower))
    both = lower[: 2 * part]
    for chip in range(2, leaves, 2):
        both = jnp.where(me_leaf == chip, lax.ppermute(lower[chip * part : (chip + 2) * part], "leaf", [(0, chip)]), both)
    other = lax.ppermute(both[part:], "leaf", [(chip, chip + 1) for chip in range(0, leaves, 2)])
    extra = jnp.where(me_leaf % 2 == 0, both[:part], other)
    held = jnp.concatenate([whole.reshape(parts, part, width), extra[None]], axis=0)
    gathered = lax.all_gather(after(held, pieces[1, 0], pieces[-1, 0]), ("col", "leaf"), axis=0, tiled=False)
    own = jnp.stack([lower, swapped])
    hop(1, 0, gathered)

    chunks, each = 2, cols // rows
    order = ((me_row + 1 + jnp.arange(rows)) % rows).astype(jnp.int32)
    near = [[sorted(range(d * each, d * each + each), key=lambda block: abs(block - c)) for c in range(cols)] for d in range(rows)]
    near = np.asarray(near, np.int32)
    reach = np.abs(near - np.arange(cols)[None, :, None]).max(axis=(0, 1))
    near_here = jnp.asarray(near)[:, me_col]
    wanted = near_here[order[: rows - 1]].reshape(-1)
    info = jnp.concatenate([me_col[None], wanted, me_row * each + jnp.arange(each)]).astype(jnp.int32)
    leaf_here = me_leaf.astype(jnp.int32)[None]
    top_args = (leaf_here, gathered, own, chunks)
    early = top_product(lay, table, order[: rows - 1], *top_args, 0, [info])
    early_in = send_over_rows(early)
    if cols > 2:
        hop(0, 1, *early)
    sent, turned = panel_product(lay, pattern[0], table, order, gathered, normed, early)
    sent_in = send_over_rows(sent)
    middle = cols // 2
    for step in range(1, middle):
        hop(1, step, *sent)
        if step + 1 < cols - 1:
            hop(0, step + 1, *sent)
    kept = own_panel_product(lay, pattern[0], table, order, gathered, turned, early_in)
    tops = top_product(lay, table, order[rows - 1 :], *top_args, 0, [kept])
    late = top_product(lay, table, order[: rows - 1], *top_args, 1, tops)
    sigma_panel = -sum(sent_in, kept).reshape(-1, normed.shape[1])
    late = [after(value, *sent_in) for value in late]
    late_in = send_over_rows(late)
    for step in range(middle, cols - 1):
        hop(1, step, sigma_panel)
        if step + 1 < cols - 1:
            hop(0, step + 1, sigma_panel)

    terms_in, tokens = [], late
    for i in range(each):
        there = {key: piece for key, piece in pieces.items() if abs(key[0]) <= reach[i]}
        term = [diagonal_product(info, a * each + i, 1, there, sigma_panel, tokens) for a in range(rows - 1)]
        terms_in.append(send_over_rows(term))
        tokens = term + late_in
    mine = diagonal_product(info, (rows - 1) * each, each, pieces, sigma_panel, term)
    rest = diag_inverse[0] - mine.reshape(diag_inverse.shape[1:])
    tops = [*tops, *top_product(lay, table, order[rows - 1 :], *top_args, 1, [mine])]
    update = []
    for block in range(each):
        total = 0.0
        for i in range(each):
            for value in terms_in[i]:
                total += jnp.where(near_here[me_row, i] == me_row * each + block, value[0], 0.0)
        update.append(total)
    sigma_diag = rest - jnp.concatenate(update, axis=0)

    sigma_top = jnp.concatenate([sum(early_in, tops[0]), sum(late_in, tops[1])], axis=0).reshape(-1, width)
    return (sigma_top, sigma_panel[None], sigma_diag[None])


def solution(mesh):
    placed = (
        P("row", ("leaf", "col")),
        P("leaf", None),
        P("leaf", None, "col"),
        P("leaf", "row", "col"),
    )

    def whole(top_inverse, pattern, panel, diag_inverse):
        rows, leaves, cols = (mesh.shape[axis] for axis in ("row", "leaf", "col"))
        size = top_inverse.shape[0]
        lay = Layout(rows, leaves, cols, size // rows // 2, size // leaves // cols)
        return jax.shard_map(
            functools.partial(per_device, lay),
            mesh=mesh,
            in_specs=placed,
            out_specs=(P("row", ("leaf", "col")), P("leaf", "row", "col"), P("leaf", "row", "col")),
            check_vma=False,
        )(top_inverse, pattern, panel, diag_inverse)

    return whole
```

```python
import functools

import jax
import jax.numpy as jnp
import numpy as np
from jax import lax
from jax.experimental import pallas as pl
from jax.experimental.pallas import tpu as pltpu
from jax.sharding import PartitionSpec as P

BLK = 128
VMEM_BYTES = 58 * 1024 * 1024


def halves(value):
    high = value.astype(jnp.bfloat16)
    low = (value - high.astype(jnp.float32)).astype(jnp.bfloat16)
    return high, low


def dot(left, right):
    return jnp.dot(left, right, preferred_element_type=jnp.float32)


class Layout:
    def __init__(self, rows, leaves, cols, half, width):
        self.rows, self.leaves, self.cols, self.half, self.width = rows, leaves, cols, half, width
        self.part = half // leaves
        self.span = width * cols
        self.counts, self.holder, self.source = [], [], []
        for r in range(rows):
            count = [min(leaves, (q * half + half - 1) // self.span + 1) for q in (2 * r + 1, 2 * (rows - 1 - r))]
            assert count[0] + count[1] <= leaves + 1
            free = list(range(count[1], leaves))
            moved = [leaf for leaf in range(1, count[0]) if leaf not in free]
            slot = {leaf: leaf for leaf in range(1, count[0]) if leaf in free}
            left = [s for s in free if s not in slot]
            slot.update(zip(moved, left))
            self.counts.append(count)
            self.holder.append(slot)
        table = np.full((rows, 2, leaves, leaves), -1, np.int32)
        for r in range(rows):
            for j in range(leaves):
                table[r, 0, 0, j] = j * (leaves + 1) + leaves
                for leaf, slot in self.holder[r].items():
                    table[r, 0, leaf, j] = slot * (leaves + 1) + j
                for leaf in range(self.counts[r][1]):
                    table[r, 1, leaf, j] = leaf * (leaves + 1) + j
        self.table = table


def place_of(lay, pat, k):
    first = pat[k] * BLK
    leaf = first // lay.span
    rest = first - leaf * lay.span
    col = rest // lay.width
    return leaf, col, (rest - col * lay.width) // BLK


def fetch_entry(lay, pat, tab, gathered, t, sems, k):
    leaf, col, sub = place_of(lay, pat, k)
    lanes = pl.ds(pl.multiple_of(sub * BLK, BLK), BLK)
    for s in range(2):
        here = tab[s, leaf, 0] >= 0

        shared = leaf == 0 if s == 0 else False

        @pl.when(jnp.logical_and(here, jnp.logical_not(shared)))
        def _():
            slot = tab[s, leaf, 0] // (lay.leaves + 1)
            pltpu.make_async_copy(
                gathered.at[col * lay.leaves + slot, pl.ds(0, lay.leaves), :, lanes], t.at[k, s], sems.at[k, s]
            ).start()

        @pl.when(jnp.logical_and(here, shared))
        def _():
            for j in range(lay.leaves):
                pltpu.make_async_copy(
                    gathered.at[col * lay.leaves + j, lay.leaves, :, lanes], t.at[k, s, j], sems.at[k, s]
                ).start()

        @pl.when(jnp.logical_not(here))
        def _():
            t[k, s] = jnp.zeros(t.shape[2:], t.dtype)


def any_valid(lay, pat, tab, kp, s):
    first = tab[s, place_of(lay, pat, 2 * kp)[0], 0] >= 0
    second = tab[s, place_of(lay, pat, 2 * kp + 1)[0], 0] >= 0
    return jnp.logical_or(first, second)


def wait_pair(lay, pat, tab, t, sems, kp, s):
    for m in range(2):
        k = 2 * kp + m

        @pl.when(tab[s, place_of(lay, pat, k)[0], 0] >= 0)
        def _():
            pltpu.make_async_copy(t.at[k, s], t.at[k, s], sems.at[k, s]).wait()


def entry_pair(t, kp, s):
    return jnp.concatenate([t[2 * kp + m, s].reshape(-1, BLK) for m in range(2)], axis=1)


def back_product(turned_high, turned_low, high, low, s):
    return dot(turned_high[s], high) + dot(turned_low[s], high) + dot(turned_high[s], low)


def panel_kernel(lay, rows, tokens, pat, tab, order, gathered, p_ref, *refs):
    outs = refs[tokens : tokens + rows - 1]
    turned_high, turned_low, t, th, tl, image, sems = refs[tokens + rows - 1 :]
    number = t.shape[0]
    each = number // 2 // rows

    @pl.loop(0, number)
    def _(k):
        fetch_entry(lay, pat, tab, gathered, t, sems, k)

    image[...] = jnp.zeros_like(image)

    group = number // 2 // p_ref.shape[0]

    @pl.loop(0, number // 2 // group)
    def _(step):
        pairs = [step * group + m for m in range(group)]
        for s in range(2):
            found = False
            for kp in pairs:
                wait_pair(lay, pat, tab, t, sems, kp, s)
                found = jnp.logical_or(found, any_valid(lay, pat, tab, kp, s))

            @pl.when(found)
            def _():
                highs, lows = [], []
                for kp in pairs:
                    high, low = halves(entry_pair(t, kp, s))
                    th[kp, s] = high
                    tl[kp, s] = low
                    highs.append(high)
                    lows.append(low)
                image[s] += lax.dot_general(
                    p_ref[step],
                    jnp.concatenate(highs + highs + lows, axis=1),
                    (((1,), (1,)), ((), ())),
                    preferred_element_type=jnp.float32,
                )

    for s in range(2):
        high, low = halves(image[s])
        turned_high[s] = high
        turned_low[s] = low

    for a in range(rows - 1):

        @pl.loop(0, each)
        def _(i):
            kp = order[a] * each + i
            out = outs[a].at[i]
            out[...] = jnp.zeros(out.shape, out.dtype)
            for s in range(2):

                @pl.when(any_valid(lay, pat, tab, kp, s))
                def _():
                    out[...] += back_product(turned_high, turned_low, th[kp, s], tl[kp, s], s).T


def own_panel_kernel(lay, rows, tokens, pat, tab, order, gathered, turned_high, turned_low, *refs):
    out_ref, t, sems = refs[tokens:]
    each = t.shape[0] // 2 // rows
    first = order[rows - 1] * each

    @pl.loop(0, 2 * each)
    def _(i):
        fetch_entry(lay, pat, tab, gathered, t, sems, 2 * first + i)

    @pl.loop(0, each)
    def _(i):
        kp = first + i
        out = out_ref.at[i]
        out[...] = jnp.zeros(out.shape, out.dtype)
        for s in range(2):
            wait_pair(lay, pat, tab, t, sems, kp, s)

            @pl.when(any_valid(lay, pat, tab, kp, s))
            def _():
                high, low = halves(entry_pair(t, kp, s))
                out[...] += back_product(turned_high, turned_low, high, low, s).T


ANY = pl.BlockSpec(memory_space=pl.ANY)
VMEM = pl.BlockSpec(memory_space=pltpu.VMEM)
SMEM = pl.BlockSpec(memory_space=pltpu.SMEM)


def estimate(flops, values):
    return pl.CostEstimate(flops=flops, bytes_accessed=4 * values, transcendentals=0)


def split_kernel(p_ref, *refs):
    out_ref = refs[-1]
    deep = out_ref.shape[2] // 3

    @pl.loop(0, out_ref.shape[0])
    def _(step):
        high, low = halves(p_ref[pl.ds(pl.multiple_of(step * deep, deep), deep), :].T)
        out_ref[step] = jnp.concatenate([high, low, high], axis=1)


def split_panel(normed, tokens):
    depth, wide = normed.shape
    group = 4 if depth % (4 * BLK) == 0 else 2
    steps, deep = depth // (group * BLK), group * BLK
    return pl.pallas_call(
        split_kernel,
        out_shape=jax.ShapeDtypeStruct((steps, wide, 3 * deep), jnp.bfloat16),
        in_specs=[VMEM] + [ANY] * len(tokens),
        out_specs=VMEM,
        compiler_params=pltpu.CompilerParams(vmem_limit_bytes=VMEM_BYTES),
        cost_estimate=estimate(8 * depth * wide, 3 * depth * wide),
    )(normed, *tokens)


def panel_product(lay, pattern, table, order, gathered, split, tokens):
    number, wide, rows = pattern.shape[0], split.shape[1], order.shape[0]
    half = lay.half
    pairs = number // 2
    block = jax.ShapeDtypeStruct((pairs // rows, 2 * BLK, wide), jnp.float32)
    turned = jax.ShapeDtypeStruct((2, wide, half), jnp.bfloat16)
    result = pl.pallas_call(
        functools.partial(panel_kernel, lay, rows, len(tokens)),
        out_shape=[block] * (rows - 1) + [turned] * 2,
        in_specs=[SMEM] * 3 + [ANY, VMEM] + [ANY] * len(tokens),
        out_specs=[VMEM] * (rows + 1),
        scratch_shapes=[
            pltpu.VMEM((number, 2, lay.leaves, lay.part, BLK), jnp.float32),
            pltpu.VMEM((pairs, 2, half, 2 * BLK), jnp.bfloat16),
            pltpu.VMEM((pairs, 2, half, 2 * BLK), jnp.bfloat16),
            pltpu.VMEM((2, wide, half), jnp.float32),
            pltpu.SemaphoreType.DMA((number, 2)),
        ],
        compiler_params=pltpu.CompilerParams(vmem_limit_bytes=VMEM_BYTES),
        cost_estimate=estimate(18 * half * number * BLK * wide, 2 * half * number * BLK),
    )(pattern, table, order, gathered, split, *tokens)
    return result[: rows - 1], result[rows - 1 :]


def own_panel_product(lay, pattern, table, order, gathered, turned, tokens):
    number, wide, rows = pattern.shape[0], turned[0].shape[1], order.shape[0]
    half = lay.half
    return pl.pallas_call(
        functools.partial(own_panel_kernel, lay, rows, len(tokens)),
        out_shape=jax.ShapeDtypeStruct((number // 2 // rows, 2 * BLK, wide), jnp.float32),
        in_specs=[SMEM] * 3 + [ANY, VMEM, VMEM] + [ANY] * len(tokens),
        out_specs=VMEM,
        scratch_shapes=[
            pltpu.VMEM((number, 2, lay.leaves, lay.part, BLK), jnp.float32),
            pltpu.SemaphoreType.DMA((number, 2)),
        ],
        compiler_params=pltpu.CompilerParams(vmem_limit_bytes=VMEM_BYTES),
        cost_estimate=estimate(24 * half * number * BLK * wide, half * number * BLK),
    )(pattern, table, order, gathered, *turned, *tokens)


def top_kernel(lay, chunks, chunk, tokens, tab, dests, leaf_ref, g_ref, own_ref, *refs):
    count = dests.shape[0]
    outs, (own_turned, held, sems) = refs[tokens : tokens + count], refs[tokens + count :]
    parts, part = lay.leaves, lay.part
    each = outs[0].shape[0]

    def place(a, i):
        block = (dests[a] * chunks + chunk) * each + i
        leaf = block // lay.cols
        return leaf, block - leaf * lay.cols

    def wanted(leaf, s):
        return jnp.logical_and(tab[s, leaf, 0] >= 0, tab[s, leaf_ref[0], 0] >= 0)

    for a in range(count):

        @pl.loop(0, each)
        def _(i):
            leaf, col = place(a, i)
            for s in range(2):

                @pl.when(wanted(leaf, s))
                def _():
                    for j in range(parts):
                        entry = tab[s, leaf, j]
                        slot = entry // (parts + 1)
                        position = entry - slot * (parts + 1)
                        pltpu.make_async_copy(
                            g_ref.at[col * lay.leaves + slot, position],
                            held.at[a, i, s, pl.ds(j * part, part)],
                            sems.at[a, i, s],
                        ).start()

    for s in range(2):
        high, low = halves(own_ref[s].T)
        own_turned[s, 0] = high
        own_turned[s, 1] = low

    for a in range(count):

        @pl.loop(0, each)
        def _(i):
            leaf, col = place(a, i)
            out = outs[a].at[i]
            out[...] = jnp.zeros(out.shape, out.dtype)
            for s in range(2):

                @pl.when(wanted(leaf, s))
                def _():
                    pltpu.make_async_copy(held.at[a, i, s], held.at[a, i, s], sems.at[a, i, s]).wait()
                    high, low = halves(held[a, i, s])
                    total = dot(own_turned[s, 0], high) + dot(own_turned[s, 1], high) + dot(own_turned[s, 0], low)
                    out[...] += total.T


def top_product(lay, table, dests, me_leaf, gathered, own, chunks, chunk, tokens=()):
    count, width, half = dests.shape[0], lay.width, lay.half
    each = gathered.shape[0] // lay.rows // chunks
    block = jax.ShapeDtypeStruct((each, width, width), jnp.float32)
    return pl.pallas_call(
        functools.partial(top_kernel, lay, chunks, chunk, len(tokens)),
        out_shape=[block] * count,
        in_specs=[SMEM] * 3 + [ANY, VMEM] + [ANY] * len(tokens),
        out_specs=[VMEM] * count,
        scratch_shapes=[
            pltpu.VMEM((2, 2, width, half), jnp.bfloat16),
            pltpu.VMEM((count, each, 2, half, width), jnp.float32),
            pltpu.SemaphoreType.DMA((count, each, 2)),
        ],
        compiler_params=pltpu.CompilerParams(vmem_limit_bytes=VMEM_BYTES),
        cost_estimate=estimate(12 * half * count * each * width * width, 2 * half * count * each * width),
    )(table, dests, me_leaf, gathered, own, *tokens)


def diagonal_kernel(steps, first, tokens, info, *refs):
    sources, refs = list(zip(steps, refs)), refs[len(steps) :]
    sigma, (out_ref, held, sems) = refs[0], refs[1 + tokens :]
    each = out_ref.shape[0]
    for i in range(each):
        away = info[1 + first + i] - info[0]
        for (step, run), source in sources:

            @pl.when(away == step)
            def _():
                rows = pl.ds(run * source.shape[0], source.shape[0])
                pltpu.make_async_copy(source, held.at[i, rows], sems.at[i]).start()

    turned_high, turned_low = halves(sigma[...].T)
    for i in range(each):
        pltpu.make_async_copy(held.at[i], held.at[i], sems.at[i]).wait()
        high, low = halves(held[i])
        total = dot(turned_high, high) + dot(turned_low, high) + dot(turned_high, low)
        out_ref[i] = total.T


def diagonal_product(info, first, each, pieces, sigma, tokens):
    depth, wide = sigma.shape
    return pl.pallas_call(
        functools.partial(diagonal_kernel, tuple(pieces), first, len(tokens)),
        out_shape=jax.ShapeDtypeStruct((each, wide, wide), jnp.float32),
        in_specs=[SMEM] + [ANY] * len(pieces) + [VMEM] + [ANY] * len(tokens),
        out_specs=VMEM,
        scratch_shapes=[pltpu.VMEM((each, depth, wide), jnp.float32), pltpu.SemaphoreType.DMA((each,))],
        compiler_params=pltpu.CompilerParams(vmem_limit_bytes=VMEM_BYTES),
        cost_estimate=estimate(6 * each * depth * wide * wide, (each + 1) * depth * wide),
    )(info, *pieces.values(), sigma, *tokens)


def after(value, *earlier):
    return pl.pallas_call(
        lambda *refs: None,
        out_shape=jax.ShapeDtypeStruct(value.shape, value.dtype),
        in_specs=[ANY] * (1 + len(earlier)),
        out_specs=ANY,
        input_output_aliases={0: 0},
        cost_estimate=estimate(0, 0),
    )(value, *earlier)


def send_over_rows(sent):
    rows = lax.axis_size("row")
    return [lax.ppermute(value, "row", [(i, (i + a + 1) % rows) for i in range(rows)]) for a, value in enumerate(sent)]


def per_device(lay, top_inverse, pattern, panel, diag_inverse):
    rows, cols, leaves = (lax.axis_size(axis) for axis in ("row", "col", "leaf"))
    me_row, me_col, me_leaf = (lax.axis_index(axis) for axis in ("row", "col", "leaf"))
    half, width, parts, part = lay.half, lay.width, lay.leaves, lay.part
    normed = panel[0]

    count = normed.shape[0] // rows
    own_rows = lax.dynamic_slice_in_dim(normed, me_row * count, count, 0)
    runs = 2
    pieces = {(0, run): own_rows[run * count // runs : (run + 1) * count // runs] for run in range(runs)}

    def hop(run, step, *earlier):
        if earlier:
            for key in sorted({(step, run), (-step, run)}):
                pieces[key] = after(pieces[key], *earlier)
        for way in (1, -1):
            at = [i for i in range(cols) if 0 <= i - way * step < cols and 0 <= i + way < cols]
            moved_on = lax.ppermute(pieces[-way * step, run], "col", [(i, i + way) for i in at])
            pieces[-way * (step + 1), run] = moved_on

    hop(0, 0)

    table = jnp.asarray(lay.table)[me_row]
    second = jnp.asarray([count[1] for count in lay.counts], jnp.int32)[me_row]
    is_moved = np.zeros((rows, leaves), bool)
    pairs = []
    for r in range(rows):
        for leaf, slot in lay.holder[r].items():
            if leaf != slot:
                is_moved[r, slot] = True
                pairs.append((leaf * rows + r, slot * rows + r))
    moved_here = jnp.asarray(is_moved)[me_row, me_leaf]
    lower, upper = top_inverse[half:], top_inverse[:half]
    swapped = lax.ppermute(upper, "row", [(r, rows - 1 - r) for r in range(rows)])
    moved = lax.ppermute(lower, ("leaf", "row"), pairs) if pairs else lower
    whole = jnp.where(me_leaf < second, swapped, jnp.where(moved_here, moved, lower))
    both = lower[: 2 * part]
    for chip in range(2, leaves, 2):
        both = jnp.where(me_leaf == chip, lax.ppermute(lower[chip * part : (chip + 2) * part], "leaf", [(0, chip)]), both)
    split = split_panel(normed, [both])
    other = lax.ppermute(both[part:], "leaf", [(chip, chip + 1) for chip in range(0, leaves, 2)])
    extra = jnp.where(me_leaf % 2 == 0, both[:part], other)
    held = jnp.concatenate([whole.reshape(parts, part, width), extra[None]], axis=0)
    gathered = lax.all_gather(after(held, pieces[1, 0], pieces[-1, 0], split), ("col", "leaf"), axis=0, tiled=False)
    own = jnp.stack([lower, swapped])
    hop(1, 0, gathered)

    chunks, each = 2, cols // rows
    order = ((me_row + 1 + jnp.arange(rows)) % rows).astype(jnp.int32)
    near = [[sorted(range(d * each, d * each + each), key=lambda block: abs(block - c)) for c in range(cols)] for d in range(rows)]
    near = np.asarray(near, np.int32)
    reach = np.abs(near - np.arange(cols)[None, :, None]).max(axis=(0, 1))
    near_here = jnp.asarray(near)[:, me_col]
    wanted = near_here[order[: rows - 1]].reshape(-1)
    info = jnp.concatenate([me_col[None], wanted, me_row * each + jnp.arange(each)]).astype(jnp.int32)
    leaf_here = me_leaf.astype(jnp.int32)[None]
    top_args = (leaf_here, gathered, own, chunks)
    early = top_product(lay, table, order[: rows - 1], *top_args, 0, [info])
    early_in = send_over_rows(early)
    if cols > 2:
        hop(0, 1, *early)
    sent, turned = panel_product(lay, pattern[0], table, order, gathered, split, early)
    sent_in = send_over_rows(sent)
    middle = cols // 2
    for step in range(1, middle):
        hop(1, step, *sent)
        if step + 1 < cols - 1:
            hop(0, step + 1, *sent)
    kept = own_panel_product(lay, pattern[0], table, order, gathered, turned, early_in)
    tops = top_product(lay, table, order[rows - 1 :], *top_args, 0, [kept])
    late = top_product(lay, table, order[: rows - 1], *top_args, 1, tops)
    sigma_panel = -sum(sent_in, kept).reshape(-1, normed.shape[1])
    late = [after(value, *sent_in) for value in late]
    late_in = send_over_rows(late)
    for step in range(middle, cols - 1):
        hop(1, step, sigma_panel)
        if step + 1 < cols - 1:
            hop(0, step + 1, sigma_panel)

    terms_in, tokens = [], late
    for i in range(each):
        there = {key: piece for key, piece in pieces.items() if abs(key[0]) <= reach[i]}
        term = [diagonal_product(info, a * each + i, 1, there, sigma_panel, tokens) for a in range(rows - 1)]
        terms_in.append(send_over_rows(term))
        tokens = term + late_in
    mine = diagonal_product(info, (rows - 1) * each, each, pieces, sigma_panel, term)
    rest = diag_inverse[0].reshape(mine.shape) - mine
    tops = [*tops, *top_product(lay, table, order[rows - 1 :], *top_args, 1, [mine])]
    for i in range(each):
        here = near_here[me_row, i] == me_row * each + jnp.arange(each)
        for value in terms_in[i]:
            rest -= jnp.where(here[:, None, None], value, 0.0)
    sigma_diag = rest.reshape(diag_inverse.shape[1:])

    sigma_top = jnp.concatenate([sum(early_in, tops[0]), sum(late_in, tops[1])], axis=0).reshape(-1, width)
    return (sigma_top, sigma_panel[None], sigma_diag[None])


def solution(mesh):
    placed = (
        P("row", ("leaf", "col")),
        P("leaf", None),
        P("leaf", None, "col"),
        P("leaf", "row", "col"),
    )

    def whole(top_inverse, pattern, panel, diag_inverse):
        rows, leaves, cols = (mesh.shape[axis] for axis in ("row", "leaf", "col"))
        size = top_inverse.shape[0]
        lay = Layout(rows, leaves, cols, size // rows // 2, size // leaves // cols)
        return jax.shard_map(
            functools.partial(per_device, lay),
            mesh=mesh,
            in_specs=placed,
            out_specs=(P("row", ("leaf", "col")), P("leaf", "row", "col"), P("leaf", "row", "col")),
            check_vma=False,
        )(top_inverse, pattern, panel, diag_inverse)

    return whole
```

```python
import functools

import jax
import jax.numpy as jnp
import numpy as np
from jax import lax
from jax.experimental import pallas as pl
from jax.experimental.pallas import tpu as pltpu
from jax.sharding import PartitionSpec as P

BLK = 128
VMEM_BYTES = 58 * 1024 * 1024


def halves(value):
    high = value.astype(jnp.bfloat16)
    low = (value - high.astype(jnp.float32)).astype(jnp.bfloat16)
    return high, low


def dot(left, right):
    return jnp.dot(left, right, preferred_element_type=jnp.float32)


class Layout:
    def __init__(self, rows, leaves, cols, half, width):
        self.rows, self.leaves, self.cols, self.half, self.width = rows, leaves, cols, half, width
        self.part = half // leaves
        self.span = width * cols
        self.counts, self.holder, self.source = [], [], []
        for r in range(rows):
            count = [min(leaves, (q * half + half - 1) // self.span + 1) for q in (2 * r + 1, 2 * (rows - 1 - r))]
            assert count[0] + count[1] <= leaves + 1
            free = list(range(count[1], leaves))
            moved = [leaf for leaf in range(1, count[0]) if leaf not in free]
            slot = {leaf: leaf for leaf in range(1, count[0]) if leaf in free}
            left = [s for s in free if s not in slot]
            slot.update(zip(moved, left))
            self.counts.append(count)
            self.holder.append(slot)
        table = np.full((rows, 2, leaves, leaves), -1, np.int32)
        for r in range(rows):
            for j in range(leaves):
                table[r, 0, 0, j] = j * (leaves + 1) + leaves
                for leaf, slot in self.holder[r].items():
                    table[r, 0, leaf, j] = slot * (leaves + 1) + j
                for leaf in range(self.counts[r][1]):
                    table[r, 1, leaf, j] = leaf * (leaves + 1) + j
        self.table = table


def place_of(lay, pat, k):
    first = pat[k] * BLK
    leaf = first // lay.span
    rest = first - leaf * lay.span
    col = rest // lay.width
    return leaf, col, (rest - col * lay.width) // BLK


def fetch_entry(lay, pat, tab, gathered, t, sems, k):
    leaf, col, sub = place_of(lay, pat, k)
    lanes = pl.ds(pl.multiple_of(sub * BLK, BLK), BLK)
    for s in range(2):
        here = tab[s, leaf, 0] >= 0

        shared = leaf == 0 if s == 0 else False

        @pl.when(jnp.logical_and(here, jnp.logical_not(shared)))
        def _():
            slot = tab[s, leaf, 0] // (lay.leaves + 1)
            pltpu.make_async_copy(
                gathered.at[col * lay.leaves + slot, pl.ds(0, lay.leaves), :, lanes], t.at[k, s], sems.at[k, s]
            ).start()

        @pl.when(jnp.logical_and(here, shared))
        def _():
            for j in range(lay.leaves):
                pltpu.make_async_copy(
                    gathered.at[col * lay.leaves + j, lay.leaves, :, lanes], t.at[k, s, j], sems.at[k, s]
                ).start()

        @pl.when(jnp.logical_not(here))
        def _():
            t[k, s] = jnp.zeros(t.shape[2:], t.dtype)


def any_valid(lay, pat, tab, kp, s):
    first = tab[s, place_of(lay, pat, 2 * kp)[0], 0] >= 0
    second = tab[s, place_of(lay, pat, 2 * kp + 1)[0], 0] >= 0
    return jnp.logical_or(first, second)


def wait_pair(lay, pat, tab, t, sems, kp, s):
    for m in range(2):
        k = 2 * kp + m

        @pl.when(tab[s, place_of(lay, pat, k)[0], 0] >= 0)
        def _():
            pltpu.make_async_copy(t.at[k, s], t.at[k, s], sems.at[k, s]).wait()


def entry_pair(t, kp, s):
    return jnp.concatenate([t[2 * kp + m, s].reshape(-1, BLK) for m in range(2)], axis=1)


def back_product(turned_high, turned_low, high, low, s):
    return dot(turned_high[s], high) + dot(turned_low[s], high) + dot(turned_high[s], low)


def panel_kernel(lay, rows, tokens, pat, tab, order, gathered, p_ref, *refs):
    outs = refs[tokens : tokens + rows - 1]
    turned_high, turned_low, t, th, tl, image, sems = refs[tokens + rows - 1 :]
    number = t.shape[0]
    each = number // 2 // rows

    @pl.loop(0, number)
    def _(k):
        fetch_entry(lay, pat, tab, gathered, t, sems, k)

    image[...] = jnp.zeros_like(image)

    group = 2 if number % 4 == 0 else 1

    @pl.loop(0, number // 2 // group)
    def _(step):
        deep = 2 * group * BLK
        span = pl.ds(pl.multiple_of(step * deep, deep), deep)
        p_high, p_low = halves(p_ref[span, :])
        stacked = jnp.concatenate([p_high, p_low, p_high], axis=0)
        pairs = [step * group + m for m in range(group)]
        for s in range(2):
            found = False
            for kp in pairs:
                wait_pair(lay, pat, tab, t, sems, kp, s)
                found = jnp.logical_or(found, any_valid(lay, pat, tab, kp, s))

            @pl.when(found)
            def _():
                highs, lows = [], []
                for kp in pairs:
                    high, low = halves(entry_pair(t, kp, s))
                    th[kp, s] = high
                    tl[kp, s] = low
                    highs.append(high)
                    lows.append(low)
                image[s] += dot(jnp.concatenate(highs + highs + lows, axis=1), stacked)

    for s in range(2):
        high, low = halves(image[s].T)
        turned_high[s] = high
        turned_low[s] = low

    for a in range(rows - 1):

        @pl.loop(0, each)
        def _(i):
            kp = order[a] * each + i
            out = outs[a].at[i]
            out[...] = jnp.zeros(out.shape, out.dtype)
            for s in range(2):

                @pl.when(any_valid(lay, pat, tab, kp, s))
                def _():
                    out[...] += back_product(turned_high, turned_low, th[kp, s], tl[kp, s], s).T


def own_panel_kernel(lay, rows, tokens, pat, tab, order, gathered, turned_high, turned_low, *refs):
    out_ref, t, sems = refs[tokens:]
    each = t.shape[0] // 2 // rows
    first = order[rows - 1] * each

    @pl.loop(0, 2 * each)
    def _(i):
        fetch_entry(lay, pat, tab, gathered, t, sems, 2 * first + i)

    @pl.loop(0, each)
    def _(i):
        kp = first + i
        out = out_ref.at[i]
        out[...] = jnp.zeros(out.shape, out.dtype)
        for s in range(2):
            wait_pair(lay, pat, tab, t, sems, kp, s)

            @pl.when(any_valid(lay, pat, tab, kp, s))
            def _():
                high, low = halves(entry_pair(t, kp, s))
                out[...] += back_product(turned_high, turned_low, high, low, s).T


ANY = pl.BlockSpec(memory_space=pl.ANY)
VMEM = pl.BlockSpec(memory_space=pltpu.VMEM)
SMEM = pl.BlockSpec(memory_space=pltpu.SMEM)


def estimate(flops, values):
    return pl.CostEstimate(flops=flops, bytes_accessed=4 * values, transcendentals=0)


def panel_product(lay, pattern, table, order, gathered, normed, tokens):
    number, wide, rows = pattern.shape[0], normed.shape[1], order.shape[0]
    half = lay.half
    pairs = number // 2
    block = jax.ShapeDtypeStruct((pairs // rows, 2 * BLK, wide), jnp.float32)
    turned = jax.ShapeDtypeStruct((2, wide, half), jnp.bfloat16)
    result = pl.pallas_call(
        functools.partial(panel_kernel, lay, rows, len(tokens)),
        out_shape=[block] * (rows - 1) + [turned] * 2,
        in_specs=[SMEM] * 3 + [ANY, VMEM] + [ANY] * len(tokens),
        out_specs=[VMEM] * (rows + 1),
        scratch_shapes=[
            pltpu.VMEM((number, 2, lay.leaves, lay.part, BLK), jnp.float32),
            pltpu.VMEM((pairs, 2, half, 2 * BLK), jnp.bfloat16),
            pltpu.VMEM((pairs, 2, half, 2 * BLK), jnp.bfloat16),
            pltpu.VMEM((2, half, wide), jnp.float32),
            pltpu.SemaphoreType.DMA((number, 2)),
        ],
        compiler_params=pltpu.CompilerParams(vmem_limit_bytes=VMEM_BYTES),
        cost_estimate=estimate(18 * half * number * BLK * wide, 2 * half * number * BLK),
    )(pattern, table, order, gathered, normed, *tokens)
    return result[: rows - 1], result[rows - 1 :]


def own_panel_product(lay, pattern, table, order, gathered, turned, tokens):
    number, wide, rows = pattern.shape[0], turned[0].shape[1], order.shape[0]
    half = lay.half
    return pl.pallas_call(
        functools.partial(own_panel_kernel, lay, rows, len(tokens)),
        out_shape=jax.ShapeDtypeStruct((number // 2 // rows, 2 * BLK, wide), jnp.float32),
        in_specs=[SMEM] * 3 + [ANY, VMEM, VMEM] + [ANY] * len(tokens),
        out_specs=VMEM,
        scratch_shapes=[
            pltpu.VMEM((number, 2, lay.leaves, lay.part, BLK), jnp.float32),
            pltpu.SemaphoreType.DMA((number, 2)),
        ],
        compiler_params=pltpu.CompilerParams(vmem_limit_bytes=VMEM_BYTES),
        cost_estimate=estimate(24 * half * number * BLK * wide, half * number * BLK),
    )(pattern, table, order, gathered, *turned, *tokens)


def top_kernel(lay, chunks, chunk, tokens, tab, dests, leaf_ref, g_ref, own_ref, *refs):
    count = dests.shape[0]
    outs, (own_turned, held, sems) = refs[tokens : tokens + count], refs[tokens + count :]
    parts, part = lay.leaves, lay.part
    each = outs[0].shape[0]

    def place(a, i):
        block = (dests[a] * chunks + chunk) * each + i
        leaf = block // lay.cols
        return leaf, block - leaf * lay.cols

    def wanted(leaf, s):
        return jnp.logical_and(tab[s, leaf, 0] >= 0, tab[s, leaf_ref[0], 0] >= 0)

    for a in range(count):

        @pl.loop(0, each)
        def _(i):
            leaf, col = place(a, i)
            for s in range(2):

                @pl.when(wanted(leaf, s))
                def _():
                    for j in range(parts):
                        entry = tab[s, leaf, j]
                        slot = entry // (parts + 1)
                        position = entry - slot * (parts + 1)
                        pltpu.make_async_copy(
                            g_ref.at[col * lay.leaves + slot, position],
                            held.at[a, i, s, pl.ds(j * part, part)],
                            sems.at[a, i, s],
                        ).start()

    for s in range(2):
        high, low = halves(own_ref[s].T)
        own_turned[s, 0] = high
        own_turned[s, 1] = low

    for a in range(count):

        @pl.loop(0, each)
        def _(i):
            leaf, col = place(a, i)
            out = outs[a].at[i]
            out[...] = jnp.zeros(out.shape, out.dtype)
            for s in range(2):

                @pl.when(wanted(leaf, s))
                def _():
                    pltpu.make_async_copy(held.at[a, i, s], held.at[a, i, s], sems.at[a, i, s]).wait()
                    high, low = halves(held[a, i, s])
                    total = dot(own_turned[s, 0], high) + dot(own_turned[s, 1], high) + dot(own_turned[s, 0], low)
                    out[...] += total.T


def top_product(lay, table, dests, me_leaf, gathered, own, chunks, chunk, tokens=()):
    count, width, half = dests.shape[0], lay.width, lay.half
    each = gathered.shape[0] // lay.rows // chunks
    block = jax.ShapeDtypeStruct((each, width, width), jnp.float32)
    return pl.pallas_call(
        functools.partial(top_kernel, lay, chunks, chunk, len(tokens)),
        out_shape=[block] * count,
        in_specs=[SMEM] * 3 + [ANY, VMEM] + [ANY] * len(tokens),
        out_specs=[VMEM] * count,
        scratch_shapes=[
            pltpu.VMEM((2, 2, width, half), jnp.bfloat16),
            pltpu.VMEM((count, each, 2, half, width), jnp.float32),
            pltpu.SemaphoreType.DMA((count, each, 2)),
        ],
        compiler_params=pltpu.CompilerParams(vmem_limit_bytes=VMEM_BYTES),
        cost_estimate=estimate(12 * half * count * each * width * width, 2 * half * count * each * width),
    )(table, dests, me_leaf, gathered, own, *tokens)


def diagonal_kernel(steps, first, tokens, info, *refs):
    sources, refs = list(zip(steps, refs)), refs[len(steps) :]
    sigma, (out_ref, held, sems) = refs[0], refs[1 + tokens :]
    each = out_ref.shape[0]
    for i in range(each):
        away = info[1 + first + i] - info[0]
        for (step, run), source in sources:

            @pl.when(away == step)
            def _():
                rows = pl.ds(run * source.shape[0], source.shape[0])
                pltpu.make_async_copy(source, held.at[i, rows], sems.at[i]).start()

    turned_high, turned_low = halves(sigma[...].T)
    for i in range(each):
        pltpu.make_async_copy(held.at[i], held.at[i], sems.at[i]).wait()
        high, low = halves(held[i])
        total = dot(turned_high, high) + dot(turned_low, high) + dot(turned_high, low)
        out_ref[i] = total.T


def diagonal_product(info, first, each, pieces, sigma, tokens):
    depth, wide = sigma.shape
    return pl.pallas_call(
        functools.partial(diagonal_kernel, tuple(pieces), first, len(tokens)),
        out_shape=jax.ShapeDtypeStruct((each, wide, wide), jnp.float32),
        in_specs=[SMEM] + [ANY] * len(pieces) + [VMEM] + [ANY] * len(tokens),
        out_specs=VMEM,
        scratch_shapes=[pltpu.VMEM((each, depth, wide), jnp.float32), pltpu.SemaphoreType.DMA((each,))],
        compiler_params=pltpu.CompilerParams(vmem_limit_bytes=VMEM_BYTES),
        cost_estimate=estimate(6 * each * depth * wide * wide, (each + 1) * depth * wide),
    )(info, *pieces.values(), sigma, *tokens)


def after(value, *earlier):
    return pl.pallas_call(
        lambda *refs: None,
        out_shape=jax.ShapeDtypeStruct(value.shape, value.dtype),
        in_specs=[ANY] * (1 + len(earlier)),
        out_specs=ANY,
        input_output_aliases={0: 0},
        cost_estimate=estimate(0, 0),
    )(value, *earlier)


def send_over_rows(sent):
    rows = lax.axis_size("row")
    return [lax.ppermute(value, "row", [(i, (i + a + 1) % rows) for i in range(rows)]) for a, value in enumerate(sent)]


def per_device(lay, top_inverse, pattern, panel, diag_inverse):
    rows, cols, leaves = (lax.axis_size(axis) for axis in ("row", "col", "leaf"))
    me_row, me_col, me_leaf = (lax.axis_index(axis) for axis in ("row", "col", "leaf"))
    half, width, parts, part = lay.half, lay.width, lay.leaves, lay.part
    normed = panel[0]

    count = normed.shape[0] // rows
    own_rows = lax.dynamic_slice_in_dim(normed, me_row * count, count, 0)
    runs = 2
    pieces = {(0, run): own_rows[run * count // runs : (run + 1) * count // runs] for run in range(runs)}

    def hop(run, step, *earlier):
        if earlier:
            for key in sorted({(step, run), (-step, run)}):
                pieces[key] = after(pieces[key], *earlier)
        for way in (1, -1):
            at = [i for i in range(cols) if 0 <= i - way * step < cols and 0 <= i + way < cols]
            moved_on = lax.ppermute(pieces[-way * step, run], "col", [(i, i + way) for i in at])
            pieces[-way * (step + 1), run] = moved_on

    hop(0, 0)

    table = jnp.asarray(lay.table)[me_row]
    second = jnp.asarray([count[1] for count in lay.counts], jnp.int32)[me_row]
    is_moved = np.zeros((rows, leaves), bool)
    pairs = []
    for r in range(rows):
        for leaf, slot in lay.holder[r].items():
            if leaf != slot:
                is_moved[r, slot] = True
                pairs.append((leaf * rows + r, slot * rows + r))
    moved_here = jnp.asarray(is_moved)[me_row, me_leaf]
    lower, upper = top_inverse[half:], top_inverse[:half]
    swapped = lax.ppermute(upper, "row", [(r, rows - 1 - r) for r in range(rows)])
    moved = lax.ppermute(lower, ("leaf", "row"), pairs) if pairs else lower
    whole = jnp.where(me_leaf < second, swapped, jnp.where(moved_here, moved, lower))
    both = lower[: 2 * part]
    for chip in range(2, leaves, 2):
        both = jnp.where(me_leaf == chip, lax.ppermute(lower[chip * part : (chip + 2) * part], "leaf", [(0, chip)]), both)
    other = lax.ppermute(both[part:], "leaf", [(chip, chip + 1) for chip in range(0, leaves, 2)])
    extra = jnp.where(me_leaf % 2 == 0, both[:part], other)
    held = jnp.concatenate([whole.reshape(parts, part, width), extra[None]], axis=0)
    gathered = lax.all_gather(after(held, pieces[1, 0], pieces[-1, 0]), ("col", "leaf"), axis=0, tiled=False)
    own = jnp.stack([lower, swapped])
    hop(1, 0, gathered)

    chunks, each = 2, cols // rows
    order = ((me_row + 1 + jnp.arange(rows)) % rows).astype(jnp.int32)
    near = [[sorted(range(d * each, d * each + each), key=lambda block: abs(block - c)) for c in range(cols)] for d in range(rows)]
    near = np.asarray(near, np.int32)
    reach = np.abs(near - np.arange(cols)[None, :, None]).max(axis=(0, 1))
    near_here = jnp.asarray(near)[:, me_col]
    wanted = near_here[order[: rows - 1]].reshape(-1)
    info = jnp.concatenate([me_col[None], wanted, me_row * each + jnp.arange(each)]).astype(jnp.int32)
    leaf_here = me_leaf.astype(jnp.int32)[None]
    top_args = (leaf_here, gathered, own, chunks)
    early = top_product(lay, table, order[: rows - 1], *top_args, 0, [info])
    early_in = send_over_rows(early)
    if cols > 2:
        hop(0, 1, *early)
    sent, turned = panel_product(lay, pattern[0], table, order, gathered, normed, early)
    sent_in = send_over_rows(sent)
    middle = cols // 2
    for step in range(1, middle):
        hop(1, step, *sent)
        if step + 1 < cols - 1:
            hop(0, step + 1, *sent)
    kept = own_panel_product(lay, pattern[0], table, order, gathered, turned, early_in)
    tops = top_product(lay, table, order[rows - 1 :], *top_args, 0, [kept])
    late = top_product(lay, table, order[: rows - 1], *top_args, 1, tops)
    sigma_panel = -sum(sent_in, kept).reshape(-1, normed.shape[1])
    late = [after(value, *sent_in) for value in late]
    late_in = send_over_rows(late)
    waiting = []
    for run, step in [(run, step + 1 - run) for step in range(middle, cols - 1) for run in (1, 0)]:
        if step < cols - 1 and step < reach[0]:
            hop(run, step, sigma_panel, *late)
        elif step < cols - 1:
            waiting.append((run, step))

    terms_in, tokens = [], late
    for i in range(each):
        there = {key: piece for key, piece in pieces.items() if abs(key[0]) <= reach[i]}
        term = [diagonal_product(info, a * each + i, 1, there, sigma_panel, tokens) for a in range(rows - 1)]
        terms_in.append(send_over_rows(term))
        while waiting:
            hop(*waiting.pop(0), *term)
        tokens = term + late_in
    mine = diagonal_product(info, (rows - 1) * each, each, pieces, sigma_panel, term)
    rest = diag_inverse[0] - mine.reshape(diag_inverse.shape[1:])
    tops = [*tops, *top_product(lay, table, order[rows - 1 :], *top_args, 1, [mine])]
    update = []
    for block in range(each):
        total = 0.0
        for i in range(each):
            for value in terms_in[i]:
                total += jnp.where(near_here[me_row, i] == me_row * each + block, value[0], 0.0)
        update.append(total)
    sigma_diag = rest - jnp.concatenate(update, axis=0)

    sigma_top = jnp.concatenate([sum(early_in, tops[0]), sum(late_in, tops[1])], axis=0).reshape(-1, width)
    return (sigma_top, sigma_panel[None], sigma_diag[None])


def solution(mesh):
    placed = (
        P("row", ("leaf", "col")),
        P("leaf", None),
        P("leaf", None, "col"),
        P("leaf", "row", "col"),
    )

    def whole(top_inverse, pattern, panel, diag_inverse):
        rows, leaves, cols = (mesh.shape[axis] for axis in ("row", "leaf", "col"))
        size = top_inverse.shape[0]
        lay = Layout(rows, leaves, cols, size // rows // 2, size // leaves // cols)
        return jax.shard_map(
            functools.partial(per_device, lay),
            mesh=mesh,
            in_specs=placed,
            out_specs=(P("row", ("leaf", "col")), P("leaf", "row", "col"), P("leaf", "row", "col")),
            check_vma=False,
        )(top_inverse, pattern, panel, diag_inverse)

    return whole
```

```python
import functools

import jax
import jax.numpy as jnp
import numpy as np
from jax import lax
from jax.experimental import pallas as pl
from jax.experimental.pallas import tpu as pltpu
from jax.sharding import PartitionSpec as P

BLK = 128
VMEM_BYTES = 58 * 1024 * 1024


def halves(value):
    high = value.astype(jnp.bfloat16)
    low = (value - high.astype(jnp.float32)).astype(jnp.bfloat16)
    return high, low


def dot(left, right):
    return jnp.dot(left, right, preferred_element_type=jnp.float32)


class Layout:
    def __init__(self, rows, leaves, cols, half, width):
        self.rows, self.leaves, self.cols, self.half, self.width = rows, leaves, cols, half, width
        self.part = half // leaves
        self.span = width * cols
        self.counts, self.holder, self.source = [], [], []
        for r in range(rows):
            count = [min(leaves, (q * half + half - 1) // self.span + 1) for q in (2 * r + 1, 2 * (rows - 1 - r))]
            assert count[0] + count[1] <= leaves + 1
            free = list(range(count[1], leaves))
            moved = [leaf for leaf in range(1, count[0]) if leaf not in free]
            slot = {leaf: leaf for leaf in range(1, count[0]) if leaf in free}
            left = [s for s in free if s not in slot]
            slot.update(zip(moved, left))
            self.counts.append(count)
            self.holder.append(slot)
        table = np.full((rows, 2, leaves, leaves), -1, np.int32)
        for r in range(rows):
            for j in range(leaves):
                table[r, 0, 0, j] = j * (leaves + 1) + leaves
                for leaf, slot in self.holder[r].items():
                    table[r, 0, leaf, j] = slot * (leaves + 1) + j
                for leaf in range(self.counts[r][1]):
                    table[r, 1, leaf, j] = leaf * (leaves + 1) + j
        self.table = table


def place_of(lay, pat, k):
    first = pat[k] * BLK
    leaf = first // lay.span
    rest = first - leaf * lay.span
    col = rest // lay.width
    return leaf, col, (rest - col * lay.width) // BLK


def fetch_entry(lay, pat, tab, gathered, t, sems, k):
    leaf, col, sub = place_of(lay, pat, k)
    lanes = pl.ds(pl.multiple_of(sub * BLK, BLK), BLK)
    for s in range(2):
        here = tab[s, leaf, 0] >= 0

        shared = leaf == 0 if s == 0 else False

        @pl.when(jnp.logical_and(here, jnp.logical_not(shared)))
        def _():
            slot = tab[s, leaf, 0] // (lay.leaves + 1)
            pltpu.make_async_copy(
                gathered.at[col * lay.leaves + slot, pl.ds(0, lay.leaves), :, lanes], t.at[k, s], sems.at[k, s]
            ).start()

        @pl.when(jnp.logical_and(here, shared))
        def _():
            for j in range(lay.leaves):
                pltpu.make_async_copy(
                    gathered.at[col * lay.leaves + j, lay.leaves, :, lanes], t.at[k, s, j], sems.at[k, s]
                ).start()

        @pl.when(jnp.logical_not(here))
        def _():
            t[k, s] = jnp.zeros(t.shape[2:], t.dtype)


def any_valid(lay, pat, tab, kp, s):
    first = tab[s, place_of(lay, pat, 2 * kp)[0], 0] >= 0
    second = tab[s, place_of(lay, pat, 2 * kp + 1)[0], 0] >= 0
    return jnp.logical_or(first, second)


def wait_pair(lay, pat, tab, t, sems, kp, s):
    for m in range(2):
        k = 2 * kp + m

        @pl.when(tab[s, place_of(lay, pat, k)[0], 0] >= 0)
        def _():
            pltpu.make_async_copy(t.at[k, s], t.at[k, s], sems.at[k, s]).wait()


def entry_pair(t, kp, s):
    return jnp.concatenate([t[2 * kp + m, s].reshape(-1, BLK) for m in range(2)], axis=1)


def back_product(turned_high, turned_low, high, low, s):
    return dot(turned_high[s], high) + dot(turned_low[s], high) + dot(turned_high[s], low)


def panel_kernel(lay, rows, tokens, pat, tab, order, gathered, p_ref, *refs):
    outs = refs[tokens : tokens + rows - 1]
    turned_high, turned_low, t, th, tl, image, sems = refs[tokens + rows - 1 :]
    number = t.shape[0]
    each = number // 2 // rows

    @pl.loop(0, number)
    def _(k):
        fetch_entry(lay, pat, tab, gathered, t, sems, k)

    image[...] = jnp.zeros_like(image)

    group = 2 if number % 4 == 0 else 1

    @pl.loop(0, number // 2 // group)
    def _(step):
        deep = 2 * group * BLK
        span = pl.ds(pl.multiple_of(step * deep, deep), deep)
        p_high, p_low = halves(p_ref[span, :])
        stacked = jnp.concatenate([p_high, p_low, p_high], axis=0)
        pairs = [step * group + m for m in range(group)]
        for s in range(2):
            found = False
            for kp in pairs:
                wait_pair(lay, pat, tab, t, sems, kp, s)
                found = jnp.logical_or(found, any_valid(lay, pat, tab, kp, s))

            @pl.when(found)
            def _():
                highs, lows = [], []
                for kp in pairs:
                    high, low = halves(entry_pair(t, kp, s))
                    th[kp, s] = high
                    tl[kp, s] = low
                    highs.append(high)
                    lows.append(low)
                image[s] += dot(jnp.concatenate(highs + highs + lows, axis=1), stacked)

    for s in range(2):
        high, low = halves(image[s].T)
        turned_high[s] = high
        turned_low[s] = low

    for a in range(rows - 1):

        @pl.loop(0, each)
        def _(i):
            kp = order[a] * each + i
            out = outs[a].at[i]
            out[...] = jnp.zeros(out.shape, out.dtype)
            for s in range(2):

                @pl.when(any_valid(lay, pat, tab, kp, s))
                def _():
                    out[...] += back_product(turned_high, turned_low, th[kp, s], tl[kp, s], s).T


def own_panel_kernel(lay, rows, tokens, pat, tab, order, gathered, turned_high, turned_low, *refs):
    out_ref, t, sems = refs[tokens:]
    each = t.shape[0] // 2 // rows
    first = order[rows - 1] * each

    @pl.loop(0, 2 * each)
    def _(i):
        fetch_entry(lay, pat, tab, gathered, t, sems, 2 * first + i)

    @pl.loop(0, each)
    def _(i):
        kp = first + i
        out = out_ref.at[i]
        out[...] = jnp.zeros(out.shape, out.dtype)
        for s in range(2):
            wait_pair(lay, pat, tab, t, sems, kp, s)

            @pl.when(any_valid(lay, pat, tab, kp, s))
            def _():
                high, low = halves(entry_pair(t, kp, s))
                out[...] += back_product(turned_high, turned_low, high, low, s).T


ANY = pl.BlockSpec(memory_space=pl.ANY)
VMEM = pl.BlockSpec(memory_space=pltpu.VMEM)
SMEM = pl.BlockSpec(memory_space=pltpu.SMEM)


def estimate(flops, values):
    return pl.CostEstimate(flops=flops, bytes_accessed=4 * values, transcendentals=0)


def panel_product(lay, pattern, table, order, gathered, normed, tokens):
    number, wide, rows = pattern.shape[0], normed.shape[1], order.shape[0]
    half = lay.half
    pairs = number // 2
    block = jax.ShapeDtypeStruct((pairs // rows, 2 * BLK, wide), jnp.float32)
    turned = jax.ShapeDtypeStruct((2, wide, half), jnp.bfloat16)
    result = pl.pallas_call(
        functools.partial(panel_kernel, lay, rows, len(tokens)),
        out_shape=[block] * (rows - 1) + [turned] * 2,
        in_specs=[SMEM] * 3 + [ANY, VMEM] + [ANY] * len(tokens),
        out_specs=[VMEM] * (rows + 1),
        scratch_shapes=[
            pltpu.VMEM((number, 2, lay.leaves, lay.part, BLK), jnp.float32),
            pltpu.VMEM((pairs, 2, half, 2 * BLK), jnp.bfloat16),
            pltpu.VMEM((pairs, 2, half, 2 * BLK), jnp.bfloat16),
            pltpu.VMEM((2, half, wide), jnp.float32),
            pltpu.SemaphoreType.DMA((number, 2)),
        ],
        compiler_params=pltpu.CompilerParams(vmem_limit_bytes=VMEM_BYTES),
        cost_estimate=estimate(18 * half * number * BLK * wide, 2 * half * number * BLK),
    )(pattern, table, order, gathered, normed, *tokens)
    return result[: rows - 1], result[rows - 1 :]


def own_panel_product(lay, pattern, table, order, gathered, turned, tokens):
    number, wide, rows = pattern.shape[0], turned[0].shape[1], order.shape[0]
    half = lay.half
    return pl.pallas_call(
        functools.partial(own_panel_kernel, lay, rows, len(tokens)),
        out_shape=jax.ShapeDtypeStruct((number // 2 // rows, 2 * BLK, wide), jnp.float32),
        in_specs=[SMEM] * 3 + [ANY, VMEM, VMEM] + [ANY] * len(tokens),
        out_specs=VMEM,
        scratch_shapes=[
            pltpu.VMEM((number, 2, lay.leaves, lay.part, BLK), jnp.float32),
            pltpu.SemaphoreType.DMA((number, 2)),
        ],
        compiler_params=pltpu.CompilerParams(vmem_limit_bytes=VMEM_BYTES),
        cost_estimate=estimate(24 * half * number * BLK * wide, half * number * BLK),
    )(pattern, table, order, gathered, *turned, *tokens)


def top_kernel(lay, chunks, chunk, tokens, tab, dests, leaf_ref, g_ref, own_ref, *refs):
    count = dests.shape[0]
    outs, (own_turned, held, sems) = refs[tokens : tokens + count], refs[tokens + count :]
    parts, part = lay.leaves, lay.part
    each = outs[0].shape[0]

    def place(a, i):
        block = (dests[a] * chunks + chunk) * each + i
        leaf = block // lay.cols
        return leaf, block - leaf * lay.cols

    def wanted(leaf, s):
        return jnp.logical_and(tab[s, leaf, 0] >= 0, tab[s, leaf_ref[0], 0] >= 0)

    for a in range(count):

        @pl.loop(0, each)
        def _(i):
            leaf, col = place(a, i)
            for s in range(2):

                @pl.when(wanted(leaf, s))
                def _():
                    for j in range(parts):
                        entry = tab[s, leaf, j]
                        slot = entry // (parts + 1)
                        position = entry - slot * (parts + 1)
                        pltpu.make_async_copy(
                            g_ref.at[col * lay.leaves + slot, position],
                            held.at[a, i, s, pl.ds(j * part, part)],
                            sems.at[a, i, s],
                        ).start()

    for s in range(2):
        high, low = halves(own_ref[s].T)
        own_turned[s, 0] = high
        own_turned[s, 1] = low

    for a in range(count):

        @pl.loop(0, each)
        def _(i):
            leaf, col = place(a, i)
            out = outs[a].at[i]
            out[...] = jnp.zeros(out.shape, out.dtype)
            for s in range(2):

                @pl.when(wanted(leaf, s))
                def _():
                    pltpu.make_async_copy(held.at[a, i, s], held.at[a, i, s], sems.at[a, i, s]).wait()
                    high, low = halves(held[a, i, s])
                    total = dot(own_turned[s, 0], high) + dot(own_turned[s, 1], high) + dot(own_turned[s, 0], low)
                    out[...] += total.T


def top_product(lay, table, dests, me_leaf, gathered, own, chunks, chunk, tokens=()):
    count, width, half = dests.shape[0], lay.width, lay.half
    each = gathered.shape[0] // lay.rows // chunks
    block = jax.ShapeDtypeStruct((each, width, width), jnp.float32)
    return pl.pallas_call(
        functools.partial(top_kernel, lay, chunks, chunk, len(tokens)),
        out_shape=[block] * count,
        in_specs=[SMEM] * 3 + [ANY, VMEM] + [ANY] * len(tokens),
        out_specs=[VMEM] * count,
        scratch_shapes=[
            pltpu.VMEM((2, 2, width, half), jnp.bfloat16),
            pltpu.VMEM((count, each, 2, half, width), jnp.float32),
            pltpu.SemaphoreType.DMA((count, each, 2)),
        ],
        compiler_params=pltpu.CompilerParams(vmem_limit_bytes=VMEM_BYTES),
        cost_estimate=estimate(12 * half * count * each * width * width, 2 * half * count * each * width),
    )(table, dests, me_leaf, gathered, own, *tokens)


def diagonal_kernel(steps, first, tokens, info, *refs):
    sources, refs = list(zip(steps, refs)), refs[len(steps) :]
    sigma, (out_ref, held, sems) = refs[0], refs[1 + tokens :]
    each = out_ref.shape[0]
    for i in range(each):
        away = info[1 + first + i] - info[0]
        for (step, run), source in sources:

            @pl.when(away == step)
            def _():
                rows = pl.ds(run * source.shape[0], source.shape[0])
                pltpu.make_async_copy(source, held.at[i, rows], sems.at[i]).start()

    turned_high, turned_low = halves(sigma[...].T)
    for i in range(each):
        pltpu.make_async_copy(held.at[i], held.at[i], sems.at[i]).wait()
        high, low = halves(held[i])
        total = dot(turned_high, high) + dot(turned_low, high) + dot(turned_high, low)
        out_ref[i] = total.T


def diagonal_product(info, first, each, pieces, sigma, tokens):
    depth, wide = sigma.shape
    return pl.pallas_call(
        functools.partial(diagonal_kernel, tuple(pieces), first, len(tokens)),
        out_shape=jax.ShapeDtypeStruct((each, wide, wide), jnp.float32),
        in_specs=[SMEM] + [ANY] * len(pieces) + [VMEM] + [ANY] * len(tokens),
        out_specs=VMEM,
        scratch_shapes=[pltpu.VMEM((each, depth, wide), jnp.float32), pltpu.SemaphoreType.DMA((each,))],
        compiler_params=pltpu.CompilerParams(vmem_limit_bytes=VMEM_BYTES),
        cost_estimate=estimate(6 * each * depth * wide * wide, (each + 1) * depth * wide),
    )(info, *pieces.values(), sigma, *tokens)


def after(value, *earlier):
    return pl.pallas_call(
        lambda *refs: None,
        out_shape=jax.ShapeDtypeStruct(value.shape, value.dtype),
        in_specs=[ANY] * (1 + len(earlier)),
        out_specs=ANY,
        input_output_aliases={0: 0},
        cost_estimate=estimate(0, 0),
    )(value, *earlier)


def send_over_rows(sent):
    rows = lax.axis_size("row")
    return [lax.ppermute(value, "row", [(i, (i + a + 1) % rows) for i in range(rows)]) for a, value in enumerate(sent)]


def per_device(lay, top_inverse, pattern, panel, diag_inverse):
    rows, cols, leaves = (lax.axis_size(axis) for axis in ("row", "col", "leaf"))
    me_row, me_col, me_leaf = (lax.axis_index(axis) for axis in ("row", "col", "leaf"))
    half, width, parts, part = lay.half, lay.width, lay.leaves, lay.part
    normed = panel[0]

    count = normed.shape[0] // rows
    own_rows = lax.dynamic_slice_in_dim(normed, me_row * count, count, 0)
    runs = 2
    pieces = {(0, run): own_rows[run * count // runs : (run + 1) * count // runs] for run in range(runs)}

    def hop(run, step, *earlier):
        if earlier:
            for key in sorted({(step, run), (-step, run)}):
                pieces[key] = after(pieces[key], *earlier)
        for way in (1, -1):
            at = [i for i in range(cols) if 0 <= i - way * step < cols and 0 <= i + way < cols]
            moved_on = lax.ppermute(pieces[-way * step, run], "col", [(i, i + way) for i in at])
            pieces[-way * (step + 1), run] = moved_on

    hop(0, 0)

    table = jnp.asarray(lay.table)[me_row]
    second = jnp.asarray([count[1] for count in lay.counts], jnp.int32)[me_row]
    is_moved = np.zeros((rows, leaves), bool)
    pairs = []
    for r in range(rows):
        for leaf, slot in lay.holder[r].items():
            if leaf != slot:
                is_moved[r, slot] = True
                pairs.append((leaf * rows + r, slot * rows + r))
    moved_here = jnp.asarray(is_moved)[me_row, me_leaf]
    lower, upper = top_inverse[half:], top_inverse[:half]
    swapped = lax.ppermute(upper, "row", [(r, rows - 1 - r) for r in range(rows)])
    moved = lax.ppermute(lower, ("leaf", "row"), pairs) if pairs else lower
    whole = jnp.where(me_leaf < second, swapped, jnp.where(moved_here, moved, lower))
    both = lower[: 2 * part]
    for chip in range(2, leaves, 2):
        both = jnp.where(me_leaf == chip, lax.ppermute(lower[chip * part : (chip + 2) * part], "leaf", [(0, chip)]), both)
    other = lax.ppermute(both[part:], "leaf", [(chip, chip + 1) for chip in range(0, leaves, 2)])
    extra = jnp.where(me_leaf % 2 == 0, both[:part], other)
    held = jnp.concatenate([whole.reshape(parts, part, width), extra[None]], axis=0)
    gathered = lax.all_gather(after(held, pieces[1, 0], pieces[-1, 0]), ("col", "leaf"), axis=0, tiled=False)
    own = jnp.stack([lower, swapped])
    hop(1, 0, gathered)

    chunks, each = 2, cols // rows
    order = ((me_row + 1 + jnp.arange(rows)) % rows).astype(jnp.int32)
    near = [[sorted(range(d * each, d * each + each), key=lambda block: abs(block - c)) for c in range(cols)] for d in range(rows)]
    near = np.asarray(near, np.int32)
    reach = np.abs(near - np.arange(cols)[None, :, None]).max(axis=(0, 1))
    near_here = jnp.asarray(near)[:, me_col]
    wanted = near_here[order[: rows - 1]].reshape(-1)
    info = jnp.concatenate([me_col[None], wanted, me_row * each + jnp.arange(each)]).astype(jnp.int32)
    leaf_here = me_leaf.astype(jnp.int32)[None]
    top_args = (leaf_here, gathered, own, chunks)
    early = top_product(lay, table, order[: rows - 1], *top_args, 0, [info])
    early_in = send_over_rows(early)
    if cols > 2:
        hop(0, 1, *early)
    sent, turned = panel_product(lay, pattern[0], table, order, gathered, normed, early)
    sent_in = send_over_rows(sent)
    middle = cols // 2
    for step in range(1, middle):
        hop(1, step, *sent)
        if step + 1 < cols - 1:
            hop(0, step + 1, *sent)
    kept = own_panel_product(lay, pattern[0], table, order, gathered, turned, early_in)
    tops = top_product(lay, table, order[rows - 1 :], *top_args, 0, [kept])
    late = top_product(lay, table, order[: rows - 1], *top_args, 1, tops)
    sigma_panel = -sum(sent_in, kept).reshape(-1, normed.shape[1])
    late = [after(value, *sent_in) for value in late]
    late_in = send_over_rows(late)
    for step in range(middle, cols - 1):
        hop(1, step, sigma_panel)
        if step + 1 < cols - 1:
            hop(0, step + 1, sigma_panel)

    terms_in, tokens = [], late
    for i in range(each):
        there = {key: piece for key, piece in pieces.items() if abs(key[0]) <= reach[i]}
        term = [diagonal_product(info, a * each + i, 1, there, sigma_panel, tokens) for a in range(rows - 1)]
        terms_in.append(send_over_rows(term))
        tokens = term + late_in
    mine = diagonal_product(info, (rows - 1) * each, each, pieces, sigma_panel, term)
    rest = diag_inverse[0] - mine.reshape(diag_inverse.shape[1:])
    tops = [*tops, *top_product(lay, table, order[rows - 1 :], *top_args, 1, [mine])]
    update = []
    for block in range(each):
        total = 0.0
        for i in range(each):
            for value in terms_in[i]:
                total += jnp.where(near_here[me_row, i] == me_row * each + block, value[0], 0.0)
        update.append(total)
    sigma_diag = rest - jnp.concatenate(update, axis=0)

    sigma_top = jnp.concatenate([sum(early_in, tops[0]), sum(late_in, tops[1])], axis=0).reshape(-1, width)
    return (sigma_top, sigma_panel[None], sigma_diag[None])


def solution(mesh):
    placed = (
        P("row", ("leaf", "col")),
        P("leaf", None),
        P("leaf", None, "col"),
        P("leaf", "row", "col"),
    )

    def whole(top_inverse, pattern, panel, diag_inverse):
        rows, leaves, cols = (mesh.shape[axis] for axis in ("row", "leaf", "col"))
        size = top_inverse.shape[0]
        lay = Layout(rows, leaves, cols, size // rows // 2, size // leaves // cols)
        return jax.shard_map(
            functools.partial(per_device, lay),
            mesh=mesh,
            in_specs=placed,
            out_specs=(P("row", ("leaf", "col")), P("leaf", "row", "col"), P("leaf", "row", "col")),
            check_vma=False,
        )(top_inverse, pattern, panel, diag_inverse)

    return whole
```
